32 devices in a mesh: dp: 8 (over z, x), mp: 4 (over y, core).
Axes of the slice: x: 2, y: 2, z: 4, core: 2. Of those that a mesh axis runs over, the one named last changes fastest.
Arguments:
- tokens: bfloat16 [16384, 512], P('dp'), may hold values from -6 to 6
- item_kind: int32 [8], P('dp'), may hold values from 0 to 1
- first_gain: float32 [512], replicated, may hold values from 0.1 to 1.9
- first_shift: float32 [512], replicated, may hold values from -1.75 to 1.75
- query_weight: bfloat16 [512, 512], P(None, 'mp'), may hold values from -0.25 to 0.25
- key_weight: bfloat16 [512, 512], P(None, 'mp'), may hold values from -0.25 to 0.25
- value_weight: bfloat16 [512, 512], P(None, 'mp'), may hold values from -0.25 to 0.25
- position_weight: bfloat16 [512, 512], P(None, 'mp'), may hold values from -0.25 to 0.25
- content_bias: float32 [512], P('mp'), may hold values from -3 to 3
- position_bias: float32 [512], P('mp'), may hold values from -3 to 3
- output_weight: bfloat16 [512, 512], P('mp'), may hold values from -1 to 1
- second_gain: float32 [512], replicated, may hold values from 0.1 to 1.9
- second_shift: float32 [512], replicated, may hold values from -1.75 to 1.75
- inner_weight: bfloat16 [512, 2048], P(None, 'mp'), may hold values from -0.25 to 0.25
- inner_bias: float32 [2048], P('mp'), may hold values from -1.75 to 1.75
- outer_weight: bfloat16 [2048, 512], P('mp'), may hold values from -0.125 to 0.125
- outer_bias: float32 [512], replicated, may hold values from -1.75 to 1.75
- cotangent: bfloat16 [16384, 512], P('dp'), may hold values from -6 to 6
Outputs:
- mixed: bfloat16 [16384, 512], P('dp')
- tokens_grad: bfloat16 [16384, 512], P('dp')
- first_gain_grad: float32 [512], replicated
- first_shift_grad: float32 [512], replicated
- query_grad: float32 [512, 512], P(None, 'mp')
- key_grad: float32 [512, 512], P(None, 'mp')
- value_grad: float32 [512, 512], P(None, 'mp')
- position_grad: float32 [512, 512], P(None, 'mp')
- content_bias_grad: float32 [512], P('mp')
- position_bias_grad: float32 [512], P('mp')
- output_grad: float32 [512, 512], P('mp')
- second_gain_grad: float32 [512], replicated
- second_shift_grad: float32 [512], replicated
- inner_grad: float32 [512, 2048], P(None, 'mp')
- inner_bias_grad: float32 [2048], P('mp')
- outer_grad: float32 [2048, 512], P('mp')
- outer_bias_grad: float32 [512], replicated
The draws below stay inside these ranges and needn't reach their ends.
Inputs may be any that keep to these rules, and one draw needn't show every extreme that they name: `item_kind`: 0: the group's 2048 bytes are one item; 1: they are two items of 1024 bytes.
All inputs are finite; a program needn't handle non-finite values.
Results may differ from the reference program's by a relative error of at most 0.017.
Values may be sent and summed in bfloat16 or wider, within the bound.
No kernel may reach another device: no remote copies, remote signals or barrier semaphores. Data moves between devices by JAX's collectives and lax.ppermute only.
A program may use at most 128 MiB of HBM per device.

```python
import math
import jax
import jax.numpy as jnp
from jax import lax

D = 512
H = 8
DH = 64
FF = 2048
LEN = 2048
TOKENS = 16384
N_DP = 8


def plant(array, stream_key, smallest, top_value):
    longest = array.shape.index(max(array.shape))
    spots = []
    for shift in (0, 1):
        where = [jax.random.randint(jax.random.fold_in(stream_key, axis), (), 0, length) for axis, length in enumerate(array.shape)]
        where[longest] = (where[longest] + shift) % array.shape[longest]
        spots.append(tuple(where))
    return array.at[spots[0]].set(smallest).at[spots[1]].set(top_value)


def shard_levels(key, extent, cuts, least, top_value):
    level = 1.0
    for axis_at, parts in cuts:
        heights = jax.random.uniform(jax.random.fold_in(jax.random.fold_in(key, 6), axis_at), (parts,), jnp.float32, least / len(cuts), top_value / len(cuts))
        level = level * jnp.repeat(jnp.exp(heights), extent[axis_at] // parts).reshape((-1,) + (1,) * (len(extent) - 1 - axis_at))
    return level


def centred(key, shape, deviation, most, split=(), held_as=jnp.bfloat16):
    level = shard_levels(key, shape, split, -0.22, 0.18) if split else 1.0
    values = jax.random.normal(key, shape, jnp.float32) * deviation * level
    return jnp.minimum(jnp.maximum(values, -most), most).astype(held_as)


def setup_inputs(seed: int = 0) -> dict:
    arg_keys = jax.random.split(jax.random.key(seed), 19)
    tokens = centred(arg_keys[0], (TOKENS, D), 1.0, 6.0, ((0, 8),))
    item_kind = plant(jax.random.randint(arg_keys[1], (N_DP,), 0, 2), jax.random.fold_in(arg_keys[1], 1), 0, 1).astype(jnp.int32)
    first_gain = jnp.clip(1.0 + 0.18 * jax.random.normal(arg_keys[2], (D,), jnp.float32), 0.1, 1.9)
    first_shift = centred(arg_keys[3], (D,), 0.3, 1.75, (), jnp.float32)
    query_weight = centred(arg_keys[4], (D, D), D ** -0.5, 0.25, ((1, 4),))
    key_weight = centred(arg_keys[5], (D, D), D ** -0.5, 0.25, ((1, 4),))
    value_weight = centred(arg_keys[6], (D, D), D ** -0.5, 0.25, ((1, 4),))
    position_weight = centred(arg_keys[7], (D, D), D ** -0.5, 0.25, ((1, 4),))
    content_bias = centred(arg_keys[8], (D,), 0.5, 3.0, ((0, 4),), jnp.float32)
    position_bias = centred(arg_keys[9], (D,), 0.5, 3.0, ((0, 4),), jnp.float32)
    output_weight = centred(arg_keys[10], (D, D), (D // 16) ** -0.5, 1.0, ((0, 4),))
    second_gain = jnp.clip(1.0 + 0.18 * jax.random.normal(arg_keys[11], (D,), jnp.float32), 0.1, 1.9)
    second_shift = centred(arg_keys[12], (D,), 0.3, 1.75, (), jnp.float32)
    inner_weight = centred(arg_keys[13], (D, FF), D ** -0.5, 0.25, ((1, 4),))
    inner_bias = centred(arg_keys[14], (FF,), 0.3, 1.75, ((0, 4),), jnp.float32)
    outer_weight = centred(arg_keys[15], (FF, D), FF ** -0.5, 0.125, ((0, 4),))
    outer_bias = centred(arg_keys[16], (D,), 0.3, 1.75, (), jnp.float32)
    cotangent = centred(arg_keys[17], (TOKENS, D), 1.0, 6.0, ((0, 8),))
    return {"tokens": tokens, "item_kind": item_kind, "first_gain": first_gain, "first_shift": first_shift, "query_weight": query_weight, "key_weight": key_weight, "value_weight": value_weight, "position_weight": position_weight, "content_bias": content_bias, "position_bias": position_bias, "output_weight": output_weight, "second_gain": second_gain, "second_shift": second_shift, "inner_weight": inner_weight, "inner_bias": inner_bias, "outer_weight": outer_weight, "outer_bias": outer_bias, "cotangent": cotangent}


EPS = 1e-05
NEG = -1e+30

@jax.custom_vjp
def low(v):
    return lax.optimization_barrier(v.astype(jnp.bfloat16)).astype(jnp.float32)

@jax.custom_vjp
def low_back(v):
    return v

def low_keep(v):
    return (low(v), None)

def low_pass(kept, grad):
    return (grad,)

def back_keep(v):
    return (v, None)

def back_low(kept, grad):
    return (low(grad),)
low.defvjp(low_keep, low_pass)
low_back.defvjp(back_keep, back_low)

def matmul(left, right):
    return jnp.dot(left, right, precision=lax.Precision.HIGHEST)

def layer_norm(values, gain_row, shift_row):
    center = values - lax.optimization_barrier(jnp.mean(values, axis=-1, keepdims=True))
    spread = lax.optimization_barrier(jnp.mean(center * center, axis=-1, keepdims=True))
    return center * lax.rsqrt(spread + EPS) * gain_row + shift_row

def sinusoid(count, model_width):
    distance = jnp.arange(count, dtype=jnp.float32)[:, None]
    freqs = jnp.exp(jnp.arange(model_width // 2, dtype=jnp.float32) * (-2.0 * math.log(10000.0) / model_width))
    angles = distance * freqs[None, :]
    return jnp.concatenate([jnp.sin(angles), jnp.cos(angles)], axis=1)

def forward(inputs, item_type, params):
    first_gain, first_shift, query_weight, key_weight, value_weight, position_weight, content_bias, position_bias, output_weight, second_gain, second_shift, inner_weight, inner_bias, outer_weight, outer_bias = params
    hidden_one = low(layer_norm(inputs, first_gain, first_shift))
    queries = low_back(matmul(hidden_one, query_weight))
    key_rows = low(low_back(matmul(hidden_one, key_weight)))
    value_rows = low(low_back(matmul(hidden_one, value_weight)))
    query_content = low(queries + content_bias)
    query_position = low(queries + position_bias)
    positions = low(low_back(matmul(low(sinusoid(LEN, D)), position_weight)))
    key_heads = key_rows.reshape(LEN, H, DH)
    value_heads = value_rows.reshape(LEN, H, DH)
    position_heads = positions.reshape(LEN, H, DH)
    row_block = min(512, LEN)
    item_half = LEN // 2
    column_ids = jnp.arange(LEN)

    @jax.checkpoint
    def attend(offset):
        row_ids = offset + jnp.arange(row_block)
        content_rows = lax.dynamic_slice_in_dim(query_content, offset, row_block, 0).reshape(row_block, H, DH)
        position_rows = lax.dynamic_slice_in_dim(query_position, offset, row_block, 0).reshape(row_block, H, DH)
        direct = jnp.einsum('qhd,khd->hqk', content_rows, key_heads, precision=lax.Precision.HIGHEST)
        relative_full = jnp.einsum('qhd,khd->hqk', position_rows, position_heads, precision=lax.Precision.HIGHEST)
        distance = jnp.clip(row_ids[:, None] - column_ids[None, :], 0, LEN - 1).astype(jnp.int32)
        relative = jnp.take_along_axis(relative_full, jnp.broadcast_to(distance[None], relative_full.shape), axis=2)
        logits = low_back((direct + relative) * 0.125)
        allowed = (column_ids[None, :] <= row_ids[:, None]) & ((item_type == 0) | (row_ids[:, None] // item_half == column_ids[None, :] // item_half))
        masked = jnp.where(allowed[None], logits, NEG)
        peak = lax.optimization_barrier(jnp.max(masked, axis=-1, keepdims=True))
        powers = jnp.exp(masked - peak)
        probabilities = low(powers / lax.optimization_barrier(jnp.sum(powers, axis=-1, keepdims=True)))
        mixed_rows = jnp.einsum('hqk,khd->qhd', probabilities, value_heads, precision=lax.Precision.HIGHEST)
        return mixed_rows.reshape(row_block, D)
    starts = jnp.arange(LEN // row_block, dtype=jnp.int32) * row_block
    attended = low(low_back(lax.map(attend, starts).reshape(LEN, D)))
    residual_one = inputs + low_back(matmul(attended, output_weight))
    hidden_two = low(layer_norm(residual_one, second_gain, second_shift))
    preact = low_back(matmul(hidden_two, inner_weight) + inner_bias)
    activated = low(jax.nn.gelu(preact))
    return residual_one + matmul(activated, outer_weight) + outer_bias

def reference(tokens, item_kind, first_gain, first_shift, query_weight, key_weight, value_weight, position_weight, content_bias, position_bias, output_weight, second_gain, second_shift, inner_weight, inner_bias, outer_weight, outer_bias, cotangent):
    params = tuple((member.astype(jnp.float32) for member in (first_gain, first_shift, query_weight, key_weight, value_weight, position_weight, content_bias, position_bias, output_weight, second_gain, second_shift, inner_weight, inner_bias, outer_weight, outer_bias)))
    inputs_all = tokens.astype(jnp.float32).reshape(N_DP, LEN, D)
    deltas_all = cotangent.astype(jnp.float32).reshape(N_DP, LEN, D)

    def one_group(totals, pieces):
        inputs, item_type, delta = pieces

        def apply(values, weights):
            return forward(values, item_type, weights)
        result, pull = jax.vjp(apply, inputs, params)
        input_grad, weight_grads = pull(delta)
        totals = jax.tree.map(jnp.add, totals, weight_grads)
        return (totals, (result.astype(jnp.bfloat16), input_grad.astype(jnp.bfloat16)))
    zeros_init = jax.tree.map(jnp.zeros_like, params)
    grads, (mixed, token_grads) = lax.scan(one_group, zeros_init, (inputs_all, item_kind, deltas_all))
    return (mixed.reshape(TOKENS, D), token_grads.reshape(TOKENS, D), grads[0], grads[1], grads[2], grads[3], grads[4], grads[5], grads[6], grads[7], grads[8], grads[9], grads[10], grads[11], grads[12], grads[13], grads[14])
```

```python
import functools
import math

import jax
import jax.numpy as jnp
import numpy as np
from jax import lax
from jax.experimental import pallas as pl
from jax.experimental.pallas import tpu as pltpu
from jax.sharding import PartitionSpec as P

DH = 64
EPS = 1e-05
NEG = -1e30
LOG2E = 1.4426950408889634
GELU_A = 0.7978845608028654
GELU_B = 0.044715

f32 = jnp.float32
bf16 = jnp.bfloat16


def sinusoid(count, model_width):
    freqs = np.exp(np.arange(model_width // 2) * (-2.0 * math.log(10000.0) / model_width))
    angles = np.arange(count)[:, None] * freqs[None, :]
    return np.sin(angles), np.cos(angles)


def dot(left, right):
    return jnp.dot(left, right, preferred_element_type=f32)


def dot_nt(left, right):
    return lax.dot_general(left, right, (((1,), (1,)), ((), ())), preferred_element_type=f32)


def whole(shape):
    return pl.BlockSpec(shape, lambda *ids: (0,) * len(shape))


def params(mib=60):
    return pltpu.CompilerParams(
        vmem_limit_bytes=mib * 2**20, dimension_semantics=("arbitrary",)
    )


def cost(microseconds):
    return pl.CostEstimate(
        flops=int(microseconds * 1.1e9), bytes_accessed=1 << 10, transcendentals=0
    )


def keep_rows(values, head):
    ids = lax.broadcasted_iota(jnp.int32, values.shape, 0)
    return jnp.where(ids // DH == head, values, jnp.zeros_like(values))


def keep_cols(values, head):
    ids = lax.broadcasted_iota(jnp.int32, values.shape, 1)
    return jnp.where(ids // DH == head, values, jnp.zeros_like(values))


def norm_parts(values):
    center = values - jnp.mean(values, axis=-1, keepdims=True)
    spread = jnp.mean(center * center, axis=-1, keepdims=True)
    scale = lax.rsqrt(spread + EPS)
    return center * scale, scale


def forward_body(
    block, half_rows,
    kind, place, tokens, cot, gain, shift, wq, wk, wv, cbias, pbias, wp, st, ct, table, table_t,
    tokens_own, cot_own, normed_out, qc_out, qp_out, v_out, ktt_out, p_out, ot_out, att_out,
    linv_out,
    wcat, kcat, vt, qa, s_scr, m_scr, l_scr, acc,
):
    ib = pl.program_id(0)
    here = pl.multiple_of(ib * block, block)
    width, cols = wp.shape
    half = width // 2
    mid = block // 2
    own = tokens_own.shape[0]

    @pl.when(ib == 0)
    def start():
        for n, ref in enumerate((wq, wk, wv)):
            wcat[:, n * cols : (n + 1) * cols] = ref[...]

    at = pl.multiple_of(place[1] * own, own)
    tokens_own[...] = tokens[pl.ds(at, own), :]
    cot_own[...] = cot[pl.ds(at, own), :]
    normed, _ = norm_parts(tokens[...].astype(f32))
    normed_out[...] = normed.astype(bf16)
    hidden = (normed * gain[...] + shift[...]).astype(bf16)
    qkv = dot(hidden, wcat[...])
    queries, keys, values = (qkv[:, n * cols : (n + 1) * cols] for n in range(3))
    qc_out[...] = ((queries + cbias[...]) * 0.125).astype(bf16)
    qp_out[...] = ((queries + pbias[...]) * 0.125).astype(bf16)
    v_out[...] = values.astype(bf16)
    kcat[pl.ds(here, block), :width] = table[...]
    kcat[pl.ds(here, block), width:] = keys.astype(bf16)
    vt[:, pl.ds(here, block)] = values.T.astype(bf16)
    keys_t = keys.T.astype(bf16)
    ktt_out[:DH] = keys_t[:DH]
    ktt_out[DH : DH + width] = table_t[...]
    ktt_out[DH + width :] = keys_t[DH:]
    queries_t = queries.T
    column = lambda row: jnp.broadcast_to(row, (8, row.shape[1])).T[:, :1]
    content = ((queries_t + column(cbias[...])) * (0.125 * LOG2E)).astype(bf16)
    position = ((queries_t + column(pbias[...])) * (0.125 * LOG2E)).astype(bf16)
    for h in range(2):
        u = dot(wp[...], keep_rows(position, h))
        us, uc = u[:half], u[half:]
        to = slice(h * block, (h + 1) * block)
        qa[:half, to] = (uc * st[...] - us * ct[...]).astype(bf16)
        qa[half:width, to] = (us * st[...] + uc * ct[...]).astype(bf16)
        qa[width:, to] = keep_rows(content, h)
    lo = jnp.where((kind[0] == 1) & (ib * block >= half_rows), half_rows // block, 0)
    fold = lambda x, op: op(x.reshape(x.shape[0] // 8, 8, x.shape[1]), axis=0)
    rj = lax.broadcasted_iota(jnp.int32, (mid, block), 0)
    ri = lax.broadcasted_iota(jnp.int32, (mid, block), 1)
    first = pl.ds(here, mid)
    second = pl.ds(pl.multiple_of(here + mid, mid), mid)

    s = dot(kcat[first, :], qa[...])
    s = jnp.where(jnp.concatenate([rj <= ri] * 2, axis=1), s, NEG)
    s_scr[first, :] = s
    m_scr[...] = fold(s, jnp.max)
    for h in range(2):
        to = slice(h * block + mid, (h + 1) * block)
        s = dot(kcat[second, :], qa[:, to])
        s = jnp.where(rj[:, :mid] <= ri[:, :mid], s, NEG)
        s_scr[second, to] = s
        m_scr[:, to] = jnp.maximum(m_scr[:, to], fold(s, jnp.max))

    def score_loop(c, carry):
        rows = pl.ds(pl.multiple_of(c * block, block), block)
        s = dot(kcat[rows, :], qa[...])
        s_scr[rows, :] = s
        m_scr[...] = jnp.maximum(m_scr[...], fold(s, jnp.max))
        return carry

    lax.fori_loop(lo, ib, score_loop, 0)
    m_scr[...] = jnp.broadcast_to(jnp.max(m_scr[...], axis=0, keepdims=True), m_scr.shape)

    p = jnp.exp2(s_scr[first, :] - m_scr[0:1])
    l_scr[...] = fold(p, jnp.sum)
    low = p.astype(bf16)
    p_out[first, :] = low
    for h in range(2):
        rows = slice(DH * h, DH * h + DH)
        to = slice(h * block + mid, (h + 1) * block)
        acc[rows] = dot(vt[rows, first], low[:, h * block : (h + 1) * block])
        p = jnp.exp2(s_scr[second, to] - m_scr[0:1, to])
        l_scr[:, to] += fold(p, jnp.sum)
        part = p.astype(bf16)
        p_out[second, to] = part
        acc[rows, mid:] += dot(vt[rows, second], part)

    def prob_loop(c, carry):
        rows = pl.ds(pl.multiple_of(c * block, block), block)
        p = jnp.exp2(s_scr[rows, :] - m_scr[0:1])
        l_scr[...] += fold(p, jnp.sum)
        low = p.astype(bf16)
        p_out[rows, :] = low
        for h in range(2):
            heads = slice(DH * h, DH * h + DH)
            acc[heads] += dot(vt[heads, rows], low[:, h * block : (h + 1) * block])
        return carry

    lax.fori_loop(lo, ib, prob_loop, 0)
    inverse = 1.0 / jnp.sum(l_scr[...], axis=0, keepdims=True)
    linv_out[...] = inverse
    attended = jnp.concatenate(
        [acc[DH * h : DH * h + DH] * inverse[:, h * block : (h + 1) * block] for h in range(2)],
        axis=0,
    )
    ot_out[...] = attended
    att_out[...] = attended.T.astype(bf16)


def attention_forward(
    kind, place, tokens, cot, gain, shift, wq, wk, wv, cbias, pbias, wp, st, ct, table, table_t,
    block,
):
    length, width = table.shape
    cols = wp.shape[1]
    count = length // block
    row = lambda n, w: pl.BlockSpec((n, w), lambda i: (i, 0))
    col = lambda n, w: pl.BlockSpec((n, w), lambda i: (0, i))
    smem = pl.BlockSpec(memory_space=pltpu.SMEM)
    shape = jax.ShapeDtypeStruct
    return pl.pallas_call(
        functools.partial(forward_body, block, length // 2),
        grid=(count,),
        in_specs=[
            smem, smem, row(block, width), row(block, width),
            whole((1, width)), whole((1, width)), *[whole((width, cols))] * 3,
            whole((1, cols)), whole((1, cols)), whole((width, cols)),
            col(width // 2, block), col(width // 2, block), row(block, width), col(width, block),
        ],
        out_specs=[
            row(block // 2, width), row(block // 2, width), row(block, width),
            row(block, cols), row(block, cols), row(block, cols), col(cols + width, block),
            col(length, 2 * block), col(cols, block), row(block, cols), col(1, 2 * block),
        ],
        out_shape=[
            shape((length // 2, width), bf16), shape((length // 2, width), bf16),
            shape((length, width), bf16),
            shape((length, cols), bf16), shape((length, cols), bf16), shape((length, cols), bf16),
            shape((cols + width, length), bf16),
            shape((length, 2 * length), bf16), shape((cols, length), f32),
            shape((length, cols), bf16), shape((1, 2 * length), f32),
        ],
        scratch_shapes=[
            pltpu.VMEM((width, 3 * cols), bf16),
            pltpu.VMEM((length, width + cols), bf16),
            pltpu.VMEM((cols, length), bf16),
            pltpu.VMEM((width + cols, 2 * block), bf16),
            pltpu.VMEM((length, 2 * block), f32),
            pltpu.VMEM((8, 2 * block), f32),
            pltpu.VMEM((8, 2 * block), f32),
            pltpu.VMEM((cols, block), f32),
        ],
        compiler_params=params(),
        cost_estimate=cost(25),
        name="attention_forward",
    )(
        kind, place, tokens, cot, gain, shift, wq, wk, wv, cbias, pbias, wp, st, ct, table, table_t
    )


def backward_body(
    count, block, half_rows,
    kind, place, p, d0, d1, d2, d3, ot, linv, qc, qp, v, ktt, wp, st, ct,
    wq, wk, wv, normed, gain, shift, sums,
    last, near, mine,
    wcat, acc, dk, dv, low, low_t, d_scr, dcat, dstack, qstack, delta, mom, colsum, dwp, cb, pb,
):
    step = pl.program_id(0)
    ib = count - 1 - step
    width, cols = wp.shape
    half = width // 2
    mid = block // 2
    own = d0.shape[0] // 2

    @pl.when(step == 0)
    def start():
        for ref in (dk, dv, dwp, cb, pb, mom, colsum):
            ref[...] = jnp.zeros(ref.shape, f32)
        for n, ref in enumerate((wq, wk, wv)):
            wcat[:, n * cols : (n + 1) * cols] = ref[...]
        for n, ref in enumerate((d0, d1, d2, d3)):
            for part in range(2):
                at = pl.multiple_of((4 * part + (place[0] ^ n)) * own, own)
                d_scr[pl.ds(at, own), :] = ref[part * own : (part + 1) * own]

    lo = jnp.where((kind[0] == 1) & (ib * block >= half_rows), half_rows // block, 0)
    here = pl.multiple_of(ib * block, block)
    dt = d_scr[pl.ds(here, block), :].astype(f32).T
    scaled = jnp.concatenate(
        [
            dt[DH * h : DH * h + DH] * linv[:, h * block : (h + 1) * block]
            for h in range(2)
        ],
        axis=0,
    )
    scaled_rows = scaled.T.astype(bf16)
    scaled = scaled.astype(bf16)
    product = scaled.astype(f32) * ot[...]
    for h in range(2):
        to = slice(h * block, (h + 1) * block)
        dcat[:, to] = keep_rows(scaled, h)
        dstack[to] = keep_cols(scaled_rows, h)
        qstack[to] = keep_cols(qc[...], h)
        delta[:, to] = jnp.sum(product[DH * h : DH * h + DH], axis=0, keepdims=True)

    first = pl.ds(here, mid)
    second = pl.ds(pl.multiple_of(here + mid, mid), mid)
    pt = p[first, :]
    dp = dot(v[first, :], dcat[...])
    ds = (pt.astype(f32) * (dp - delta[...])).astype(bf16)
    dv[first, :] += dot(pt, dstack[...])
    dk[first, :] += dot(ds, qstack[...])
    for h in range(2):
        to = slice(h * block + mid, (h + 1) * block)
        rows = slice(DH * h, DH * h + DH + width)
        acc[h] = dot(ktt[rows, first], ds[:, h * block : (h + 1) * block])
        pt2 = p[second, to]
        dp2 = dot(v[second, :], dcat[:, to])
        ds2 = (pt2.astype(f32) * (dp2 - delta[:, to])).astype(bf16)
        dv[second, :] += dot(pt2, dstack[to])
        dk[second, :] += dot(ds2, qstack[to])
        acc[h, :, mid:] += dot(ktt[rows, second], ds2)

    def loop(c, carry):
        rows = pl.ds(pl.multiple_of(c * block, block), block)
        pt = p[rows, :]
        dp = dot(v[rows, :], dcat[...])
        ds = (pt.astype(f32) * (dp - delta[...])).astype(bf16)
        dv[rows, :] += dot(pt, dstack[...])
        dk[rows, :] += dot(ds, qstack[...])
        for h in range(2):
            acc[h] += dot(
                ktt[DH * h : DH * h + DH + width, rows], ds[:, h * block : (h + 1) * block]
            )
        return carry

    lax.fori_loop(lo, ib, loop, 0)
    wpt = wp[...].astype(f32).T.astype(bf16)
    dqs = []
    for h in range(2):
        base = DH * (1 - h)
        gs = acc[h, base : base + half]
        gc = acc[h, base + half : base + width]
        rs = (st[...] * gc - ct[...] * gs).astype(bf16)
        rc = (ct[...] * gc + st[...] * gs).astype(bf16)
        wh = wpt[DH * h : DH * h + DH]
        by_position = (dot(wh[:, :half], rs) + dot(wh[:, half:], rc)) * 0.125
        by_content = acc[h, width * h : width * h + DH] * 0.125
        qph = keep_cols(qp[...], h)
        dwp[:half] += dot(rs, qph)
        dwp[half:] += dot(rc, qph)
        cb[DH * h : DH * h + DH] += by_content
        pb[DH * h : DH * h + DH] += by_position
        dqs.append(by_content + by_position)
    dqt = jnp.concatenate(dqs, axis=0)
    rows = pl.ds(here, block)
    for n, (value, value_t) in enumerate(
        ((dqt.T, dqt), (dk[rows, :], dk[rows, :].T), (dv[rows, :], dv[rows, :].T))
    ):
        to = slice(n * cols, (n + 1) * cols)
        low[:, to] = value.astype(bf16)
        low_t[to] = value_t.astype(bf16)
    mom[...] += dot(low_t[...], normed[...])
    colsum[...] += jnp.sum(low[...].astype(f32), axis=0, keepdims=True)
    for ref, core in ((near, 1 - place[1]), (mine, place[1])):
        at = pl.multiple_of(core * own, own)
        ref[...] = dot_nt(low[pl.ds(at, own), :], wcat[...]).astype(ref.dtype)

    @pl.when(step == count - 1)
    def finish():
        as_row = lambda values: jnp.broadcast_to(
            jnp.sum(values, axis=1, keepdims=True), (values.shape[0], 128)
        ).T[:1]
        parts = last.shape[0]
        share = width // parts
        extra = cols // parts
        column = jnp.broadcast_to(colsum[...], (8, 3 * cols)).T[:, :1]
        weights = wcat[...].astype(f32).T
        by_gain = jnp.sum(mom[...] * weights, axis=0, keepdims=True)
        by_shift = jnp.sum(column * weights, axis=0, keepdims=True)
        full = (gain[...] * mom[...] + shift[...] * column).T.astype(bf16)
        biases = jnp.concatenate(
            [as_row(cb[...]), as_row(pb[...]), jnp.zeros((1, width - 2 * cols), f32)], axis=1
        )
        tail = jnp.concatenate(
            [by_gain, by_shift, sums[...], biases, jnp.zeros((10, width), f32)], axis=0
        ).astype(bf16)
        by_table = dwp[...].astype(bf16)
        for r in range(parts):
            at = slice(r * share, (r + 1) * share)
            last[r, :extra] = jnp.zeros((extra, width), bf16)
            last[r, extra : extra + share, : 3 * cols] = full[at]
            last[r, extra : extra + share, 3 * cols :] = by_table[at]
            last[r, extra + share :] = tail


def attention_backward(
    kind, place, p, grads, ot, linv, qc, qp, v, ktt, wp, st, ct, wq, wk, wv, normed,
    gain, shift, sums, block,
):
    length, width = normed.shape
    cols = qc.shape[1]
    count = length // block
    quarter = length // 4
    col = lambda n, w: pl.BlockSpec((n, w), lambda i: (0, count - 1 - i))
    row = lambda n, w: pl.BlockSpec((n, w), lambda i: (count - 1 - i, 0))
    smem = pl.BlockSpec(memory_space=pltpu.SMEM)
    parts = first_parts()
    message = (parts, (width + cols) // parts + 16, width)
    return pl.pallas_call(
        functools.partial(backward_body, count, block, length // 2),
        grid=(count,),
        in_specs=[
            smem, smem, col(length, 2 * block),
            *[whole((quarter, cols))] * 4,
            col(cols, block), col(1, 2 * block), row(block, cols), row(block, cols),
            whole(v.shape), whole(ktt.shape), whole(wp.shape),
            col(width // 2, block), col(width // 2, block),
            *[whole((width, cols))] * 3, row(block, width),
            whole(gain.shape), whole(shift.shape), whole(sums.shape),
        ],
        out_specs=[whole(message), row(block // 2, width), row(block // 2, width)],
        out_shape=[
            jax.ShapeDtypeStruct(message, bf16),
            jax.ShapeDtypeStruct((length // 2, width), bf16),
            jax.ShapeDtypeStruct((length // 2, width), f32),
        ],
        scratch_shapes=[
            pltpu.VMEM((width, 3 * cols), bf16),
            pltpu.VMEM((2, DH + width, block), f32),
            pltpu.VMEM((length, cols), f32),
            pltpu.VMEM((length, cols), f32),
            pltpu.VMEM((block, 3 * cols), bf16),
            pltpu.VMEM((3 * cols, block), bf16),
            pltpu.VMEM((length, cols), bf16),
            pltpu.VMEM((cols, 2 * block), bf16),
            pltpu.VMEM((2 * block, cols), bf16),
            pltpu.VMEM((2 * block, cols), bf16),
            pltpu.VMEM((1, 2 * block), f32),
            pltpu.VMEM((3 * cols, width), f32),
            pltpu.VMEM((1, 3 * cols), f32),
            pltpu.VMEM((width, cols), f32),
            pltpu.VMEM((cols, block), f32),
            pltpu.VMEM((cols, block), f32),
        ],
        compiler_params=params(),
        cost_estimate=cost(100),
        name="attention_backward",
    )(
        kind, place, p, *grads, ot, linv, qc, qp, v, ktt, wp, st, ct, wq, wk, wv, normed,
        gain, shift, sums,
    )


def feed_body(
    place, tokens, cot, own_att, a1, a2, a3, w0, w1, w2, w3, i0, i1, u0, u1, b0, b1,
    bu, gain, shift,
    back_keep, back_send, out_keep, out_send, res_own, grad0, grad1,
    back_scr, res_scr, sum0, sum1,
):
    step = pl.program_id(0)
    own, width = res_own.shape
    cols = a1.shape[1]
    share = i0.shape[1]
    c = cot[...]
    residual = tokens[...].astype(f32)
    residual = residual + dot(own_att[...].reshape(2 * own, cols), w0[...])
    for att, wo in ((a1, w1), (a2, w2), (a3, w3)):
        residual = residual + dot(att[...], wo[...])
    res_scr[...] = residual
    normed, _ = norm_parts(residual)
    hidden = (normed * gain[...] + shift[...]).astype(bf16)
    hidden_t = hidden.T
    mixed = None
    back = None
    for n, wi, wu, bi, total in ((0, i0, u0, b0, sum0), (1, i1, u1, b1, sum1)):
        x = dot(hidden, wi[...]) + bi[...]
        square = x * x
        t = jnp.tanh(GELU_A * x * (1.0 + GELU_B * square))
        act = (0.5 * x * (1.0 + t)).astype(bf16)
        slope = 0.5 * (1.0 + t) + (0.5 * GELU_A) * x * (1.0 - t * t) * (
            1.0 + (3.0 * GELU_B) * square
        )
        out_n = dot(act, wu[...])
        pre = (dot_nt(c, wu[...]) * slope).astype(bf16)
        back_n = dot_nt(pre, wi[...])
        mixed = out_n if mixed is None else mixed + out_n
        back = back_n if back is None else back + back_n
        inner = dot(hidden_t, pre)
        outer = dot(act.T, c)
        bias = jnp.sum(pre.astype(f32), axis=0, keepdims=True)
        bias = jnp.broadcast_to(bias, (16, share))

        @pl.when(step == 0)
        def first(total=total, inner=inner, outer=outer, bias=bias):
            total[:width] = inner
            total[width : width + share] = outer
            total[width + share :] = bias

        @pl.when(step > 0)
        def later(total=total, inner=inner, outer=outer, bias=bias):
            total[:width] += inner
            total[width : width + share] += outer
            total[width + share :] += bias

    back_scr[...] = back
    mine = pl.multiple_of(place[2] * own, own)
    other = pl.multiple_of((1 - place[2]) * own, own)
    res_own[...] = res_scr[pl.ds(mine, own), :]
    back_keep[...] = back_scr[pl.ds(mine, own), :]
    back_send[...] = back_scr[pl.ds(other, own), :].astype(bf16)
    out_keep[...] = mixed + residual + bu[...]
    out_send[...] = mixed.astype(bf16)

    @pl.when(step == pl.num_programs(0) - 1)
    def finish():
        parts = grad0.shape[0]
        mid = width // parts
        end = mid + share // parts
        for total, grad in ((sum0, grad0), (sum1, grad1)):
            bias = total[width + share :].astype(bf16)
            for r in range(parts):
                grad[r, :mid] = total[r * mid : (r + 1) * mid].astype(bf16)
                at = width + r * (end - mid)
                grad[r, mid:end] = total[at : at + end - mid].astype(bf16)
                grad[r, end:] = bias


def feed(place, tokens, cot, own_att, atts, wos, wis, wus, bis, bu, gain, shift):
    rows, width = tokens.shape
    cols = own_att.shape[1]
    share = wis[0].shape[1]
    own = rows // 4
    spec = lambda s: pl.BlockSpec(s, lambda i, place: (0,) * len(s))
    step = lambda n, w: pl.BlockSpec((n, w), lambda i, place: (i, 0))
    parts = first_parts()
    grad_shape = (parts, (width + share) // parts + 16, width)
    att = pl.BlockSpec((1, 2, 1, own, cols), lambda i, place: (i, 0, place[1], 0, 0))
    others = (*wos, *wis, *wus, *bis, bu, gain, shift)
    shape = jax.ShapeDtypeStruct
    return pl.pallas_call(
        feed_body,
        grid_spec=pltpu.PrefetchScalarGridSpec(
            num_scalar_prefetch=1,
            grid=(2,),
            in_specs=[step(2 * own, width), step(2 * own, width), att]
            + [step(2 * own, cols)] * 3
            + [spec(o.shape) for o in others],
            out_specs=[
                step(own, width), step(own, width), step(2 * own, width), step(2 * own, width),
                step(own, width), spec(grad_shape), spec(grad_shape),
            ],
            scratch_shapes=[pltpu.VMEM((2 * own, width), f32)] * 2
            + [pltpu.VMEM((width + share + 16, width), f32)] * 2,
        ),
        out_shape=[
            shape((2 * own, width), f32), shape((2 * own, width), bf16),
            shape((rows, width), f32), shape((rows, width), bf16),
            shape((2 * own, width), f32), shape(grad_shape, bf16), shape(grad_shape, bf16),
        ],
        compiler_params=params(),
        cost_estimate=cost(13),
        name="feed",
    )(place, tokens, cot, own_att.reshape(2, 2, 2, own, cols), *atts, *others)


def turn_body(
    place, keep, got, residual, cot, a0, a1, a2, a3, w0, w1, w2, w3, gain,
    res_out, sums_out, g0, g1, g2, g3, o0, o1, o2, o3, total,
):
    step = pl.program_id(0)
    back = keep[...] + got[...].astype(f32)
    c = cot[...].astype(f32)
    normed, scale = norm_parts(residual[...])
    fold = lambda values: jnp.sum(values, axis=0, keepdims=True)
    sums = jnp.concatenate([fold(back * normed), fold(back), fold(c)], axis=0)
    e = back * gain[...]
    inner = (
        e
        - jnp.mean(e, axis=-1, keepdims=True)
        - normed * jnp.mean(e * normed, axis=-1, keepdims=True)
    )
    res = c + scale * inner
    res_out[...] = res
    branch = res.astype(bf16)
    for wo, out in ((w0, g0), (w1, g1), (w2, g2), (w3, g3)):
        out[...] = dot_nt(branch, wo[...]).astype(bf16)
    products = [dot(att[...].T, branch) for att in (a0, a1, a2, a3)]

    @pl.when(step == 0)
    def first():
        sums_out[...] = sums
        for n in range(4):
            total[n] = products[n]

    @pl.when(step == 1)
    def second():
        sums_out[...] += sums
        for n, out in enumerate((o0, o1, o2, o3)):
            out[...] = (total[n] + products[n]).astype(out.dtype)


def turn(place, keep, got, residual, cot, own_att, others, wos, gain):
    rows, width = keep.shape
    own = rows // 2
    cols = wos[0].shape[0]
    spec = lambda s: pl.BlockSpec(s, lambda i, place: (0,) * len(s))
    step = lambda w: pl.BlockSpec((own, w), lambda i, place: (i, 0))
    half = lambda w: pl.BlockSpec((own, w), lambda i, place: (2 * i + place[2], 0))
    shapes = [((rows, width), f32), ((3, width), f32)]
    shapes = shapes + [((rows, cols), bf16)] * 4
    shapes = shapes + [((cols, width), t) for t in (f32, bf16, bf16, bf16)]
    return pl.pallas_call(
        turn_body,
        grid_spec=pltpu.PrefetchScalarGridSpec(
            num_scalar_prefetch=1,
            grid=(2,),
            in_specs=[step(width), step(width), step(width), half(width)]
            + [pl.BlockSpec((own, cols), lambda i, place: (4 * i + place[0], 0))]
            + [half(cols)] * 3
            + [spec(w.shape) for w in wos]
            + [spec(gain.shape)],
            out_specs=[step(width), spec((3, width))]
            + [step(cols)] * 4
            + [spec((cols, width))] * 4,
            scratch_shapes=[pltpu.VMEM((4, cols, width), f32)],
        ),
        out_shape=[jax.ShapeDtypeStruct(s, t) for s, t in shapes],
        compiler_params=params(),
        cost_estimate=cost(60),
        name="turn",
    )(place, keep, got, residual, cot, own_att, *others, *wos, gain)


def close_body(place, keep0, keep1, near0, near1, got, t0, t1, res, gain, out):
    own = t0.shape[0]
    for part, keep, near, tokens in ((0, keep0, near0, t0), (1, keep1, near1, t1)):
        rows = slice(part * own, (part + 1) * own)
        total = keep[...] + near[...].astype(f32) + got[rows].astype(f32)
        normed, scale = norm_parts(tokens[...].astype(f32))
        e = total * gain[...]
        inner = (
            e
            - jnp.mean(e, axis=-1, keepdims=True)
            - normed * jnp.mean(e * normed, axis=-1, keepdims=True)
        )
        out[rows] = (res[rows] + scale * inner).astype(bf16)


def close(place, keep, near, got, tokens, res, gain):
    rows, width = got.shape
    own = rows // 2
    spec = pl.BlockSpec((rows, width), lambda i, place: (0, 0))
    at = lambda part: pl.BlockSpec((own, width), lambda i, place: (2 * part + place[2], 0))
    return pl.pallas_call(
        close_body,
        grid_spec=pltpu.PrefetchScalarGridSpec(
            num_scalar_prefetch=1,
            grid=(1,),
            in_specs=[
                at(0), at(1), at(0), at(1), spec, at(0), at(1), spec,
                pl.BlockSpec((1, width), lambda i, place: (0, 0)),
            ],
            out_specs=spec,
        ),
        out_shape=jax.ShapeDtypeStruct((rows, width), bf16),
        compiler_params=params(),
        cost_estimate=cost(2),
        name="close",
    )(place, keep, keep, near, near, got, tokens, tokens, res, gain)


def collect_body(place, m0, m1, g0, g1, g2, g3, mixed, grad):
    own = g0.shape[0] // 2
    core, high = place[1], place[2]
    for part in range(2):
        for flip, ref in ((0, m0), (1, m1)):
            for at_high in range(2):
                put = pl.multiple_of((4 * part + 2 * at_high + (core ^ flip)) * own, own)
                mixed[pl.ds(put, own), :] = ref[(2 * part + at_high) * own :][:own]
        for n, ref in enumerate((g0, g1, g2, g3)):
            put = pl.multiple_of((4 * part + (place[0] ^ n)) * own, own)
            grad[pl.ds(put, own), :] = ref[part * own : (part + 1) * own]


def collect(place, mixed, grads):
    rows, width = grads[0].shape
    vmem = pl.BlockSpec(memory_space=pltpu.VMEM)
    shape = jax.ShapeDtypeStruct((4 * rows, width), bf16)
    return pl.pallas_call(
        collect_body,
        in_specs=[pl.BlockSpec(memory_space=pltpu.SMEM)] + [vmem] * 6,
        out_specs=[vmem] * 2,
        out_shape=[shape] * 2,
        compiler_params=pltpu.CompilerParams(vmem_limit_bytes=60 * 2**20),
        cost_estimate=cost(3),
        name="collect",
    )(place, *mixed, *grads)


def swap(value, axis, mask):
    size = lax.axis_size(axis)
    return lax.ppermute(value, axis, [(i, i ^ mask) for i in range(size)])


def block_of(value, index, count):
    return lax.dynamic_slice_in_dim(value, index * count, count, 0)


def gather_mp(value):
    beyond = swap(value, "mp", 2)
    return [value, swap(value, "mp", 1), beyond, swap(beyond, "mp", 1)]


def levels(size):
    bits = size.bit_length() - 1
    out = []
    shift = 0
    while shift < bits:
        wide = min(3, bits - shift)
        out.append((shift, wide))
        shift += wide
    return out


def groups_of(shift, wide):
    size = lax.axis_size("dp")
    count = 1 << wide
    return [
        [base + (n << shift) for n in range(count)]
        for base in range(size)
        if not (base >> shift) & (count - 1)
    ]


def exchange(value, shift, wide):
    return lax.all_to_all(
        value, "dp", split_axis=0, concat_axis=0, tiled=True,
        axis_index_groups=None if 1 << wide == lax.axis_size("dp") else groups_of(shift, wide),
    )


def gather_dp(value):
    sizes = [1 << wide for _, wide in levels(lax.axis_size("dp"))]
    whole_value = lax.all_gather(value, "dp", axis=0)
    if len(sizes) > 1:
        whole_value = whole_value.reshape(*sizes[::-1], *value.shape)
        whole_value = whole_value.transpose(
            *reversed(range(len(sizes))), len(sizes), len(sizes) + 1
        )
    return whole_value.reshape(sizes[0], -1, value.shape[1])


def first_parts():
    return 1 << levels(lax.axis_size("dp"))[0][1]


def reduce_dp(parts, before=None):
    for at, (shift, wide) in enumerate(levels(lax.axis_size("dp"))):
        if at:
            count = 1 << wide
            small = jnp.broadcast_to(total[None, -16:], (count, 16, total.shape[1]))
            rows = total[:-16].reshape(count, -1, total.shape[1])
            parts = jnp.concatenate([rows, small], axis=1).astype(bf16)
        got = exchange(parts, shift, wide)
        if before is not None:
            got, before = lax.optimization_barrier((got, before))
        total = jnp.sum(got.astype(f32), axis=0)
    return total[:-16].astype(bf16), total[-16:], before


def spread_dp(value):
    for shift, wide in reversed(levels(lax.axis_size("dp"))):
        count = 1 << wide
        parts = jnp.broadcast_to(value[None], (count,) + value.shape)
        value = exchange(parts, shift, wide).reshape((count * value.shape[0],) + value.shape[1:])
    return value.reshape(first_parts(), -1, value.shape[1])


def shards(
    tokens, item_kind, first_gain, first_shift, query_weight, key_weight, value_weight,
    position_weight, content_bias, position_bias, output_weight, second_gain, second_shift,
    inner_weight, inner_bias, outer_weight, outer_bias, cotangent,
):
    length, width = tokens.shape
    cols = query_weight.shape[1]
    share = inner_weight.shape[1]
    mp = lax.axis_index("mp").astype(jnp.int32)
    core, high = mp & 1, mp >> 1
    place = jnp.stack([mp, core, high])
    half = length // 2
    block = min(512, half)
    per_half = half // block
    own = half // 4
    sin_table, cos_table = sinusoid(length, width)
    table = jnp.asarray(np.concatenate([sin_table, cos_table], axis=1), bf16)
    table_t = jnp.asarray(np.concatenate([sin_table, cos_table], axis=1).T, bf16)
    st = jnp.asarray(sin_table.T, f32)
    ct = jnp.asarray(cos_table.T, f32)
    gain1, shift1, gain2, shift2, bu = (
        v[None] for v in (first_gain, first_shift, second_gain, second_shift, outer_bias)
    )

    tie = lax.optimization_barrier
    wos = [output_weight] + [swap(output_weight, "mp", n) for n in (1, 2, 3)]
    wis = [inner_weight, swap(inner_weight, "mp", 1)]
    wus = [outer_weight, swap(outer_weight, "mp", 1)]
    bis = [inner_bias[None], swap(inner_bias[None], "mp", 1)]

    projections = (query_weight, key_weight, value_weight)
    tokens_own, cot_own, normed, qc, qp, v, ktt, p, ot, attended, linv = attention_forward(
        item_kind, place, tokens, cotangent, gain1, shift1, *projections, content_bias[None],
        position_bias[None], position_weight, st, ct, table, table_t, block,
    )
    blocks = attended.reshape(4, 2, own, cols)
    pick = lambda c: lax.dynamic_index_in_dim(blocks, c, 1, False).reshape(4 * own, cols)
    near, far = pick(1 - core), pick(core)
    atts = [swap(near, "mp", 1), swap(far, "mp", 2), swap(near, "mp", 3)]
    back_keep, back_send, out_keep, out_send, residual, keep, near = feed(
        place, tokens_own, cot_own, attended, atts, wos, wis, wus, bis, bu, gain2, shift2
    )
    back_got = swap(back_send, "mp", 2)
    near_got = swap(near, "mp", 1)
    feed_sum = (keep.astype(f32) + near_got.astype(f32)).astype(bf16)
    feed_part, feed_small, _ = reduce_dp(feed_sum)

    res, sums, *turned = turn(
        place, back_keep, back_got, residual, cot_own, attended, atts, wos, gain2
    )
    grads, weight_parts = turned[:4], turned[4:]
    grads = [grads[0]] + [swap(grads[n], "mp", n) for n in (1, 2, 3)]
    grads, weight_parts, out_send, feed_part = tie(
        (grads, weight_parts, out_send, feed_part)
    )
    feed_total = spread_dp(feed_part)
    weight_parts = [weight_parts[0]] + [swap(weight_parts[n], "mp", n) for n in (1, 2, 3)]
    out_got = swap(out_send, "mp", 2)

    last, near, keep = attention_backward(
        item_kind, place, p, grads, ot, linv, qc, qp, v, ktt, position_weight,
        st, ct, *projections, normed, gain1, shift1, sums, block,
    )
    last, near, keep, weight_parts, out_got, feed_total = tie(
        (last, near, keep, weight_parts, out_got, feed_total)
    )
    near = swap(near, "mp", 1)
    parts = first_parts()
    out_sum = sum(x.astype(f32) for x in weight_parts).astype(bf16)
    last = lax.dynamic_update_slice(
        last, out_sum.reshape(parts, cols // parts, width), (0, 0, 0)
    )
    pick = lambda x: lax.dynamic_index_in_dim(x.reshape(2, 2, own, width), 1 - high, 1, False)
    far = (pick(keep) + pick(near).astype(f32)).astype(bf16).reshape(2 * own, width)
    far = swap(far, "mp", 2)
    mixed = (out_keep + out_got.astype(f32)).astype(bf16)
    mixed = [mixed, swap(mixed, "mp", 1)]
    grad = close(place, keep, near, far, tokens_own, res, gain1)
    last_part, last_small, grad = reduce_dp(last, grad)
    tokens_grad = gather_mp(grad)
    last_total = spread_dp(last_part).astype(f32)
    mixed, tokens_grad = collect(place, mixed, tokens_grad)

    summed = last_small[:5]
    summed = summed + swap(summed, "mp", 1)
    summed = summed + swap(summed, "mp", 2)
    feed_total = feed_total.astype(f32)
    split = width // parts
    begin = cols // parts
    inner_grad = feed_total[:, :split].reshape(width, share)
    outer_grad = feed_total[:, split:].reshape(share, width)
    whole_grad = last_total[:, begin:].reshape(width, width)

    return (
        mixed,
        tokens_grad,
        summed[0],
        summed[1],
        whole_grad[:, :cols],
        whole_grad[:, cols : 2 * cols],
        whole_grad[:, 2 * cols : 3 * cols],
        whole_grad[:, 3 * cols :],
        last_small[5, :cols],
        last_small[5, cols : 2 * cols],
        last_total[:, :begin].reshape(cols, width),
        summed[2],
        summed[3],
        inner_grad,
        feed_small[0],
        outer_grad,
        summed[4],
    )


def solution(mesh):
    return jax.shard_map(
        shards,
        mesh=mesh,
        in_specs=(
            P("dp", None), P("dp"), P(), P(), P(None, "mp"), P(None, "mp"), P(None, "mp"),
            P(None, "mp"), P("mp"), P("mp"), P("mp", None), P(), P(), P(None, "mp"), P("mp"),
            P("mp", None), P(), P("dp", None),
        ),
        out_specs=(
            P("dp", None), P("dp", None), P(), P(), P(None, "mp"), P(None, "mp"), P(None, "mp"),
            P(None, "mp"), P("mp"), P("mp"), P("mp", None), P(), P(), P(None, "mp"), P("mp"),
            P("mp", None), P(),
        ),
        check_vma=False,
    )
```

```python
import functools
import math

import jax
import jax.numpy as jnp
import numpy as np
from jax import lax
from jax.experimental import pallas as pl
from jax.experimental.pallas import tpu as pltpu
from jax.sharding import PartitionSpec as P

DH = 64
EPS = 1e-05
NEG = -1e30
LOG2E = 1.4426950408889634
GELU_A = 0.7978845608028654
GELU_B = 0.044715

f32 = jnp.float32
bf16 = jnp.bfloat16


def sinusoid(count, model_width):
    freqs = np.exp(np.arange(model_width // 2) * (-2.0 * math.log(10000.0) / model_width))
    angles = np.arange(count)[:, None] * freqs[None, :]
    return np.sin(angles), np.cos(angles)


def dot(left, right):
    return jnp.dot(left, right, preferred_element_type=f32)


def dot_nt(left, right):
    return lax.dot_general(left, right, (((1,), (1,)), ((), ())), preferred_element_type=f32)


def whole(shape):
    return pl.BlockSpec(shape, lambda *ids: (0,) * len(shape))


def params(mib=60):
    return pltpu.CompilerParams(
        vmem_limit_bytes=mib * 2**20, dimension_semantics=("arbitrary",)
    )


def cost(microseconds):
    return pl.CostEstimate(
        flops=int(microseconds * 1.1e9), bytes_accessed=1 << 10, transcendentals=0
    )


def keep_rows(values, head):
    ids = lax.broadcasted_iota(jnp.int32, values.shape, 0)
    return jnp.where(ids // DH == head, values, jnp.zeros_like(values))


def keep_cols(values, head):
    ids = lax.broadcasted_iota(jnp.int32, values.shape, 1)
    return jnp.where(ids // DH == head, values, jnp.zeros_like(values))


def norm_parts(values):
    center = values - jnp.mean(values, axis=-1, keepdims=True)
    spread = jnp.mean(center * center, axis=-1, keepdims=True)
    scale = lax.rsqrt(spread + EPS)
    return center * scale, scale


def forward_body(
    block, half_rows,
    kind, place, tokens, cot, gain, shift, wq, wk, wv, cbias, pbias, wp, st, ct, table, table_t,
    tokens_own, cot_own, normed_out, qc_out, qp_out, v_out, ktt_out, p_out, ot_out, att_out,
    linv_out,
    wcat, kcat, vt, qa, s_scr, m_scr, l_scr, acc,
):
    ib = pl.program_id(0)
    here = pl.multiple_of(ib * block, block)
    width, cols = wp.shape
    half = width // 2
    mid = block // 2
    own = tokens_own.shape[0]

    @pl.when(ib == 0)
    def start():
        for n, ref in enumerate((wq, wk, wv)):
            wcat[:, n * cols : (n + 1) * cols] = ref[...]

    at = pl.multiple_of(place[1] * own, own)
    tokens_own[...] = tokens[pl.ds(at, own), :]
    cot_own[...] = cot[pl.ds(at, own), :]
    normed, _ = norm_parts(tokens[...].astype(f32))
    normed_out[...] = normed.astype(bf16)
    hidden = (normed * gain[...] + shift[...]).astype(bf16)
    qkv = dot(hidden, wcat[...])
    queries, keys, values = (qkv[:, n * cols : (n + 1) * cols] for n in range(3))
    qc_out[...] = ((queries + cbias[...]) * 0.125).astype(bf16)
    qp_out[...] = ((queries + pbias[...]) * 0.125).astype(bf16)
    v_out[...] = values.astype(bf16)
    kcat[pl.ds(here, block), :width] = table[...]
    kcat[pl.ds(here, block), width:] = keys.astype(bf16)
    vt[:, pl.ds(here, block)] = values.T.astype(bf16)
    keys_t = keys.T.astype(bf16)
    ktt_out[:DH] = keys_t[:DH]
    ktt_out[DH : DH + width] = table_t[...]
    ktt_out[DH + width :] = keys_t[DH:]
    queries_t = queries.T
    column = lambda row: jnp.broadcast_to(row, (8, row.shape[1])).T[:, :1]
    content = ((queries_t + column(cbias[...])) * (0.125 * LOG2E)).astype(bf16)
    position = ((queries_t + column(pbias[...])) * (0.125 * LOG2E)).astype(bf16)
    for h in range(2):
        u = dot(wp[...], keep_rows(position, h))
        us, uc = u[:half], u[half:]
        to = slice(h * block, (h + 1) * block)
        qa[:half, to] = (uc * st[...] - us * ct[...]).astype(bf16)
        qa[half:width, to] = (us * st[...] + uc * ct[...]).astype(bf16)
        qa[width:, to] = keep_rows(content, h)
    lo = jnp.where((kind[0] == 1) & (ib * block >= half_rows), half_rows // block, 0)
    fold = lambda x, op: op(x.reshape(x.shape[0] // 8, 8, x.shape[1]), axis=0)
    rj = lax.broadcasted_iota(jnp.int32, (mid, block), 0)
    ri = lax.broadcasted_iota(jnp.int32, (mid, block), 1)
    first = pl.ds(here, mid)
    second = pl.ds(pl.multiple_of(here + mid, mid), mid)

    s = dot(kcat[first, :], qa[...])
    s = jnp.where(jnp.concatenate([rj <= ri] * 2, axis=1), s, NEG)
    s_scr[first, :] = s
    m_scr[...] = fold(s, jnp.max)
    for h in range(2):
        to = slice(h * block + mid, (h + 1) * block)
        s = dot(kcat[second, :], qa[:, to])
        s = jnp.where(rj[:, :mid] <= ri[:, :mid], s, NEG)
        s_scr[second, to] = s
        m_scr[:, to] = jnp.maximum(m_scr[:, to], fold(s, jnp.max))

    def score_loop(c, carry):
        rows = pl.ds(pl.multiple_of(c * block, block), block)
        s = dot(kcat[rows, :], qa[...])
        s_scr[rows, :] = s
        m_scr[...] = jnp.maximum(m_scr[...], fold(s, jnp.max))
        return carry

    lax.fori_loop(lo, ib, score_loop, 0)
    m_scr[...] = jnp.broadcast_to(jnp.max(m_scr[...], axis=0, keepdims=True), m_scr.shape)

    p = jnp.exp2(s_scr[first, :] - m_scr[0:1])
    l_scr[...] = fold(p, jnp.sum)
    low = p.astype(bf16)
    p_out[first, :] = low
    for h in range(2):
        rows = slice(DH * h, DH * h + DH)
        to = slice(h * block + mid, (h + 1) * block)
        acc[rows] = dot(vt[rows, first], low[:, h * block : (h + 1) * block])
        p = jnp.exp2(s_scr[second, to] - m_scr[0:1, to])
        l_scr[:, to] += fold(p, jnp.sum)
        part = p.astype(bf16)
        p_out[second, to] = part
        acc[rows, mid:] += dot(vt[rows, second], part)

    def prob_loop(c, carry):
        rows = pl.ds(pl.multiple_of(c * block, block), block)
        p = jnp.exp2(s_scr[rows, :] - m_scr[0:1])
        l_scr[...] += fold(p, jnp.sum)
        low = p.astype(bf16)
        p_out[rows, :] = low
        for h in range(2):
            heads = slice(DH * h, DH * h + DH)
            acc[heads] += dot(vt[heads, rows], low[:, h * block : (h + 1) * block])
        return carry

    lax.fori_loop(lo, ib, prob_loop, 0)
    inverse = 1.0 / jnp.sum(l_scr[...], axis=0, keepdims=True)
    linv_out[...] = inverse
    attended = jnp.concatenate(
        [acc[DH * h : DH * h + DH] * inverse[:, h * block : (h + 1) * block] for h in range(2)],
        axis=0,
    )
    ot_out[...] = attended
    att_out[...] = attended.T.astype(bf16)


def attention_forward(
    kind, place, tokens, cot, gain, shift, wq, wk, wv, cbias, pbias, wp, st, ct, table, table_t,
    block,
):
    length, width = table.shape
    cols = wp.shape[1]
    count = length // block
    row = lambda n, w: pl.BlockSpec((n, w), lambda i: (i, 0))
    col = lambda n, w: pl.BlockSpec((n, w), lambda i: (0, i))
    smem = pl.BlockSpec(memory_space=pltpu.SMEM)
    shape = jax.ShapeDtypeStruct
    return pl.pallas_call(
        functools.partial(forward_body, block, length // 2),
        grid=(count,),
        in_specs=[
            smem, smem, row(block, width), row(block, width),
            whole((1, width)), whole((1, width)), *[whole((width, cols))] * 3,
            whole((1, cols)), whole((1, cols)), whole((width, cols)),
            col(width // 2, block), col(width // 2, block), row(block, width), col(width, block),
        ],
        out_specs=[
            row(block // 2, width), row(block // 2, width), row(block, width),
            row(block, cols), row(block, cols), row(block, cols), col(cols + width, block),
            col(length, 2 * block), col(cols, block), row(block, cols), col(1, 2 * block),
        ],
        out_shape=[
            shape((length // 2, width), bf16), shape((length // 2, width), bf16),
            shape((length, width), bf16),
            shape((length, cols), bf16), shape((length, cols), bf16), shape((length, cols), bf16),
            shape((cols + width, length), bf16),
            shape((length, 2 * length), bf16), shape((cols, length), f32),
            shape((length, cols), bf16), shape((1, 2 * length), f32),
        ],
        scratch_shapes=[
            pltpu.VMEM((width, 3 * cols), bf16),
            pltpu.VMEM((length, width + cols), bf16),
            pltpu.VMEM((cols, length), bf16),
            pltpu.VMEM((width + cols, 2 * block), bf16),
            pltpu.VMEM((length, 2 * block), f32),
            pltpu.VMEM((8, 2 * block), f32),
            pltpu.VMEM((8, 2 * block), f32),
            pltpu.VMEM((cols, block), f32),
        ],
        compiler_params=params(),
        cost_estimate=cost(25),
        name="attention_forward",
    )(
        kind, place, tokens, cot, gain, shift, wq, wk, wv, cbias, pbias, wp, st, ct, table, table_t
    )


def backward_body(
    count, block, half_rows,
    kind, place, p, d0, d1, d2, d3, ot, linv, qc, qp, v, ktt, wp, st, ct,
    wq, wk, wv, normed, gain, shift, sums,
    last, small, near, mine,
    wcat, acc, dk, dv, low, low_t, d_scr, dcat, dstack, qstack, delta, mom, colsum, dwp, cb, pb,
):
    step = pl.program_id(0)
    ib = count - 1 - step
    width, cols = wp.shape
    half = width // 2
    mid = block // 2
    own = d0.shape[0] // 2

    @pl.when(step == 0)
    def start():
        for ref in (dk, dv, dwp, cb, pb, mom, colsum):
            ref[...] = jnp.zeros(ref.shape, f32)
        for n, ref in enumerate((wq, wk, wv)):
            wcat[:, n * cols : (n + 1) * cols] = ref[...]
        for n, ref in enumerate((d0, d1, d2, d3)):
            for part in range(2):
                at = pl.multiple_of((4 * part + (place[0] ^ n)) * own, own)
                d_scr[pl.ds(at, own), :] = ref[part * own : (part + 1) * own]

    lo = jnp.where((kind[0] == 1) & (ib * block >= half_rows), half_rows // block, 0)
    here = pl.multiple_of(ib * block, block)
    dt = d_scr[pl.ds(here, block), :].astype(f32).T
    scaled = jnp.concatenate(
        [
            dt[DH * h : DH * h + DH] * linv[:, h * block : (h + 1) * block]
            for h in range(2)
        ],
        axis=0,
    )
    scaled_rows = scaled.T.astype(bf16)
    scaled = scaled.astype(bf16)
    product = scaled.astype(f32) * ot[...]
    for h in range(2):
        to = slice(h * block, (h + 1) * block)
        dcat[:, to] = keep_rows(scaled, h)
        dstack[to] = keep_cols(scaled_rows, h)
        qstack[to] = keep_cols(qc[...], h)
        delta[:, to] = jnp.sum(product[DH * h : DH * h + DH], axis=0, keepdims=True)

    first = pl.ds(here, mid)
    second = pl.ds(pl.multiple_of(here + mid, mid), mid)
    pt = p[first, :]
    dp = dot(v[first, :], dcat[...])
    ds = (pt.astype(f32) * (dp - delta[...])).astype(bf16)
    dv[first, :] += dot(pt, dstack[...])
    dk[first, :] += dot(ds, qstack[...])
    for h in range(2):
        to = slice(h * block + mid, (h + 1) * block)
        rows = slice(DH * h, DH * h + DH + width)
        acc[h] = dot(ktt[rows, first], ds[:, h * block : (h + 1) * block])
        pt2 = p[second, to]
        dp2 = dot(v[second, :], dcat[:, to])
        ds2 = (pt2.astype(f32) * (dp2 - delta[:, to])).astype(bf16)
        dv[second, :] += dot(pt2, dstack[to])
        dk[second, :] += dot(ds2, qstack[to])
        acc[h, :, mid:] += dot(ktt[rows, second], ds2)

    def loop(c, carry):
        rows = pl.ds(pl.multiple_of(c * block, block), block)
        pt = p[rows, :]
        dp = dot(v[rows, :], dcat[...])
        ds = (pt.astype(f32) * (dp - delta[...])).astype(bf16)
        dv[rows, :] += dot(pt, dstack[...])
        dk[rows, :] += dot(ds, qstack[...])
        for h in range(2):
            acc[h] += dot(
                ktt[DH * h : DH * h + DH + width, rows], ds[:, h * block : (h + 1) * block]
            )
        return carry

    lax.fori_loop(lo, ib, loop, 0)
    wpt = wp[...].astype(f32).T.astype(bf16)
    dqs = []
    for h in range(2):
        base = DH * (1 - h)
        gs = acc[h, base : base + half]
        gc = acc[h, base + half : base + width]
        rs = (st[...] * gc - ct[...] * gs).astype(bf16)
        rc = (ct[...] * gc + st[...] * gs).astype(bf16)
        wh = wpt[DH * h : DH * h + DH]
        by_position = (dot(wh[:, :half], rs) + dot(wh[:, half:], rc)) * 0.125
        by_content = acc[h, width * h : width * h + DH] * 0.125
        qph = keep_cols(qp[...], h)
        dwp[:half] += dot(rs, qph)
        dwp[half:] += dot(rc, qph)
        cb[DH * h : DH * h + DH] += by_content
        pb[DH * h : DH * h + DH] += by_position
        dqs.append(by_content + by_position)
    dqt = jnp.concatenate(dqs, axis=0)
    rows = pl.ds(here, block)
    for n, (value, value_t) in enumerate(
        ((dqt.T, dqt), (dk[rows, :], dk[rows, :].T), (dv[rows, :], dv[rows, :].T))
    ):
        to = slice(n * cols, (n + 1) * cols)
        low[:, to] = value.astype(bf16)
        low_t[to] = value_t.astype(bf16)
    mom[...] += dot(low_t[...], normed[...])
    colsum[...] += jnp.sum(low[...].astype(f32), axis=0, keepdims=True)
    for ref, core in ((near, 1 - place[1]), (mine, place[1])):
        at = pl.multiple_of(core * own, own)
        ref[...] = dot_nt(low[pl.ds(at, own), :], wcat[...]).astype(ref.dtype)

    @pl.when(step == count - 1)
    def finish():
        as_row = lambda values: jnp.broadcast_to(
            jnp.sum(values, axis=1, keepdims=True), (values.shape[0], 128)
        ).T[:1]
        column = jnp.broadcast_to(colsum[...], (8, 3 * cols)).T[:, :1]
        weights = wcat[...].astype(f32).T
        by_gain = jnp.sum(mom[...] * weights, axis=0, keepdims=True)
        by_shift = jnp.sum(column * weights, axis=0, keepdims=True)
        full = (gain[...] * mom[...] + shift[...] * column).T.astype(bf16)
        biases = jnp.concatenate(
            [as_row(cb[...]), as_row(pb[...]), jnp.zeros((1, width - 2 * cols), f32)], axis=1
        )
        small[...] = jnp.concatenate(
            [by_gain, by_shift, sums[...], biases, jnp.zeros((9, width), f32)], axis=0
        ).astype(bf16)
        last[:cols] = jnp.zeros((cols, width), bf16)
        last[cols:, : 3 * cols] = full
        last[cols:, 3 * cols :] = dwp[...].astype(bf16)


def attention_backward(
    kind, place, p, grads, ot, linv, qc, qp, v, ktt, wp, st, ct, wq, wk, wv, normed,
    gain, shift, sums, block,
):
    length, width = normed.shape
    cols = qc.shape[1]
    count = length // block
    quarter = length // 4
    col = lambda n, w: pl.BlockSpec((n, w), lambda i: (0, count - 1 - i))
    row = lambda n, w: pl.BlockSpec((n, w), lambda i: (count - 1 - i, 0))
    smem = pl.BlockSpec(memory_space=pltpu.SMEM)
    message = (cols + width, width)
    return pl.pallas_call(
        functools.partial(backward_body, count, block, length // 2),
        grid=(count,),
        in_specs=[
            smem, smem, col(length, 2 * block),
            *[whole((quarter, cols))] * 4,
            col(cols, block), col(1, 2 * block), row(block, cols), row(block, cols),
            whole(v.shape), whole(ktt.shape), whole(wp.shape),
            col(width // 2, block), col(width // 2, block),
            *[whole((width, cols))] * 3, row(block, width),
            whole(gain.shape), whole(shift.shape), whole(sums.shape),
        ],
        out_specs=[
            whole(message), whole((16, width)), row(block // 2, width), row(block // 2, width)
        ],
        out_shape=[
            jax.ShapeDtypeStruct(message, bf16),
            jax.ShapeDtypeStruct((16, width), bf16),
            jax.ShapeDtypeStruct((length // 2, width), bf16),
            jax.ShapeDtypeStruct((length // 2, width), bf16),
        ],
        scratch_shapes=[
            pltpu.VMEM((width, 3 * cols), bf16),
            pltpu.VMEM((2, DH + width, block), f32),
            pltpu.VMEM((length, cols), f32),
            pltpu.VMEM((length, cols), f32),
            pltpu.VMEM((block, 3 * cols), bf16),
            pltpu.VMEM((3 * cols, block), bf16),
            pltpu.VMEM((length, cols), bf16),
            pltpu.VMEM((cols, 2 * block), bf16),
            pltpu.VMEM((2 * block, cols), bf16),
            pltpu.VMEM((2 * block, cols), bf16),
            pltpu.VMEM((1, 2 * block), f32),
            pltpu.VMEM((3 * cols, width), f32),
            pltpu.VMEM((1, 3 * cols), f32),
            pltpu.VMEM((width, cols), f32),
            pltpu.VMEM((cols, block), f32),
            pltpu.VMEM((cols, block), f32),
        ],
        compiler_params=params(),
        cost_estimate=cost(8),
        name="attention_backward",
    )(
        kind, place, p, *grads, ot, linv, qc, qp, v, ktt, wp, st, ct, wq, wk, wv, normed,
        gain, shift, sums,
    )


def feed_body(
    place, tokens, cot, own_att, a1, a2, a3, w0, w1, w2, w3, i0, i1, u0, u1, b0, b1,
    bu, gain, shift,
    back_keep, back_send, out, res_own, bias, near, keep,
    hidden_t, act_t, pres, cots,
):
    step = pl.program_id(0)
    own, width = res_own.shape
    steps = cots.shape[0] // own

    @pl.when(step < steps)
    def rows():
        c = cot[...]
        residual = tokens[...].astype(f32)
        residual = residual + dot(own_att[...].reshape(own_att.shape[-2:]), w0[...])
        for att, wo in ((a1, w1), (a2, w2), (a3, w3)):
            residual = residual + dot(att[...], wo[...])
        normed, _ = norm_parts(residual)
        hidden = (normed * gain[...] + shift[...]).astype(bf16)
        here = pl.ds(pl.multiple_of(step * own, own), own)
        cots[here, :] = c
        hidden_t[:, here] = hidden.T
        mixed = 0.5 * (residual + bu[...])
        back = None
        sums = []
        for n, wi, wu, bi in ((0, i0, u0, b0), (1, i1, u1, b1)):
            x = dot(hidden, wi[...]) + bi[...]
            square = x * x
            t = jnp.tanh(GELU_A * x * (1.0 + GELU_B * square))
            act = (0.5 * x * (1.0 + t)).astype(bf16)
            slope = 0.5 * (1.0 + t) + (0.5 * GELU_A) * x * (1.0 - t * t) * (
                1.0 + (3.0 * GELU_B) * square
            )
            act_t[n, :, here] = act.T
            mixed = mixed + dot(act, wu[...])
            pre = (dot_nt(c, wu[...]) * slope).astype(bf16)
            pres[n, here, :] = pre
            sums.append(jnp.sum(pre.astype(f32), axis=0, keepdims=True))
            back_n = dot_nt(pre, wi[...])
            back = back_n if back is None else back + back_n
        out[...] = mixed.astype(bf16)
        sums = jnp.concatenate(sums, axis=0)

        @pl.when(step == 0)
        def first():
            bias[...] = sums

        @pl.when(step > 0)
        def later():
            bias[...] += sums

        @pl.when(step % 2 == place[2])
        def mine():
            res_own[...] = residual
            back_keep[...] = back.astype(bf16)

        @pl.when(step % 2 != place[2])
        def other():
            back_send[...] = back.astype(bf16)

    for n, ref in ((1, near), (0, keep)):

        @pl.when(step == steps + 1 - n)
        def grads(n=n, ref=ref):
            parts, length, _ = ref.shape
            share = length // 2
            inner = dot(hidden_t[...], pres[n]).astype(bf16)
            outer = dot(act_t[n], cots[...]).astype(bf16)
            for r in range(parts):
                ref[r, :share] = inner[r * share : (r + 1) * share]
                ref[r, share:] = outer[r * share : (r + 1) * share]


def feed(place, tokens, cot, own_att, atts, wos, wis, wus, bis, bu, gain, shift):
    rows, width = tokens.shape
    cols = own_att.shape[1]
    share = wis[0].shape[1]
    own = rows // 4
    spec = lambda s: pl.BlockSpec(s, lambda i, place: (0,) * len(s))
    at = lambda i: jnp.minimum(i, 3)
    step = lambda w: pl.BlockSpec((own, w), lambda i, place: (at(i), 0))
    half = pl.BlockSpec((own, width), lambda i, place: (at(i) // 2, 0))
    parts = first_parts()
    grad_shape = (parts, (width + share) // parts, width)
    att = pl.BlockSpec((1, 1, own, cols), lambda i, place: (at(i), place[1], 0, 0))
    others = (*wos, *wis, *wus, *bis, bu, gain, shift)
    shape = jax.ShapeDtypeStruct
    return pl.pallas_call(
        feed_body,
        grid_spec=pltpu.PrefetchScalarGridSpec(
            num_scalar_prefetch=1,
            grid=(6,),
            in_specs=[step(width), step(width), att]
            + [step(cols)] * 3
            + [spec(o.shape) for o in others],
            out_specs=[
                half, half, step(width), half, spec((2, share)), spec(grad_shape),
                spec(grad_shape),
            ],
            scratch_shapes=[
                pltpu.VMEM((width, rows), bf16),
                pltpu.VMEM((2, share, rows), bf16),
                pltpu.VMEM((2, rows, share), bf16),
                pltpu.VMEM((rows, width), bf16),
            ],
        ),
        out_shape=[
            shape((2 * own, width), bf16), shape((2 * own, width), bf16),
            shape((rows, width), bf16), shape((2 * own, width), f32), shape((2, share), f32),
            shape(grad_shape, bf16), shape(grad_shape, bf16),
        ],
        compiler_params=params(),
        cost_estimate=cost(13),
        name="feed",
    )(place, tokens, cot, own_att.reshape(4, 2, own, cols), *atts, *others)


def turn_body(
    place, keep, got, residual, cot, a0, a1, a2, a3, w0, w1, w2, w3, gain,
    res_out, sums_out, g0, g1, g2, g3, o0, o1, o2, o3, total,
):
    step = pl.program_id(0)
    back = keep[...].astype(f32) + got[...].astype(f32)
    c = cot[...].astype(f32)
    normed, scale = norm_parts(residual[...])
    fold = lambda values: jnp.sum(values, axis=0, keepdims=True)
    sums = jnp.concatenate([fold(back * normed), fold(back), fold(c)], axis=0)
    e = back * gain[...]
    inner = (
        e
        - jnp.mean(e, axis=-1, keepdims=True)
        - normed * jnp.mean(e * normed, axis=-1, keepdims=True)
    )
    res = c + scale * inner
    branch = res.astype(bf16)
    res_out[...] = branch
    for wo, out in ((w0, g0), (w1, g1), (w2, g2), (w3, g3)):
        out[...] = dot_nt(branch, wo[...]).astype(bf16)
    products = [dot(att[...].T, branch) for att in (a0, a1, a2, a3)]

    @pl.when(step == 0)
    def first():
        sums_out[...] = sums
        for n in range(4):
            total[n] = products[n]

    @pl.when(step == 1)
    def second():
        sums_out[...] += sums
        for n, out in enumerate((o0, o1, o2, o3)):
            out[...] = (total[n] + products[n]).astype(out.dtype)


def turn(place, keep, got, residual, cot, own_att, others, wos, gain):
    rows, width = keep.shape
    own = rows // 2
    cols = wos[0].shape[0]
    spec = lambda s: pl.BlockSpec(s, lambda i, place: (0,) * len(s))
    step = lambda w: pl.BlockSpec((own, w), lambda i, place: (i, 0))
    half = lambda w: pl.BlockSpec((own, w), lambda i, place: (2 * i + place[2], 0))
    shapes = [((rows, width), bf16), ((3, width), f32)]
    shapes = shapes + [((rows, cols), bf16)] * 4
    shapes = shapes + [((cols, width), t) for t in (f32, bf16, bf16, bf16)]
    return pl.pallas_call(
        turn_body,
        grid_spec=pltpu.PrefetchScalarGridSpec(
            num_scalar_prefetch=1,
            grid=(2,),
            in_specs=[step(width), step(width), step(width), half(width)]
            + [pl.BlockSpec((own, cols), lambda i, place: (4 * i + place[0], 0))]
            + [half(cols)] * 3
            + [spec(w.shape) for w in wos]
            + [spec(gain.shape)],
            out_specs=[step(width), spec((3, width))]
            + [step(cols)] * 4
            + [spec((cols, width))] * 4,
            scratch_shapes=[pltpu.VMEM((4, cols, width), f32)],
        ),
        out_shape=[jax.ShapeDtypeStruct(s, t) for s, t in shapes],
        compiler_params=params(),
        cost_estimate=cost(60),
        name="turn",
    )(place, keep, got, residual, cot, own_att, *others, *wos, gain)


def close_body(place, keep0, keep1, near0, near1, got, t0, t1, res, gain, out):
    own = t0.shape[0]
    for part, keep, near, tokens in ((0, keep0, near0, t0), (1, keep1, near1, t1)):
        rows = slice(part * own, (part + 1) * own)
        total = keep[...].astype(f32) + near[...].astype(f32) + got[rows].astype(f32)
        normed, scale = norm_parts(tokens[...].astype(f32))
        e = total * gain[...]
        inner = (
            e
            - jnp.mean(e, axis=-1, keepdims=True)
            - normed * jnp.mean(e * normed, axis=-1, keepdims=True)
        )
        out[rows] = (res[rows].astype(f32) + scale * inner).astype(bf16)


def close(place, keep, near, got, tokens, res, gain):
    rows, width = got.shape
    own = rows // 2
    spec = pl.BlockSpec((rows, width), lambda i, place: (0, 0))
    at = lambda part: pl.BlockSpec((own, width), lambda i, place: (2 * part + place[2], 0))
    return pl.pallas_call(
        close_body,
        grid_spec=pltpu.PrefetchScalarGridSpec(
            num_scalar_prefetch=1,
            grid=(1,),
            in_specs=[
                at(0), at(1), at(0), at(1), spec, at(0), at(1), spec,
                pl.BlockSpec((1, width), lambda i, place: (0, 0)),
            ],
            out_specs=spec,
        ),
        out_shape=jax.ShapeDtypeStruct((rows, width), bf16),
        compiler_params=params(),
        cost_estimate=cost(2),
        name="close",
    )(place, keep, keep, near, near, got, tokens, tokens, res, gain)


def collect_body(place, m0, m1, g0, g1, g2, g3, mixed, grad, sems):
    own = g0.shape[0] // 2
    core = place[1]
    copies = []
    for part in range(2):
        for flip, ref in ((0, m0), (1, m1)):
            for at_high in range(2):
                put = pl.multiple_of((4 * part + 2 * at_high + (core ^ flip)) * own, own)
                copies.append((ref.at[pl.ds((2 * part + at_high) * own, own)], mixed, put))
        for n, ref in enumerate((g0, g1, g2, g3)):
            put = pl.multiple_of((4 * part + (place[0] ^ n)) * own, own)
            copies.append((ref.at[pl.ds(part * own, own)], grad, put))
    copies = [
        pltpu.make_async_copy(source, target.at[pl.ds(put, own)], sems.at[at])
        for at, (source, target, put) in enumerate(copies)
    ]
    for copy in copies:
        copy.start()
    for copy in copies:
        copy.wait()


def collect(place, mixed, grads):
    rows, width = grads[0].shape
    hbm = pl.BlockSpec(memory_space=pl.ANY)
    shape = jax.ShapeDtypeStruct((4 * rows, width), bf16)
    return pl.pallas_call(
        collect_body,
        in_specs=[pl.BlockSpec(memory_space=pltpu.SMEM)]
        + [pl.BlockSpec(memory_space=pltpu.VMEM)] * 6,
        out_specs=[hbm] * 2,
        out_shape=[shape] * 2,
        scratch_shapes=[pltpu.SemaphoreType.DMA((16,))],
        compiler_params=pltpu.CompilerParams(vmem_limit_bytes=16 * 2**20),
        cost_estimate=cost(3),
        name="collect",
    )(place, *mixed, *grads)


def swap(value, axis, mask):
    size = lax.axis_size(axis)
    return lax.ppermute(value, axis, [(i, i ^ mask) for i in range(size)])


def block_of(value, index, count):
    return lax.dynamic_slice_in_dim(value, index * count, count, 0)


def levels(size):
    bits = size.bit_length() - 1
    out = []
    shift = 0
    while shift < bits:
        wide = min(3, bits - shift)
        out.append((shift, wide))
        shift += wide
    return out


def groups_of(shift, wide):
    size = lax.axis_size("dp")
    count = 1 << wide
    return [
        [base + (n << shift) for n in range(count)]
        for base in range(size)
        if not (base >> shift) & (count - 1)
    ]


def exchange(value, shift, wide):
    return lax.all_to_all(
        value, "dp", split_axis=0, concat_axis=0, tiled=True,
        axis_index_groups=None if 1 << wide == lax.axis_size("dp") else groups_of(shift, wide),
    )


def gather_dp(value):
    sizes = [1 << wide for _, wide in levels(lax.axis_size("dp"))]
    whole_value = lax.all_gather(value, "dp", axis=0)
    if len(sizes) > 1:
        whole_value = whole_value.reshape(*sizes[::-1], *value.shape)
        whole_value = whole_value.transpose(
            *reversed(range(len(sizes))), len(sizes), len(sizes) + 1
        )
    return whole_value.reshape(sizes[0], -1, value.shape[1])


def first_parts():
    return 1 << levels(lax.axis_size("dp"))[0][1]


def start_dp(parts):
    return exchange(parts, *levels(lax.axis_size("dp"))[0])


def fold_dp(got):
    total = jnp.sum(got.astype(f32), axis=0)
    for shift, wide in levels(lax.axis_size("dp"))[1:]:
        parts = total.astype(bf16).reshape(1 << wide, -1, total.shape[1])
        total = jnp.sum(exchange(parts, shift, wide).astype(f32), axis=0)
    return total.astype(bf16)


def masks():
    return [1 << bit for bit in range(lax.axis_size("dp").bit_length() - 1)]


def halves(value, mask):
    bit = (lax.axis_index("dp") & mask) != 0
    rows = value.shape[0] // 2
    low, high = value[:rows], value[rows:]
    return jnp.where(bit, low, high), jnp.where(bit, high, low)


def give(value, small, mask):
    return jnp.concatenate([halves(value, mask)[0], small], axis=0)


def halve_dp(value, small, mask, other=None):
    got, other = lax.optimization_barrier((swap(give(value, small, mask), "dp", mask), other))
    got = got.astype(f32)
    kept = halves(value, mask)[1]
    rows = kept.shape[0]
    value = (kept.astype(f32) + got[:rows]).astype(bf16)
    return value, (small.astype(f32) + got[rows:]).astype(bf16), other


def after(value, *others):
    return lax.optimization_barrier((value, others))[0]


def double_dp(value, mask, other=None):
    bit = (lax.axis_index("dp") & mask) != 0
    got, other = lax.optimization_barrier((swap(value, "dp", mask), other))
    value = jnp.concatenate([jnp.where(bit, got, value), jnp.where(bit, value, got)], axis=0)
    return value, other


def by_index(value):
    bits = len(masks())
    width = value.shape[-1]
    value = value.reshape((2,) * bits + (-1, width)).transpose(*reversed(range(bits)), bits, bits + 1)
    wides = [wide for _, wide in levels(lax.axis_size("dp"))]
    value = value.reshape(*[1 << wide for wide in reversed(wides)], -1, width)
    count = len(wides)
    value = value.transpose(*reversed(range(count)), count, count + 1)
    return value.reshape(1 << wides[0], -1, width)


def shards(
    tokens, item_kind, first_gain, first_shift, query_weight, key_weight, value_weight,
    position_weight, content_bias, position_bias, output_weight, second_gain, second_shift,
    inner_weight, inner_bias, outer_weight, outer_bias, cotangent,
):
    length, width = tokens.shape
    cols = query_weight.shape[1]
    share = inner_weight.shape[1]
    mp = lax.axis_index("mp").astype(jnp.int32)
    core, high = mp & 1, mp >> 1
    place = jnp.stack([mp, core, high])
    half = length // 2
    block = min(512, half)
    per_half = half // block
    own = half // 4
    sin_table, cos_table = sinusoid(length, width)
    table = jnp.asarray(np.concatenate([sin_table, cos_table], axis=1), bf16)
    table_t = jnp.asarray(np.concatenate([sin_table, cos_table], axis=1).T, bf16)
    st = jnp.asarray(sin_table.T, f32)
    ct = jnp.asarray(cos_table.T, f32)
    gain1, shift1, gain2, shift2, bu = (
        v[None] for v in (first_gain, first_shift, second_gain, second_shift, outer_bias)
    )

    tie = lax.optimization_barrier
    wos = [output_weight] + [swap(output_weight, "mp", n) for n in (1, 2, 3)]
    bis = [inner_bias[None], swap(inner_bias[None], "mp", 1)]
    projections = (query_weight, key_weight, value_weight)
    tokens_own, cot_own, normed, qc, qp, v, ktt, p, ot, attended, linv = attention_forward(
        item_kind, place, tokens, cotangent, gain1, shift1, *projections, content_bias[None],
        position_bias[None], position_weight, st, ct, table, table_t, block,
    )
    blocks = attended.reshape(4, 2, own, cols)
    pick = lambda c: lax.dynamic_index_in_dim(blocks, c, 1, False).reshape(4 * own, cols)
    near, far = pick(1 - core), pick(core)
    near, far, wi, wu, wos, bis = tie((near, far, inner_weight, outer_weight, wos, bis))
    wis = [inner_weight, swap(wi, "mp", 1)]
    wus = [outer_weight, swap(wu, "mp", 1)]
    atts = [swap(near, "mp", 1), swap(far, "mp", 2), swap(near, "mp", 3)]
    back_keep, back_send, out, residual, bias, near, keep = feed(
        place, tokens_own, cot_own, attended, atts, wos, wis, wus, bis, bu, gain2, shift2
    )
    back_got = swap(back_send, "mp", 2)
    near_got = swap(near, "mp", 1)
    feed_sum = (keep.astype(f32) + near_got.astype(f32)).astype(bf16)
    feed_got = start_dp(feed_sum)

    res, sums, *turned = turn(
        place, back_keep, back_got, residual, cot_own, attended, atts, wos, gain2
    )
    grads, weight_parts = turned[:4], turned[4:]
    grads = [grads[0]] + [swap(grads[n], "mp", n) for n in (1, 2, 3)]
    sums = jnp.concatenate([sums, bias[:1] + swap(bias[1:], "mp", 1)], axis=0)
    grads, weight_parts, out_send, sums = tie((grads, weight_parts, out, sums))
    weight_parts = [weight_parts[0]] + [swap(weight_parts[n], "mp", n) for n in (1, 2, 3)]
    out_got = swap(out_send, "mp", 2)

    last, small, near, keep = attention_backward(
        item_kind, place, p, grads, ot, linv, qc, qp, v, ktt, position_weight,
        st, ct, *projections, normed, gain1, shift1, sums, block,
    )
    last, small, near, keep, weight_parts, out_got, feed_got = tie(
        (last, small, near, keep, weight_parts, out_got, feed_got)
    )
    near = swap(near, "mp", 1)
    out_sum = sum(x.astype(f32) for x in weight_parts).astype(bf16)
    last = lax.dynamic_update_slice(last, out_sum, (0, 0))
    pick = lambda x: lax.dynamic_index_in_dim(x.reshape(2, 2, own, width), 1 - high, 1, False)
    far = (pick(keep).astype(f32) + pick(near).astype(f32)).astype(bf16).reshape(2 * own, width)
    first, *middle = masks()
    feed_total = fold_dp(after(feed_got, give(last, small, first), far))
    far = swap(far, "mp", 2)

    last, small, far = halve_dp(last, small, first, far)
    mixed = (out.astype(f32) + out_got.astype(f32)).astype(bf16)
    mixed = [mixed, swap(mixed, "mp", 1)]
    grad = close(place, keep, near, far, tokens_own, res, gain1)
    beyond = swap(grad, "mp", 2)
    for mask in reversed(masks()):
        feed_total, _ = double_dp(feed_total, mask)
    for mask in middle:
        last, small, _ = halve_dp(last, small, mask)
    for mask in reversed(middle):
        last, _ = double_dp(last, mask)
    tokens_grad = [grad, swap(grad, "mp", 1), beyond, swap(beyond, "mp", 1)]
    small = after(small, last)
    mixed, tokens_grad = collect(place, mixed, tokens_grad)
    last_total, (mixed, tokens_grad) = double_dp(last, first, (mixed, tokens_grad))
    last_total = last_total.astype(f32)
    last_small = small.astype(f32)
    feed_total = by_index(feed_total)

    summed = last_small[:5]
    summed = summed + swap(summed, "mp", 1)
    summed = summed + swap(summed, "mp", 2)
    feed_total = feed_total.astype(f32)
    split = width // first_parts()
    inner_grad = feed_total[:, :split].reshape(width, share)
    outer_grad = feed_total[:, split:].reshape(share, width)
    whole_grad = last_total[cols:]

    return (
        mixed,
        tokens_grad,
        summed[0],
        summed[1],
        whole_grad[:, :cols],
        whole_grad[:, cols : 2 * cols],
        whole_grad[:, 2 * cols : 3 * cols],
        whole_grad[:, 3 * cols :],
        last_small[6, :cols],
        last_small[6, cols : 2 * cols],
        last_total[:cols],
        summed[2],
        summed[3],
        inner_grad,
        last_small[5],
        outer_grad,
        summed[4],
    )


def solution(mesh):
    return jax.shard_map(
        shards,
        mesh=mesh,
        in_specs=(
            P("dp", None), P("dp"), P(), P(), P(None, "mp"), P(None, "mp"), P(None, "mp"),
            P(None, "mp"), P("mp"), P("mp"), P("mp", None), P(), P(), P(None, "mp"), P("mp"),
            P("mp", None), P(), P("dp", None),
        ),
        out_specs=(
            P("dp", None), P("dp", None), P(), P(), P(None, "mp"), P(None, "mp"), P(None, "mp"),
            P(None, "mp"), P("mp"), P("mp"), P("mp", None), P(), P(), P(None, "mp"), P("mp"),
            P("mp", None), P(),
        ),
        check_vma=False,
    )
```

```python
import functools
import math

import jax
import jax.numpy as jnp
import numpy as np
from jax import lax
from jax.experimental import pallas as pl
from jax.experimental.pallas import tpu as pltpu
from jax.sharding import PartitionSpec as P

DH = 64
EPS = 1e-05
NEG = -1e30
LOG2E = 1.4426950408889634
GELU_A = 0.7978845608028654
GELU_B = 0.044715

f32 = jnp.float32
bf16 = jnp.bfloat16


def sinusoid(count, model_width):
    freqs = np.exp(np.arange(model_width // 2) * (-2.0 * math.log(10000.0) / model_width))
    angles = np.arange(count)[:, None] * freqs[None, :]
    return np.sin(angles), np.cos(angles)


def dot(left, right):
    return jnp.dot(left, right, preferred_element_type=f32)


def dot_nt(left, right):
    return lax.dot_general(left, right, (((1,), (1,)), ((), ())), preferred_element_type=f32)


def whole(shape):
    return pl.BlockSpec(shape, lambda *ids: (0,) * len(shape))


def params(mib=60):
    return pltpu.CompilerParams(
        vmem_limit_bytes=mib * 2**20, dimension_semantics=("arbitrary",)
    )


def cost(microseconds):
    return pl.CostEstimate(
        flops=int(microseconds * 1.1e9), bytes_accessed=1 << 10, transcendentals=0
    )


def keep_rows(values, head):
    ids = lax.broadcasted_iota(jnp.int32, values.shape, 0)
    return jnp.where(ids // DH == head, values, jnp.zeros_like(values))


def keep_cols(values, head):
    ids = lax.broadcasted_iota(jnp.int32, values.shape, 1)
    return jnp.where(ids // DH == head, values, jnp.zeros_like(values))


def norm_parts(values):
    center = values - jnp.mean(values, axis=-1, keepdims=True)
    spread = jnp.mean(center * center, axis=-1, keepdims=True)
    scale = lax.rsqrt(spread + EPS)
    return center * scale, scale


def forward_body(
    block, half_rows,
    kind, tokens, gain, shift, wq, wk, wv, cbias, pbias, wp, st, ct, table,
    normed_out, qc_out, qp_out, v_out, kt_out, p_out, ot_out, att_out, linv_out,
    pbuf, puts, sems, wcat, kcat, vt, qa, s_scr, m_scr, l_scr, acc,
):
    ib = pl.program_id(0)
    here = pl.multiple_of(ib * block, block)
    width, cols = wp.shape
    half = width // 2
    mid = block // 2

    def put(of, c, slot):
        at = pl.multiple_of(c * block, block), pl.multiple_of(of * 2 * block, 2 * block)
        target = p_out.at[pl.ds(at[0], block), pl.ds(at[1], 2 * block)]
        return pltpu.make_async_copy(pbuf.at[slot], target, sems.at[slot])

    @pl.when(ib == 0)
    def start():
        puts[0] = 0
        for n, ref in enumerate((wq, wk, wv)):
            wcat[:, n * cols : (n + 1) * cols] = ref[...]

    normed, _ = norm_parts(tokens[...].astype(f32))
    normed_out[...] = normed.astype(bf16)
    hidden = (normed * gain[...] + shift[...]).astype(bf16)
    qkv = dot(hidden, wcat[...])
    queries, keys, values = (qkv[:, n * cols : (n + 1) * cols] for n in range(3))
    qc_out[...] = ((queries + cbias[...]) * 0.125).astype(bf16)
    qp_out[...] = ((queries + pbias[...]) * 0.125).astype(bf16)
    v_out[...] = values.astype(bf16)
    kcat[pl.ds(here, block), :width] = table[...]
    kcat[pl.ds(here, block), width:] = keys.astype(bf16)
    vt[:, pl.ds(here, block)] = values.T.astype(bf16)
    kt_out[...] = keys.T.astype(bf16)
    queries_t = queries.T
    column = lambda row: jnp.broadcast_to(row, (8, row.shape[1])).T[:, :1]
    content = ((queries_t + column(cbias[...])) * (0.125 * LOG2E)).astype(bf16)
    position = ((queries_t + column(pbias[...])) * (0.125 * LOG2E)).astype(bf16)
    for h in range(2):
        u = dot(wp[...], keep_rows(position, h))
        us, uc = u[:half], u[half:]
        to = slice(h * block, (h + 1) * block)
        qa[:half, to] = (uc * st[...] - us * ct[...]).astype(bf16)
        qa[half:width, to] = (us * st[...] + uc * ct[...]).astype(bf16)
        qa[width:, to] = keep_rows(content, h)
    lo = jnp.where((kind[0] == 1) & (ib * block >= half_rows), half_rows // block, 0)
    fold = lambda x, op: op(x.reshape(x.shape[0] // 8, 8, x.shape[1]), axis=0)
    rj = lax.broadcasted_iota(jnp.int32, (mid, block), 0)
    ri = lax.broadcasted_iota(jnp.int32, (mid, block), 1)
    first = pl.ds(here, mid)
    second = pl.ds(pl.multiple_of(here + mid, mid), mid)

    s = dot(kcat[first, :], qa[...])
    s = jnp.where(jnp.concatenate([rj <= ri] * 2, axis=1), s, NEG)
    s_scr[first, :] = s
    m_scr[...] = fold(s, jnp.max)
    for h in range(2):
        to = slice(h * block + mid, (h + 1) * block)
        s = dot(kcat[second, :], qa[:, to])
        s = jnp.where(rj[:, :mid] <= ri[:, :mid], s, NEG)
        s_scr[second, to] = s
        m_scr[:, to] = jnp.maximum(m_scr[:, to], fold(s, jnp.max))

    def score_loop(c, carry):
        rows = pl.ds(pl.multiple_of(c * block, block), block)
        s = dot(kcat[rows, :], qa[...])
        s_scr[rows, :] = s
        m_scr[...] = jnp.maximum(m_scr[...], fold(s, jnp.max))
        return carry

    lax.fori_loop(lo, ib, score_loop, 0)
    m_scr[...] = jnp.broadcast_to(jnp.max(m_scr[...], axis=0, keepdims=True), m_scr.shape)

    done = puts[0]
    slot = done & 1

    @pl.when(done >= 2)
    def free():
        put(ib, ib, slot).wait()

    p = jnp.exp2(s_scr[first, :] - m_scr[0:1])
    l_scr[...] = fold(p, jnp.sum)
    low = p.astype(bf16)
    pbuf[slot, :mid] = low
    for h in range(2):
        rows = slice(DH * h, DH * h + DH)
        to = slice(h * block + mid, (h + 1) * block)
        acc[rows] = dot(vt[rows, first], low[:, h * block : (h + 1) * block])
        p = jnp.exp2(s_scr[second, to] - m_scr[0:1, to])
        l_scr[:, to] += fold(p, jnp.sum)
        part = p.astype(bf16)
        pbuf[slot, mid:, to] = part
        acc[rows, mid:] += dot(vt[rows, second], part)

    put(ib, ib, slot).start()

    def prob_loop(c, done):
        slot = done & 1

        @pl.when(done >= 2)
        def free():
            put(ib, c, slot).wait()

        rows = pl.ds(pl.multiple_of(c * block, block), block)
        p = jnp.exp2(s_scr[rows, :] - m_scr[0:1])
        l_scr[...] += fold(p, jnp.sum)
        low = p.astype(bf16)
        pbuf[slot] = low
        put(ib, c, slot).start()
        for h in range(2):
            heads = slice(DH * h, DH * h + DH)
            acc[heads] += dot(vt[heads, rows], low[:, h * block : (h + 1) * block])
        return done + 1

    puts[0] = lax.fori_loop(lo, ib, prob_loop, done + 1)
    inverse = 1.0 / jnp.sum(l_scr[...], axis=0, keepdims=True)
    linv_out[...] = inverse
    attended = jnp.concatenate(
        [acc[DH * h : DH * h + DH] * inverse[:, h * block : (h + 1) * block] for h in range(2)],
        axis=0,
    )
    ot_out[...] = attended
    att_out[...] = attended.T.astype(bf16)

    @pl.when(ib == pl.num_programs(0) - 1)
    def finish():
        for slot in range(2):
            put(ib, ib, slot).wait()


def attention_forward(
    kind, tokens, gain, shift, wq, wk, wv, cbias, pbias, wp, st, ct, table, block
):
    length, width = table.shape
    cols = wp.shape[1]
    count = length // block
    row = lambda n, w: pl.BlockSpec((n, w), lambda i: (i, 0))
    col = lambda n, w: pl.BlockSpec((n, w), lambda i: (0, i))
    shape = jax.ShapeDtypeStruct
    return pl.pallas_call(
        functools.partial(forward_body, block, length // 2),
        grid=(count,),
        in_specs=[
            pl.BlockSpec(memory_space=pltpu.SMEM), row(block, width),
            whole((1, width)), whole((1, width)), *[whole((width, cols))] * 3,
            whole((1, cols)), whole((1, cols)), whole((width, cols)),
            col(width // 2, block), col(width // 2, block), row(block, width),
        ],
        out_specs=[
            row(block, width), row(block, cols), row(block, cols), row(block, cols),
            col(cols, block), pl.BlockSpec(memory_space=pl.ANY), col(cols, block),
            row(block, cols), col(1, 2 * block),
        ],
        out_shape=[
            shape((length, width), bf16),
            shape((length, cols), bf16), shape((length, cols), bf16), shape((length, cols), bf16),
            shape((cols, length), bf16),
            shape((length, 2 * length), bf16), shape((cols, length), f32),
            shape((length, cols), bf16), shape((1, 2 * length), f32),
        ],
        scratch_shapes=[
            pltpu.VMEM((2, block, 2 * block), bf16),
            pltpu.SMEM((1,), jnp.int32),
            pltpu.SemaphoreType.DMA((2,)),
            pltpu.VMEM((width, 3 * cols), bf16),
            pltpu.VMEM((length, width + cols), bf16),
            pltpu.VMEM((cols, length), bf16),
            pltpu.VMEM((width + cols, 2 * block), bf16),
            pltpu.VMEM((length, 2 * block), f32),
            pltpu.VMEM((8, 2 * block), f32),
            pltpu.VMEM((8, 2 * block), f32),
            pltpu.VMEM((cols, block), f32),
        ],
        compiler_params=params(),
        cost_estimate=cost(25),
        name="attention_forward",
    )(kind, tokens, gain, shift, wq, wk, wv, cbias, pbias, wp, st, ct, table)


def backward_body(
    count, block, half_rows,
    kind, place, p, d0, d1, d2, d3, ot, linv, qc, qp, v, kt, tt, wp, st, ct,
    wq, wk, wv, normed, gain, shift, sums,
    given, kept, small, near, mine,
    last, ktt, wcat, acc, dk, dv, low, low_t, d_scr, dcat, dstack, qstack, delta, mom, colsum, dwp, cb, pb,
):
    step = pl.program_id(0)
    ib = count - 1 - step
    width, cols = wp.shape
    half = width // 2
    mid = block // 2
    own = d0.shape[0] // 2

    @pl.when(step == 0)
    def start():
        for ref in (dk, dv, dwp, cb, pb, mom, colsum):
            ref[...] = jnp.zeros(ref.shape, f32)
        for n, ref in enumerate((wq, wk, wv)):
            wcat[:, n * cols : (n + 1) * cols] = ref[...]
        ktt[:DH] = kt[:DH]
        ktt[DH : DH + width] = tt[...]
        ktt[DH + width :] = kt[DH:]
        for n, ref in enumerate((d0, d1, d2, d3)):
            for part in range(2):
                at = pl.multiple_of((4 * part + (place[0] ^ n)) * own, own)
                d_scr[pl.ds(at, own), :] = ref[part * own : (part + 1) * own]

    lo = jnp.where((kind[0] == 1) & (ib * block >= half_rows), half_rows // block, 0)
    here = pl.multiple_of(ib * block, block)
    dt = d_scr[pl.ds(here, block), :].astype(f32).T
    scaled = jnp.concatenate(
        [
            dt[DH * h : DH * h + DH] * linv[:, h * block : (h + 1) * block]
            for h in range(2)
        ],
        axis=0,
    )
    scaled_rows = scaled.T.astype(bf16)
    scaled = scaled.astype(bf16)
    product = scaled.astype(f32) * ot[...]
    for h in range(2):
        to = slice(h * block, (h + 1) * block)
        dcat[:, to] = keep_rows(scaled, h)
        dstack[to] = keep_cols(scaled_rows, h)
        qstack[to] = keep_cols(qc[...], h)
        delta[:, to] = jnp.sum(product[DH * h : DH * h + DH], axis=0, keepdims=True)

    first = pl.ds(here, mid)
    second = pl.ds(pl.multiple_of(here + mid, mid), mid)
    pt = p[first, :]
    dp = dot(v[first, :], dcat[...])
    ds = (pt.astype(f32) * (dp - delta[...])).astype(bf16)
    dv[first, :] += dot(pt, dstack[...])
    dk[first, :] += dot(ds, qstack[...])
    for h in range(2):
        to = slice(h * block + mid, (h + 1) * block)
        rows = slice(DH * h, DH * h + DH + width)
        acc[h] = dot(ktt[rows, first], ds[:, h * block : (h + 1) * block])
        pt2 = p[second, to]
        dp2 = dot(v[second, :], dcat[:, to])
        ds2 = (pt2.astype(f32) * (dp2 - delta[:, to])).astype(bf16)
        dv[second, :] += dot(pt2, dstack[to])
        dk[second, :] += dot(ds2, qstack[to])
        acc[h, :, mid:] += dot(ktt[rows, second], ds2)

    def loop(c, carry):
        rows = pl.ds(pl.multiple_of(c * block, block), block)
        pt = p[rows, :]
        dp = dot(v[rows, :], dcat[...])
        ds = (pt.astype(f32) * (dp - delta[...])).astype(bf16)
        dv[rows, :] += dot(pt, dstack[...])
        dk[rows, :] += dot(ds, qstack[...])
        for h in range(2):
            acc[h] += dot(
                ktt[DH * h : DH * h + DH + width, rows], ds[:, h * block : (h + 1) * block]
            )
        return carry

    lax.fori_loop(lo, ib, loop, 0)
    wpt = wp[...].astype(f32).T.astype(bf16)
    dqs = []
    for h in range(2):
        base = DH * (1 - h)
        gs = acc[h, base : base + half]
        gc = acc[h, base + half : base + width]
        rs = (st[...] * gc - ct[...] * gs).astype(bf16)
        rc = (ct[...] * gc + st[...] * gs).astype(bf16)
        wh = wpt[DH * h : DH * h + DH]
        by_position = (dot(wh[:, :half], rs) + dot(wh[:, half:], rc)) * 0.125
        by_content = acc[h, width * h : width * h + DH] * 0.125
        qph = keep_cols(qp[...], h)
        dwp[:half] += dot(rs, qph)
        dwp[half:] += dot(rc, qph)
        cb[DH * h : DH * h + DH] += by_content
        pb[DH * h : DH * h + DH] += by_position
        dqs.append(by_content + by_position)
    dqt = jnp.concatenate(dqs, axis=0)
    rows = pl.ds(here, block)
    for n, (value, value_t) in enumerate(
        ((dqt.T, dqt), (dk[rows, :], dk[rows, :].T), (dv[rows, :], dv[rows, :].T))
    ):
        to = slice(n * cols, (n + 1) * cols)
        low[:, to] = value.astype(bf16)
        low_t[to] = value_t.astype(bf16)
    mom[...] += dot(low_t[...], normed[...])
    colsum[...] += jnp.sum(low[...].astype(f32), axis=0, keepdims=True)
    for ref, core in ((near, 1 - place[1]), (mine, place[1])):
        at = pl.multiple_of(core * own, own)
        ref[...] = dot_nt(low[pl.ds(at, own), :], wcat[...]).astype(ref.dtype)

    @pl.when(step == count - 1)
    def finish():
        as_row = lambda values: jnp.broadcast_to(
            jnp.sum(values, axis=1, keepdims=True), (values.shape[0], 128)
        ).T[:1]
        column = jnp.broadcast_to(colsum[...], (8, 3 * cols)).T[:, :1]
        weights = wcat[...].astype(f32).T
        by_gain = jnp.sum(mom[...] * weights, axis=0, keepdims=True)
        by_shift = jnp.sum(column * weights, axis=0, keepdims=True)
        full = (gain[...] * mom[...] + shift[...] * column).T.astype(bf16)
        biases = jnp.concatenate(
            [as_row(cb[...]), as_row(pb[...]), jnp.zeros((1, width - 2 * cols), f32)], axis=1
        )
        small[...] = jnp.concatenate(
            [by_gain, by_shift, sums[...], biases, jnp.zeros((9, width), f32)], axis=0
        ).astype(bf16)
        last[:cols] = jnp.zeros((cols, width), bf16)
        last[cols:, : 3 * cols] = full
        last[cols:, 3 * cols :] = dwp[...].astype(bf16)
        rows = kept.shape[0]
        given[:rows] = last[pl.ds(pl.multiple_of((1 - place[3]) * rows, rows), rows), :]
        given[rows:] = small[...]
        kept[...] = last[pl.ds(pl.multiple_of(place[3] * rows, rows), rows), :]


def attention_backward(
    kind, place, p, grads, ot, linv, qc, qp, v, kt, tt, wp, st, ct, wq, wk, wv, normed,
    gain, shift, sums, block,
):
    length, width = normed.shape
    cols = qc.shape[1]
    count = length // block
    quarter = length // 4
    col = lambda n, w: pl.BlockSpec((n, w), lambda i: (0, count - 1 - i))
    row = lambda n, w: pl.BlockSpec((n, w), lambda i: (count - 1 - i, 0))
    smem = pl.BlockSpec(memory_space=pltpu.SMEM)
    rows = (cols + width) // 2
    return pl.pallas_call(
        functools.partial(backward_body, count, block, length // 2),
        grid=(count,),
        in_specs=[
            smem, smem, col(length, 2 * block),
            *[whole((quarter, cols))] * 4,
            col(cols, block), col(1, 2 * block), row(block, cols), row(block, cols),
            whole(v.shape), whole(kt.shape), whole(tt.shape), whole(wp.shape),
            col(width // 2, block), col(width // 2, block),
            *[whole((width, cols))] * 3, row(block, width),
            whole(gain.shape), whole(shift.shape), whole(sums.shape),
        ],
        out_specs=[
            whole((rows + 16, width)), whole((rows, width)), whole((16, width)), row(block // 2, width), row(block // 2, width)
        ],
        out_shape=[
            jax.ShapeDtypeStruct((rows + 16, width), bf16),
            jax.ShapeDtypeStruct((rows, width), bf16),
            jax.ShapeDtypeStruct((16, width), bf16),
            jax.ShapeDtypeStruct((length // 2, width), bf16),
            jax.ShapeDtypeStruct((length // 2, width), bf16),
        ],
        scratch_shapes=[
            pltpu.VMEM((2 * rows, width), bf16),
            pltpu.VMEM((cols + width, length), bf16),
            pltpu.VMEM((width, 3 * cols), bf16),
            pltpu.VMEM((2, DH + width, block), f32),
            pltpu.VMEM((length, cols), f32),
            pltpu.VMEM((length, cols), f32),
            pltpu.VMEM((block, 3 * cols), bf16),
            pltpu.VMEM((3 * cols, block), bf16),
            pltpu.VMEM((length, cols), bf16),
            pltpu.VMEM((cols, 2 * block), bf16),
            pltpu.VMEM((2 * block, cols), bf16),
            pltpu.VMEM((2 * block, cols), bf16),
            pltpu.VMEM((1, 2 * block), f32),
            pltpu.VMEM((3 * cols, width), f32),
            pltpu.VMEM((1, 3 * cols), f32),
            pltpu.VMEM((width, cols), f32),
            pltpu.VMEM((cols, block), f32),
            pltpu.VMEM((cols, block), f32),
        ],
        compiler_params=params(),
        cost_estimate=cost(8),
        name="attention_backward",
    )(
        kind, place, p, *grads, ot, linv, qc, qp, v, kt, tt, wp, st, ct, wq, wk, wv, normed,
        gain, shift, sums,
    )


def feed_body(
    place, tokens, cot, own_att, a1, a2, a3, w0, w1, w2, w3, i0, i1, u0, u1, b0, b1,
    bu, gain, shift,
    back_keep, back_send, out, res_own, bias, near, keep,
    hidden_t, act_t, pres, cots,
):
    step = pl.program_id(0)
    own, width = res_own.shape
    steps = cots.shape[0] // (2 * own)

    @pl.when(step < steps)
    def rows():
        c = cot[...].reshape(2 * own, width)
        residual = tokens[...].reshape(2 * own, width).astype(f32)
        residual = residual + dot(own_att[...].reshape(2 * own, own_att.shape[-1]), w0[...])
        for att, wo in ((a1, w1), (a2, w2), (a3, w3)):
            residual = residual + dot(att[...], wo[...])
        normed, _ = norm_parts(residual)
        hidden = (normed * gain[...] + shift[...]).astype(bf16)
        here = pl.ds(pl.multiple_of(step * 2 * own, 2 * own), 2 * own)
        cots[here, :] = c
        hidden_t[:, here] = hidden.T
        mixed = 0.5 * (residual + bu[...])
        back = None
        sums = []
        for n, wi, wu, bi in ((0, i0, u0, b0), (1, i1, u1, b1)):
            x = dot(hidden, wi[...]) + bi[...]
            square = x * x
            t = jnp.tanh(GELU_A * x * (1.0 + GELU_B * square))
            act = (0.5 * x * (1.0 + t)).astype(bf16)
            slope = 0.5 * (1.0 + t) + (0.5 * GELU_A) * x * (1.0 - t * t) * (
                1.0 + (3.0 * GELU_B) * square
            )
            act_t[n, :, here] = act.T
            mixed = mixed + dot(act, wu[...])
            pre = (dot_nt(c, wu[...]) * slope).astype(bf16)
            pres[n, here, :] = pre
            sums.append(jnp.sum(pre.astype(f32), axis=0, keepdims=True))
            back_n = dot_nt(pre, wi[...])
            back = back_n if back is None else back + back_n
        out[...] = mixed.astype(bf16)
        sums = jnp.concatenate(sums, axis=0)
        low = place[2] == 0
        res_own[...] = jnp.where(low, residual[:own], residual[own:])
        back_keep[...] = jnp.where(low, back[:own], back[own:]).astype(bf16)
        back_send[...] = jnp.where(low, back[own:], back[:own]).astype(bf16)

        @pl.when(step == 0)
        def first():
            bias[...] = sums

        @pl.when(step > 0)
        def later():
            bias[...] += sums

    @pl.when(step == steps)
    def grads():
        for n, ref in ((1, near), (0, keep)):
            parts, length, _ = ref.shape
            share = length // 2
            inner = dot(hidden_t[...], pres[n]).astype(bf16)
            outer = dot(act_t[n], cots[...]).astype(bf16)
            for r in range(parts):
                ref[r, :share] = inner[r * share : (r + 1) * share]
                ref[r, share:] = outer[r * share : (r + 1) * share]


def feed(place, tokens, cot, own_att, atts, wos, wis, wus, bis, bu, gain, shift):
    length, width = tokens.shape
    cols = own_att.shape[1]
    share = wis[0].shape[1]
    rows = length // 2
    own = rows // 4
    spec = lambda s: pl.BlockSpec(s, lambda i, place: (0,) * len(s))
    at = lambda i: jnp.minimum(i, 1)
    step = lambda w: pl.BlockSpec((2 * own, w), lambda i, place: (at(i), 0))
    half = pl.BlockSpec((own, width), lambda i, place: (at(i), 0))
    parts = first_parts()
    grad_shape = (parts, (width + share) // parts, width)
    mine = lambda w: pl.BlockSpec((2, 1, own, w), lambda i, place: (at(i), place[1], 0, 0))
    split = lambda x: x.reshape(4, 2, own, x.shape[1])
    others = (*wos, *wis, *wus, *bis, bu, gain, shift)
    shape = jax.ShapeDtypeStruct
    return pl.pallas_call(
        feed_body,
        grid_spec=pltpu.PrefetchScalarGridSpec(
            num_scalar_prefetch=1,
            grid=(3,),
            in_specs=[mine(width), mine(width), mine(cols)]
            + [step(cols)] * 3
            + [spec(o.shape) for o in others],
            out_specs=[
                half, half, step(width), half, spec((2, share)), spec(grad_shape),
                spec(grad_shape),
            ],
            scratch_shapes=[
                pltpu.VMEM((width, rows), bf16),
                pltpu.VMEM((2, share, rows), bf16),
                pltpu.VMEM((2, rows, share), bf16),
                pltpu.VMEM((rows, width), bf16),
            ],
        ),
        out_shape=[
            shape((2 * own, width), bf16), shape((2 * own, width), bf16),
            shape((rows, width), bf16), shape((2 * own, width), f32), shape((2, share), f32),
            shape(grad_shape, bf16), shape(grad_shape, bf16),
        ],
        compiler_params=params(),
        cost_estimate=cost(13),
        name="feed",
    )(place, split(tokens), split(cot), split(own_att), *atts, *others)


def turn_body(
    place, keep, got, residual, cot, a0, a1, a2, a3, w0, w1, w2, w3, gain,
    res_out, sums_out, g0, g1, g2, g3, o0, o1, o2, o3,
):
    rows, width = keep.shape
    back = keep[...].astype(f32) + got[...].astype(f32)
    c = cot[...].reshape(rows, width).astype(f32)
    normed, scale = norm_parts(residual[...])
    fold = lambda values: jnp.sum(values, axis=0, keepdims=True)
    sums_out[...] = jnp.concatenate([fold(back * normed), fold(back), fold(c)], axis=0)
    e = back * gain[...]
    inner = (
        e
        - jnp.mean(e, axis=-1, keepdims=True)
        - normed * jnp.mean(e * normed, axis=-1, keepdims=True)
    )
    branch = (c + scale * inner).astype(bf16)
    res_out[...] = branch
    for wo, out in ((w0, g0), (w1, g1), (w2, g2), (w3, g3)):
        out[...] = dot_nt(branch, wo[...]).astype(bf16)
    for att, out in ((a0, o0), (a1, o1), (a2, o2), (a3, o3)):
        out[...] = dot(att[...].reshape(rows, out.shape[0]).T, branch).astype(out.dtype)


def turn(place, keep, got, residual, cot, own_att, others, wos, gain):
    rows, width = keep.shape
    own = rows // 2
    cols = wos[0].shape[0]
    spec = lambda s: pl.BlockSpec(s, lambda i, place: (0,) * len(s))
    mine = lambda w: pl.BlockSpec((2, 1, own, w), lambda i, place: (0, place[0], 0, 0))
    half = lambda w: pl.BlockSpec((2, 1, own, w), lambda i, place: (0, place[2], 0, 0))
    split = lambda x: x.reshape(2, -1, own, x.shape[1])
    shapes = [((rows, width), bf16), ((3, width), f32)]
    shapes = shapes + [((rows, cols), bf16)] * 4
    shapes = shapes + [((cols, width), t) for t in (f32, bf16, bf16, bf16)]
    return pl.pallas_call(
        turn_body,
        grid_spec=pltpu.PrefetchScalarGridSpec(
            num_scalar_prefetch=1,
            grid=(1,),
            in_specs=[spec(keep.shape)] * 3
            + [mine(width), mine(cols)]
            + [half(cols)] * 3
            + [spec(w.shape) for w in wos]
            + [spec(gain.shape)],
            out_specs=[spec(s) for s, _ in shapes],
        ),
        out_shape=[jax.ShapeDtypeStruct(s, t) for s, t in shapes],
        compiler_params=params(),
        cost_estimate=cost(60),
        name="turn",
    )(
        place, keep, got, residual, split(cot), split(own_att), *[split(x) for x in others],
        *wos, gain,
    )


def close_body(place, keep0, keep1, near0, near1, got, t0, t1, res, gain, out):
    own = t0.shape[0]
    for part, keep, near, tokens in ((0, keep0, near0, t0), (1, keep1, near1, t1)):
        rows = slice(part * own, (part + 1) * own)
        total = keep[...].astype(f32) + near[...].astype(f32) + got[rows].astype(f32)
        normed, scale = norm_parts(tokens[...].astype(f32))
        e = total * gain[...]
        inner = (
            e
            - jnp.mean(e, axis=-1, keepdims=True)
            - normed * jnp.mean(e * normed, axis=-1, keepdims=True)
        )
        out[rows] = (res[rows].astype(f32) + scale * inner).astype(bf16)


def close(place, keep, near, got, tokens, res, gain):
    rows, width = got.shape
    own = rows // 2
    spec = pl.BlockSpec((rows, width), lambda i, place: (0, 0))
    mine = lambda part: pl.BlockSpec((own, width), lambda i, place: (4 * part + place[0], 0))
    at = lambda part: pl.BlockSpec((own, width), lambda i, place: (2 * part + place[2], 0))
    return pl.pallas_call(
        close_body,
        grid_spec=pltpu.PrefetchScalarGridSpec(
            num_scalar_prefetch=1,
            grid=(1,),
            in_specs=[
                at(0), at(1), at(0), at(1), spec, mine(0), mine(1), spec,
                pl.BlockSpec((1, width), lambda i, place: (0, 0)),
            ],
            out_specs=spec,
        ),
        out_shape=jax.ShapeDtypeStruct((rows, width), bf16),
        compiler_params=params(),
        cost_estimate=cost(2),
        name="close",
    )(place, keep, keep, near, near, got, tokens, tokens, res, gain)


def collect_body(place, m0, m1, g0, g1, g2, g3, mixed, grad, sems):
    own = g0.shape[0] // 2
    core = place[1]
    copies = []
    for part in range(2):
        for flip, ref in ((0, m0), (1, m1)):
            for at_high in range(2):
                put = pl.multiple_of((4 * part + 2 * at_high + (core ^ flip)) * own, own)
                copies.append((ref.at[pl.ds((2 * part + at_high) * own, own)], mixed, put))
        for n, ref in enumerate((g0, g1, g2, g3)):
            put = pl.multiple_of((4 * part + (place[0] ^ n)) * own, own)
            copies.append((ref.at[pl.ds(part * own, own)], grad, put))
    copies = [
        pltpu.make_async_copy(source, target.at[pl.ds(put, own)], sems.at[at])
        for at, (source, target, put) in enumerate(copies)
    ]
    for copy in copies:
        copy.start()
    for copy in copies:
        copy.wait()


def collect(place, mixed, grads):
    rows, width = grads[0].shape
    hbm = pl.BlockSpec(memory_space=pl.ANY)
    shape = jax.ShapeDtypeStruct((4 * rows, width), bf16)
    return pl.pallas_call(
        collect_body,
        in_specs=[pl.BlockSpec(memory_space=pltpu.SMEM)]
        + [pl.BlockSpec(memory_space=pltpu.VMEM)] * 6,
        out_specs=[hbm] * 2,
        out_shape=[shape] * 2,
        scratch_shapes=[pltpu.SemaphoreType.DMA((16,))],
        compiler_params=pltpu.CompilerParams(vmem_limit_bytes=16 * 2**20),
        cost_estimate=cost(3),
        name="collect",
    )(place, *mixed, *grads)


def swap(value, axis, mask):
    size = lax.axis_size(axis)
    return lax.ppermute(value, axis, [(i, i ^ mask) for i in range(size)])


def block_of(value, index, count):
    return lax.dynamic_slice_in_dim(value, index * count, count, 0)


def levels(size):
    bits = size.bit_length() - 1
    out = []
    shift = 0
    while shift < bits:
        wide = min(3, bits - shift)
        out.append((shift, wide))
        shift += wide
    return out


def groups_of(shift, wide):
    size = lax.axis_size("dp")
    count = 1 << wide
    return [
        [base + (n << shift) for n in range(count)]
        for base in range(size)
        if not (base >> shift) & (count - 1)
    ]


def exchange(value, shift, wide):
    return lax.all_to_all(
        value, "dp", split_axis=0, concat_axis=0, tiled=True,
        axis_index_groups=None if 1 << wide == lax.axis_size("dp") else groups_of(shift, wide),
    )


def gather_dp(value):
    sizes = [1 << wide for _, wide in levels(lax.axis_size("dp"))]
    whole_value = lax.all_gather(value, "dp", axis=0)
    if len(sizes) > 1:
        whole_value = whole_value.reshape(*sizes[::-1], *value.shape)
        whole_value = whole_value.transpose(
            *reversed(range(len(sizes))), len(sizes), len(sizes) + 1
        )
    return whole_value.reshape(sizes[0], -1, value.shape[1])


def first_parts():
    return 1 << levels(lax.axis_size("dp"))[0][1]


def start_dp(parts):
    return exchange(parts, *levels(lax.axis_size("dp"))[0])


def fold_dp(got):
    total = jnp.sum(got.astype(f32), axis=0)
    for shift, wide in levels(lax.axis_size("dp"))[1:]:
        parts = total.astype(bf16).reshape(1 << wide, -1, total.shape[1])
        total = jnp.sum(exchange(parts, shift, wide).astype(f32), axis=0)
    return total.astype(bf16)


def masks():
    return [1 << bit for bit in range(lax.axis_size("dp").bit_length() - 1)]


def halves(value, mask):
    bit = (lax.axis_index("dp") & mask) != 0
    rows = value.shape[0] // 2
    low, high = value[:rows], value[rows:]
    return jnp.where(bit, low, high), jnp.where(bit, high, low)


def give(value, small, mask):
    return jnp.concatenate([halves(value, mask)[0], small], axis=0)


def halve_dp(value, small, mask, other=None):
    return take(give(value, small, mask), halves(value, mask)[1], small, mask, other)


def take(given, kept, small, mask, other=None):
    got, other = lax.optimization_barrier((swap(given, "dp", mask), other))
    got = got.astype(f32)
    rows = kept.shape[0]
    value = (kept.astype(f32) + got[:rows]).astype(bf16)
    return value, (small.astype(f32) + got[rows:]).astype(bf16), other


def after(value, *others):
    return lax.optimization_barrier((value, others))[0]


def double_dp(value, mask, other=None):
    bit = (lax.axis_index("dp") & mask) != 0
    got, other = lax.optimization_barrier((swap(value, "dp", mask), other))
    value = jnp.concatenate([jnp.where(bit, got, value), jnp.where(bit, value, got)], axis=0)
    return value, other


def by_index(value):
    bits = len(masks())
    width = value.shape[-1]
    value = value.reshape((2,) * bits + (-1, width)).transpose(*reversed(range(bits)), bits, bits + 1)
    wides = [wide for _, wide in levels(lax.axis_size("dp"))]
    value = value.reshape(*[1 << wide for wide in reversed(wides)], -1, width)
    count = len(wides)
    value = value.transpose(*reversed(range(count)), count, count + 1)
    return value.reshape(1 << wides[0], -1, width)


def shards(
    tokens, item_kind, first_gain, first_shift, query_weight, key_weight, value_weight,
    position_weight, content_bias, position_bias, output_weight, second_gain, second_shift,
    inner_weight, inner_bias, outer_weight, outer_bias, cotangent,
):
    length, width = tokens.shape
    cols = query_weight.shape[1]
    share = inner_weight.shape[1]
    mp = lax.axis_index("mp").astype(jnp.int32)
    core, high = mp & 1, mp >> 1
    low = lax.axis_index("dp").astype(jnp.int32) & 1
    place = jnp.stack([mp, core, high, low])
    half = length // 2
    block = min(512, half)
    per_half = half // block
    own = half // 4
    sin_table, cos_table = sinusoid(length, width)
    table = jnp.asarray(np.concatenate([sin_table, cos_table], axis=1), bf16)
    table_t = jnp.asarray(np.concatenate([sin_table, cos_table], axis=1).T, bf16)
    st = jnp.asarray(sin_table.T, f32)
    ct = jnp.asarray(cos_table.T, f32)
    gain1, shift1, gain2, shift2, bu = (
        v[None] for v in (first_gain, first_shift, second_gain, second_shift, outer_bias)
    )

    tie = lax.optimization_barrier
    wos = [output_weight] + [swap(output_weight, "mp", n) for n in (1, 2, 3)]
    bis = [inner_bias[None], swap(inner_bias[None], "mp", 1)]
    projections = (query_weight, key_weight, value_weight)
    normed, qc, qp, v, kt, p, ot, attended, linv = attention_forward(
        item_kind, tokens, gain1, shift1, *projections, content_bias[None], position_bias[None],
        position_weight, st, ct, table, block,
    )
    blocks = attended.reshape(4, 2, own, cols)
    pick = lambda c: lax.dynamic_index_in_dim(blocks, c, 1, False).reshape(4 * own, cols)
    near, far = pick(1 - core), pick(core)
    near, far, wi, wu, wos, bis = tie((near, far, inner_weight, outer_weight, wos, bis))
    wis = [inner_weight, swap(wi, "mp", 1)]
    wus = [outer_weight, swap(wu, "mp", 1)]
    atts = [swap(near, "mp", 1), swap(far, "mp", 2), swap(near, "mp", 3)]
    back_keep, back_send, out, residual, bias, near, keep = feed(
        place, tokens, cotangent, attended, atts, wos, wis, wus, bis, bu, gain2, shift2
    )
    back_got = swap(back_send, "mp", 2)
    near_got = swap(near, "mp", 1)
    feed_sum = (keep.astype(f32) + near_got.astype(f32)).astype(bf16)
    feed_got = start_dp(feed_sum)

    res, sums, *turned = turn(
        place, back_keep, back_got, residual, cotangent, attended, atts, wos, gain2
    )
    grads, weight_parts = turned[:4], turned[4:]
    grads = [grads[0]] + [swap(grads[n], "mp", n) for n in (1, 2, 3)]
    sums = jnp.concatenate([sums, bias[:1] + swap(bias[1:], "mp", 1)], axis=0)
    out_send = after(out, grads[1])
    weight_parts = after(weight_parts, grads[1])
    weight_parts = [weight_parts[0]] + [swap(weight_parts[n], "mp", n) for n in (1, 2, 3)]
    out_got = swap(out_send, "mp", 2)

    given, kept, small, near, keep = attention_backward(
        item_kind, place, p, grads, ot, linv, qc, qp, v, kt, table_t, position_weight,
        st, ct, *projections, normed, gain1, shift1, sums, block,
    )
    given, kept, small, near, keep, weight_parts, out_got, feed_got = tie(
        (given, kept, small, near, keep, weight_parts, out_got, feed_got)
    )
    near = swap(near, "mp", 1)
    out_sum = sum(x.astype(f32) for x in weight_parts)
    fill = lambda value, there: (
        value.astype(f32)
        + jnp.pad(out_sum * there.astype(f32), ((0, value.shape[0] - cols), (0, 0)))
    ).astype(bf16)
    given = fill(given, low)
    kept = fill(kept, 1 - low)
    pick = lambda x: lax.dynamic_index_in_dim(x.reshape(2, 2, own, width), 1 - high, 1, False)
    far = (pick(keep).astype(f32) + pick(near).astype(f32)).astype(bf16).reshape(2 * own, width)
    first, *middle = masks()
    feed_total = fold_dp(after(feed_got, given, far))
    far = swap(far, "mp", 2)

    last, small, far = take(given, kept, small, first, far)
    mixed = (out.astype(f32) + out_got.astype(f32)).astype(bf16)
    mixed = [mixed, swap(mixed, "mp", 1)]
    grad = close(place, keep, near, far, tokens, res, gain1)
    beyond = swap(grad, "mp", 2)
    for mask in reversed(masks()):
        feed_total, _ = double_dp(feed_total, mask)
    for mask in middle:
        last, small, _ = halve_dp(last, small, mask)
    for mask in reversed(middle):
        last, _ = double_dp(last, mask)
    tokens_grad = [grad, swap(grad, "mp", 1), beyond, swap(beyond, "mp", 1)]
    small = after(small, last)
    mixed, tokens_grad = collect(place, mixed, tokens_grad)
    last_total, (mixed, tokens_grad) = double_dp(last, first, (mixed, tokens_grad))
    last_total = last_total.astype(f32)
    last_small = small.astype(f32)
    feed_total = by_index(feed_total)

    summed = last_small[:5]
    summed = summed + swap(summed, "mp", 1)
    summed = summed + swap(summed, "mp", 2)
    feed_total = feed_total.astype(f32)
    split = width // first_parts()
    inner_grad = feed_total[:, :split].reshape(width, share)
    outer_grad = feed_total[:, split:].reshape(share, width)
    whole_grad = last_total[cols:]

    return (
        mixed,
        tokens_grad,
        summed[0],
        summed[1],
        whole_grad[:, :cols],
        whole_grad[:, cols : 2 * cols],
        whole_grad[:, 2 * cols : 3 * cols],
        whole_grad[:, 3 * cols :],
        last_small[6, :cols],
        last_small[6, cols : 2 * cols],
        last_total[:cols],
        summed[2],
        summed[3],
        inner_grad,
        last_small[5],
        outer_grad,
        summed[4],
    )


def solution(mesh):
    return jax.shard_map(
        shards,
        mesh=mesh,
        in_specs=(
            P("dp", None), P("dp"), P(), P(), P(None, "mp"), P(None, "mp"), P(None, "mp"),
            P(None, "mp"), P("mp"), P("mp"), P("mp", None), P(), P(), P(None, "mp"), P("mp"),
            P("mp", None), P(), P("dp", None),
        ),
        out_specs=(
            P("dp", None), P("dp", None), P(), P(), P(None, "mp"), P(None, "mp"), P(None, "mp"),
            P(None, "mp"), P("mp"), P("mp"), P("mp", None), P(), P(), P(None, "mp"), P("mp"),
            P("mp", None), P(),
        ),
        check_vma=False,
    )
```

```python
import functools
import math

import jax
import jax.numpy as jnp
import numpy as np
from jax import lax
from jax.experimental import pallas as pl
from jax.experimental.pallas import tpu as pltpu
from jax.sharding import PartitionSpec as P

DH = 64
EPS = 1e-05
NEG = -1e30
LOG2E = 1.4426950408889634
GELU_A = 0.7978845608028654
GELU_B = 0.044715

f32 = jnp.float32
bf16 = jnp.bfloat16


def sinusoid(count, model_width):
    freqs = np.exp(np.arange(model_width // 2) * (-2.0 * math.log(10000.0) / model_width))
    angles = np.arange(count)[:, None] * freqs[None, :]
    return np.sin(angles), np.cos(angles)


def dot(left, right):
    return jnp.dot(left, right, preferred_element_type=f32)


def dot_nt(left, right):
    return lax.dot_general(left, right, (((1,), (1,)), ((), ())), preferred_element_type=f32)


def whole(shape):
    return pl.BlockSpec(shape, lambda *ids: (0,) * len(shape))


def params(mib=57):
    return pltpu.CompilerParams(
        vmem_limit_bytes=mib * 2**20, dimension_semantics=("arbitrary",)
    )


def cost(microseconds):
    return pl.CostEstimate(
        flops=int(microseconds * 1.1e9), bytes_accessed=1 << 10, transcendentals=0
    )


def keep_rows(values, head):
    ids = lax.broadcasted_iota(jnp.int32, values.shape, 0)
    return jnp.where(ids // DH == head, values, jnp.zeros_like(values))


def keep_cols(values, head):
    ids = lax.broadcasted_iota(jnp.int32, values.shape, 1)
    return jnp.where(ids // DH == head, values, jnp.zeros_like(values))


def norm_parts(values):
    center = values - jnp.mean(values, axis=-1, keepdims=True)
    spread = jnp.mean(center * center, axis=-1, keepdims=True)
    scale = lax.rsqrt(spread + EPS)
    return center * scale, scale


def forward_body(
    block, half_rows,
    kind, tokens, gain, shift, wq, wk, wv, cbias, pbias, wp, st, ct, table,
    normed_out, qc_out, qp_out, v_out, kt_out, p_out, ot_out, near_out, far_out, linv_out,
    pbuf, puts, sems, wcat, kcat, vt, qa, s_scr, m_scr, l_scr, acc,
):
    ib = pl.program_id(0)
    here = pl.multiple_of(ib * block, block)
    width, cols = wp.shape
    half = width // 2
    mid = block // 2

    def put(of, c, slot):
        at = pl.multiple_of(c * block, block), pl.multiple_of(of * 2 * block, 2 * block)
        target = p_out.at[pl.ds(at[0], block), pl.ds(at[1], 2 * block)]
        return pltpu.make_async_copy(pbuf.at[slot], target, sems.at[slot])

    @pl.when(ib == 0)
    def start():
        puts[0] = 0
        for n, ref in enumerate((wq, wk, wv)):
            wcat[:, n * cols : (n + 1) * cols] = ref[...]

    normed, _ = norm_parts(tokens[...].astype(f32))
    normed_out[...] = normed.astype(bf16)
    hidden = (normed * gain[...] + shift[...]).astype(bf16)
    qkv = dot(hidden, wcat[...])
    queries, keys, values = (qkv[:, n * cols : (n + 1) * cols] for n in range(3))
    qc_out[...] = ((queries + cbias[...]) * 0.125).astype(bf16)
    qp_out[...] = ((queries + pbias[...]) * 0.125).astype(bf16)
    v_out[...] = values.astype(bf16)
    kcat[pl.ds(here, block), :width] = table[...]
    kcat[pl.ds(here, block), width:] = keys.astype(bf16)
    vt[:, pl.ds(here, block)] = values.T.astype(bf16)
    kt_out[...] = keys.T.astype(bf16)
    queries_t = queries.T
    column = lambda row: jnp.broadcast_to(row, (8, row.shape[1])).T[:, :1]
    content = ((queries_t + column(cbias[...])) * (0.125 * LOG2E)).astype(bf16)
    position = ((queries_t + column(pbias[...])) * (0.125 * LOG2E)).astype(bf16)
    for h in range(2):
        u = dot(wp[...], keep_rows(position, h))
        us, uc = u[:half], u[half:]
        to = slice(h * block, (h + 1) * block)
        qa[:half, to] = (uc * st[...] - us * ct[...]).astype(bf16)
        qa[half:width, to] = (us * st[...] + uc * ct[...]).astype(bf16)
        qa[width:, to] = keep_rows(content, h)
    lo = jnp.where((kind[0] == 1) & (ib * block >= half_rows), half_rows // block, 0)
    fold = lambda x, op: op(x.reshape(x.shape[0] // 8, 8, x.shape[1]), axis=0)
    rj = lax.broadcasted_iota(jnp.int32, (mid, block), 0)
    ri = lax.broadcasted_iota(jnp.int32, (mid, block), 1)
    first = pl.ds(here, mid)
    second = pl.ds(pl.multiple_of(here + mid, mid), mid)

    s = dot(kcat[first, :], qa[...])
    s = jnp.where(jnp.concatenate([rj <= ri] * 2, axis=1), s, NEG)
    s_scr[first, :] = s
    m_scr[...] = fold(s, jnp.max)
    for h in range(2):
        to = slice(h * block + mid, (h + 1) * block)
        s = dot(kcat[second, :], qa[:, to])
        s = jnp.where(rj[:, :mid] <= ri[:, :mid], s, NEG)
        s_scr[second, to] = s
        m_scr[:, to] = jnp.maximum(m_scr[:, to], fold(s, jnp.max))

    def score_loop(c, carry):
        rows = pl.ds(pl.multiple_of(c * block, block), block)
        s = dot(kcat[rows, :], qa[...])
        s_scr[rows, :] = s
        m_scr[...] = jnp.maximum(m_scr[...], fold(s, jnp.max))
        return carry

    lax.fori_loop(lo, ib, score_loop, 0)
    m_scr[...] = jnp.broadcast_to(jnp.max(m_scr[...], axis=0, keepdims=True), m_scr.shape)

    done = puts[0]
    slot = done & 3

    @pl.when(done >= 4)
    def free():
        put(ib, ib, slot).wait()

    p = jnp.exp2(s_scr[first, :] - m_scr[0:1])
    l_scr[...] = fold(p, jnp.sum)
    low = p.astype(bf16)
    pbuf[slot, :mid] = low
    for h in range(2):
        rows = slice(DH * h, DH * h + DH)
        to = slice(h * block + mid, (h + 1) * block)
        acc[rows] = dot(vt[rows, first], low[:, h * block : (h + 1) * block])
        p = jnp.exp2(s_scr[second, to] - m_scr[0:1, to])
        l_scr[:, to] += fold(p, jnp.sum)
        part = p.astype(bf16)
        pbuf[slot, mid:, to] = part
        acc[rows, mid:] += dot(vt[rows, second], part)

    put(ib, ib, slot).start()

    def prob_loop(c, done):
        slot = done & 3

        @pl.when(done >= 4)
        def free():
            put(ib, c, slot).wait()

        rows = pl.ds(pl.multiple_of(c * block, block), block)
        p = jnp.exp2(s_scr[rows, :] - m_scr[0:1])
        l_scr[...] += fold(p, jnp.sum)
        low = p.astype(bf16)
        pbuf[slot] = low
        put(ib, c, slot).start()
        for h in range(2):
            heads = slice(DH * h, DH * h + DH)
            acc[heads] += dot(vt[heads, rows], low[:, h * block : (h + 1) * block])
        return done + 1

    puts[0] = lax.fori_loop(lo, ib, prob_loop, done + 1)
    inverse = 1.0 / jnp.sum(l_scr[...], axis=0, keepdims=True)
    linv_out[...] = inverse
    attended = jnp.concatenate(
        [acc[DH * h : DH * h + DH] * inverse[:, h * block : (h + 1) * block] for h in range(2)],
        axis=0,
    )
    ot_out[...] = attended
    rows = attended.T.astype(bf16)
    even = (lax.axis_index("mp") & 1) == 0
    near_out[...] = jnp.where(even, rows[mid:], rows[:mid])
    far_out[...] = jnp.where(even, rows[:mid], rows[mid:])

    @pl.when(ib == pl.num_programs(0) - 1)
    def finish():
        for slot in range(4):
            put(ib, ib, slot).wait()


def attention_forward(
    kind, tokens, gain, shift, wq, wk, wv, cbias, pbias, wp, st, ct, table, block
):
    length, width = table.shape
    cols = wp.shape[1]
    count = length // block
    row = lambda n, w: pl.BlockSpec((n, w), lambda i: (i, 0))
    col = lambda n, w: pl.BlockSpec((n, w), lambda i: (0, i))
    shape = jax.ShapeDtypeStruct
    return pl.pallas_call(
        functools.partial(forward_body, block, length // 2),
        grid=(count,),
        in_specs=[
            pl.BlockSpec(memory_space=pltpu.SMEM), row(block, width),
            whole((1, width)), whole((1, width)), *[whole((width, cols))] * 3,
            whole((1, cols)), whole((1, cols)), whole((width, cols)),
            col(width // 2, block), col(width // 2, block), row(block, width),
        ],
        out_specs=[
            row(block, width), row(block, cols), row(block, cols), row(block, cols),
            col(cols, block), pl.BlockSpec(memory_space=pl.ANY), col(cols, block),
            row(block // 2, cols), row(block // 2, cols), col(1, 2 * block),
        ],
        out_shape=[
            shape((length, width), bf16),
            shape((length, cols), bf16), shape((length, cols), bf16), shape((length, cols), bf16),
            shape((cols, length), bf16),
            shape((length, 2 * length), bf16), shape((cols, length), f32),
            shape((length // 2, cols), bf16), shape((length // 2, cols), bf16),
            shape((1, 2 * length), f32),
        ],
        scratch_shapes=[
            pltpu.VMEM((4, block, 2 * block), bf16),
            pltpu.SMEM((1,), jnp.int32),
            pltpu.SemaphoreType.DMA((4,)),
            pltpu.VMEM((width, 3 * cols), bf16),
            pltpu.VMEM((length, width + cols), bf16),
            pltpu.VMEM((cols, length), bf16),
            pltpu.VMEM((width + cols, 2 * block), bf16),
            pltpu.VMEM((length, 2 * block), f32),
            pltpu.VMEM((8, 2 * block), f32),
            pltpu.VMEM((8, 2 * block), f32),
            pltpu.VMEM((cols, block), f32),
        ],
        compiler_params=params(),
        cost_estimate=cost(25),
        name="attention_forward",
    )(kind, tokens, gain, shift, wq, wk, wv, cbias, pbias, wp, st, ct, table)


def backward_body(
    count, block, half_rows,
    kind, place, p, d0, d1, d2, d3, ot, linv, qc, qp, v, kt, tt, wp, st, ct,
    wq, wk, wv, normed, gain, shift, sums,
    given, kept, small, near, mine,
    last, ktt, wcat, acc, dk, dv, low, low_t, d_scr, dcat, dstack, qstack, delta, mom, colsum, dwp, cb, pb,
):
    step = pl.program_id(0)
    ib = count - 1 - step
    width, cols = wp.shape
    half = width // 2
    mid = block // 2
    own = d0.shape[0] // 2

    @pl.when(step == 0)
    def start():
        for ref in (dk, dv, dwp, cb, pb, mom, colsum):
            ref[...] = jnp.zeros(ref.shape, f32)
        for n, ref in enumerate((wq, wk, wv)):
            wcat[:, n * cols : (n + 1) * cols] = ref[...]
        ktt[:DH] = kt[:DH]
        ktt[DH : DH + width] = tt[...]
        ktt[DH + width :] = kt[DH:]
        for n, ref in enumerate((d0, d1, d2, d3)):
            for part in range(2):
                at = pl.multiple_of((4 * part + (place[0] ^ n)) * own, own)
                d_scr[pl.ds(at, own), :] = ref[part * own : (part + 1) * own]

    lo = jnp.where((kind[0] == 1) & (ib * block >= half_rows), half_rows // block, 0)
    here = pl.multiple_of(ib * block, block)
    dt = d_scr[pl.ds(here, block), :].astype(f32).T
    scaled = jnp.concatenate(
        [
            dt[DH * h : DH * h + DH] * linv[:, h * block : (h + 1) * block]
            for h in range(2)
        ],
        axis=0,
    )
    scaled_rows = scaled.T.astype(bf16)
    scaled = scaled.astype(bf16)
    product = scaled.astype(f32) * ot[...]
    for h in range(2):
        to = slice(h * block, (h + 1) * block)
        dcat[:, to] = keep_rows(scaled, h)
        dstack[to] = keep_cols(scaled_rows, h)
        qstack[to] = keep_cols(qc[...], h)
        delta[:, to] = jnp.sum(product[DH * h : DH * h + DH], axis=0, keepdims=True)

    first = pl.ds(here, mid)
    second = pl.ds(pl.multiple_of(here + mid, mid), mid)
    pt = p[first, :]
    dp = dot(v[first, :], dcat[...])
    ds = (pt.astype(f32) * (dp - delta[...])).astype(bf16)
    dv[first, :] += dot(pt, dstack[...])
    dk[first, :] += dot(ds, qstack[...])
    for h in range(2):
        to = slice(h * block + mid, (h + 1) * block)
        rows = slice(DH * h, DH * h + DH + width)
        acc[h] = dot(ktt[rows, first], ds[:, h * block : (h + 1) * block])
        pt2 = p[second, to]
        dp2 = dot(v[second, :], dcat[:, to])
        ds2 = (pt2.astype(f32) * (dp2 - delta[:, to])).astype(bf16)
        dv[second, :] += dot(pt2, dstack[to])
        dk[second, :] += dot(ds2, qstack[to])
        acc[h, :, mid:] += dot(ktt[rows, second], ds2)

    def loop(c, carry):
        rows = pl.ds(pl.multiple_of(c * block, block), block)
        pt = p[rows, :]
        dp = dot(v[rows, :], dcat[...])
        ds = (pt.astype(f32) * (dp - delta[...])).astype(bf16)
        dv[rows, :] += dot(pt, dstack[...])
        dk[rows, :] += dot(ds, qstack[...])
        for h in range(2):
            acc[h] += dot(
                ktt[DH * h : DH * h + DH + width, rows], ds[:, h * block : (h + 1) * block]
            )
        return carry

    lax.fori_loop(lo, ib, loop, 0)
    wpt = wp[...].astype(f32).T.astype(bf16)
    dqs = []
    for h in range(2):
        base = DH * (1 - h)
        gs = acc[h, base : base + half]
        gc = acc[h, base + half : base + width]
        rs = (st[...] * gc - ct[...] * gs).astype(bf16)
        rc = (ct[...] * gc + st[...] * gs).astype(bf16)
        wh = wpt[DH * h : DH * h + DH]
        by_position = (dot(wh[:, :half], rs) + dot(wh[:, half:], rc)) * 0.125
        by_content = acc[h, width * h : width * h + DH] * 0.125
        qph = keep_cols(qp[...], h)
        dwp[:half] += dot(rs, qph)
        dwp[half:] += dot(rc, qph)
        cb[DH * h : DH * h + DH] += by_content
        pb[DH * h : DH * h + DH] += by_position
        dqs.append(by_content + by_position)
    dqt = jnp.concatenate(dqs, axis=0)
    rows = pl.ds(here, block)
    for n, (value, value_t) in enumerate(
        ((dqt.T, dqt), (dk[rows, :], dk[rows, :].T), (dv[rows, :], dv[rows, :].T))
    ):
        to = slice(n * cols, (n + 1) * cols)
        low[:, to] = value.astype(bf16)
        low_t[to] = value_t.astype(bf16)
    mom[...] += dot(low_t[...], normed[...])
    colsum[...] += jnp.sum(low[...].astype(f32), axis=0, keepdims=True)
    for ref, core in ((near, 1 - place[1]), (mine, place[1])):
        at = pl.multiple_of(core * own, own)
        ref[...] = dot_nt(low[pl.ds(at, own), :], wcat[...]).astype(ref.dtype)

    @pl.when(step == count - 1)
    def finish():
        as_row = lambda values: jnp.broadcast_to(
            jnp.sum(values, axis=1, keepdims=True), (values.shape[0], 128)
        ).T[:1]
        column = jnp.broadcast_to(colsum[...], (8, 3 * cols)).T[:, :1]
        weights = wcat[...].astype(f32).T
        by_gain = jnp.sum(mom[...] * weights, axis=0, keepdims=True)
        by_shift = jnp.sum(column * weights, axis=0, keepdims=True)
        full = (gain[...] * mom[...] + shift[...] * column).T.astype(bf16)
        biases = jnp.concatenate(
            [as_row(cb[...]), as_row(pb[...]), jnp.zeros((1, width - 2 * cols), f32)], axis=1
        )
        small[...] = jnp.concatenate(
            [by_gain, by_shift, sums[...], biases, jnp.zeros((9, width), f32)], axis=0
        ).astype(bf16)
        last[:cols] = jnp.zeros((cols, width), bf16)
        last[cols:, : 3 * cols] = full
        last[cols:, 3 * cols :] = dwp[...].astype(bf16)
        rows = kept.shape[0]
        given[:rows] = last[pl.ds(pl.multiple_of((1 - place[3]) * rows, rows), rows), :]
        given[rows:] = small[...]
        kept[...] = last[pl.ds(pl.multiple_of(place[3] * rows, rows), rows), :]


def attention_backward(
    kind, place, p, grads, ot, linv, qc, qp, v, kt, tt, wp, st, ct, wq, wk, wv, normed,
    gain, shift, sums, block,
):
    length, width = normed.shape
    cols = qc.shape[1]
    count = length // block
    quarter = length // 4
    col = lambda n, w: pl.BlockSpec((n, w), lambda i: (0, count - 1 - i))
    row = lambda n, w: pl.BlockSpec((n, w), lambda i: (count - 1 - i, 0))
    smem = pl.BlockSpec(memory_space=pltpu.SMEM)
    rows = (cols + width) // 2
    return pl.pallas_call(
        functools.partial(backward_body, count, block, length // 2),
        grid=(count,),
        in_specs=[
            smem, smem, col(length, 2 * block),
            *[whole((quarter, cols))] * 4,
            col(cols, block), col(1, 2 * block), row(block, cols), row(block, cols),
            whole(v.shape), whole(kt.shape), whole(tt.shape), whole(wp.shape),
            col(width // 2, block), col(width // 2, block),
            *[whole((width, cols))] * 3, row(block, width),
            whole(gain.shape), whole(shift.shape), whole(sums.shape),
        ],
        out_specs=[
            whole((rows + 16, width)), whole((rows, width)), whole((16, width)), row(block // 2, width), row(block // 2, width)
        ],
        out_shape=[
            jax.ShapeDtypeStruct((rows + 16, width), bf16),
            jax.ShapeDtypeStruct((rows, width), bf16),
            jax.ShapeDtypeStruct((16, width), bf16),
            jax.ShapeDtypeStruct((length // 2, width), bf16),
            jax.ShapeDtypeStruct((length // 2, width), bf16),
        ],
        scratch_shapes=[
            pltpu.VMEM((2 * rows, width), bf16),
            pltpu.VMEM((cols + width, length), bf16),
            pltpu.VMEM((width, 3 * cols), bf16),
            pltpu.VMEM((2, DH + width, block), f32),
            pltpu.VMEM((length, cols), f32),
            pltpu.VMEM((length, cols), f32),
            pltpu.VMEM((block, 3 * cols), bf16),
            pltpu.VMEM((3 * cols, block), bf16),
            pltpu.VMEM((length, cols), bf16),
            pltpu.VMEM((cols, 2 * block), bf16),
            pltpu.VMEM((2 * block, cols), bf16),
            pltpu.VMEM((2 * block, cols), bf16),
            pltpu.VMEM((1, 2 * block), f32),
            pltpu.VMEM((3 * cols, width), f32),
            pltpu.VMEM((1, 3 * cols), f32),
            pltpu.VMEM((width, cols), f32),
            pltpu.VMEM((cols, block), f32),
            pltpu.VMEM((cols, block), f32),
        ],
        compiler_params=params(),
        cost_estimate=cost(8),
        name="attention_backward",
    )(
        kind, place, p, *grads, ot, linv, qc, qp, v, kt, tt, wp, st, ct, wq, wk, wv, normed,
        gain, shift, sums,
    )


def feed_body(
    place, tokens, cot, own_att, a1, a2, a3, w0, w1, w2, w3, i0, i1, u0, u1, b0, b1,
    bu, gain, shift,
    back_keep, back_send, out, res_own, bias, near, keep,
    hidden_t, act_t, pres, cots,
):
    step = pl.program_id(0)
    own, width = res_own.shape
    steps = cots.shape[0] // (2 * own)

    @pl.when(step < steps)
    def rows():
        c = cot[...].reshape(2 * own, width)
        residual = tokens[...].reshape(2 * own, width).astype(f32)
        for att, wo in ((own_att, w0), (a1, w1), (a2, w2), (a3, w3)):
            residual = residual + dot(att[...], wo[...])
        normed, _ = norm_parts(residual)
        hidden = (normed * gain[...] + shift[...]).astype(bf16)
        here = pl.ds(pl.multiple_of(step * 2 * own, 2 * own), 2 * own)
        cots[here, :] = c
        hidden_t[:, here] = hidden.T
        mixed = 0.5 * (residual + bu[...])
        back = None
        sums = []
        for n, wi, wu, bi in ((0, i0, u0, b0), (1, i1, u1, b1)):
            x = dot(hidden, wi[...]) + bi[...]
            square = x * x
            t = jnp.tanh(GELU_A * x * (1.0 + GELU_B * square))
            act = (0.5 * x * (1.0 + t)).astype(bf16)
            slope = 0.5 * (1.0 + t) + (0.5 * GELU_A) * x * (1.0 - t * t) * (
                1.0 + (3.0 * GELU_B) * square
            )
            act_t[n, :, here] = act.T
            mixed = mixed + dot(act, wu[...])
            pre = (dot_nt(c, wu[...]) * slope).astype(bf16)
            pres[n, here, :] = pre
            sums.append(jnp.sum(pre.astype(f32), axis=0, keepdims=True))
            back_n = dot_nt(pre, wi[...])
            back = back_n if back is None else back + back_n
        out[...] = mixed.astype(bf16)
        sums = jnp.concatenate(sums, axis=0)
        low = place[2] == 0
        res_own[...] = jnp.where(low, residual[:own], residual[own:])
        back_keep[...] = jnp.where(low, back[:own], back[own:]).astype(bf16)
        back_send[...] = jnp.where(low, back[own:], back[:own]).astype(bf16)

        @pl.when(step == 0)
        def first():
            bias[...] = sums

        @pl.when(step > 0)
        def later():
            bias[...] += sums

    @pl.when(step == steps)
    def grads():
        for n, ref in ((1, near), (0, keep)):
            parts, length, _ = ref.shape
            share = length // 2
            inner = dot(hidden_t[...], pres[n]).astype(bf16)
            outer = dot(act_t[n], cots[...]).astype(bf16)
            for r in range(parts):
                ref[r, :share] = inner[r * share : (r + 1) * share]
                ref[r, share:] = outer[r * share : (r + 1) * share]


def feed(place, tokens, cot, own_att, atts, wos, wis, wus, bis, bu, gain, shift):
    length, width = tokens.shape
    cols = own_att.shape[1]
    share = wis[0].shape[1]
    rows = length // 2
    own = rows // 4
    spec = lambda s: pl.BlockSpec(s, lambda i, place: (0,) * len(s))
    at = lambda i: jnp.minimum(i, 1)
    step = lambda w: pl.BlockSpec((2 * own, w), lambda i, place: (at(i), 0))
    half = pl.BlockSpec((own, width), lambda i, place: (at(i), 0))
    parts = first_parts()
    grad_shape = (parts, (width + share) // parts, width)
    mine = lambda w: pl.BlockSpec((2, 1, own, w), lambda i, place: (at(i), place[1], 0, 0))
    split = lambda x: x.reshape(4, 2, own, x.shape[1])
    others = (*wos, *wis, *wus, *bis, bu, gain, shift)
    shape = jax.ShapeDtypeStruct
    return pl.pallas_call(
        feed_body,
        grid_spec=pltpu.PrefetchScalarGridSpec(
            num_scalar_prefetch=1,
            grid=(3,),
            in_specs=[mine(width), mine(width)]
            + [step(cols)] * 4
            + [spec(o.shape) for o in others],
            out_specs=[
                half, half, step(width), half, spec((2, share)), spec(grad_shape),
                spec(grad_shape),
            ],
            scratch_shapes=[
                pltpu.VMEM((width, rows), bf16),
                pltpu.VMEM((2, share, rows), bf16),
                pltpu.VMEM((2, rows, share), bf16),
                pltpu.VMEM((rows, width), bf16),
            ],
        ),
        out_shape=[
            shape((2 * own, width), bf16), shape((2 * own, width), bf16),
            shape((rows, width), bf16), shape((2 * own, width), f32), shape((2, share), f32),
            shape(grad_shape, bf16), shape(grad_shape, bf16),
        ],
        compiler_params=params(),
        cost_estimate=cost(13),
        name="feed",
    )(place, split(tokens), split(cot), own_att, *atts, *others)


def turn_body(
    place, keep, got, residual, cot, a0, a1, a2, a3, w0, w1, w2, w3, gain,
    res_out, sums_out, g0, g1, g2, g3, o0, o1, o2, o3,
):
    rows, width = keep.shape
    back = keep[...].astype(f32) + got[...].astype(f32)
    c = cot[...].reshape(rows, width).astype(f32)
    normed, scale = norm_parts(residual[...])
    fold = lambda values: jnp.sum(values, axis=0, keepdims=True)
    sums_out[...] = jnp.concatenate([fold(back * normed), fold(back), fold(c)], axis=0)
    e = back * gain[...]
    inner = (
        e
        - jnp.mean(e, axis=-1, keepdims=True)
        - normed * jnp.mean(e * normed, axis=-1, keepdims=True)
    )
    branch = (c + scale * inner).astype(bf16)
    res_out[...] = branch
    for wo, out in ((w0, g0), (w1, g1), (w2, g2), (w3, g3)):
        out[...] = dot_nt(branch, wo[...]).astype(bf16)
    for att, out in ((a0, o0), (a1, o1), (a2, o2), (a3, o3)):
        out[...] = dot(att[...].reshape(rows, out.shape[0]).T, branch).astype(out.dtype)


def turn(place, keep, got, residual, cot, own_att, others, wos, gain):
    rows, width = keep.shape
    own = rows // 2
    cols = wos[0].shape[0]
    spec = lambda s: pl.BlockSpec(s, lambda i, place: (0,) * len(s))
    mine = lambda w: pl.BlockSpec((2, 1, own, w), lambda i, place: (0, place[0], 0, 0))
    half = lambda w: pl.BlockSpec((2, 1, own, w), lambda i, place: (0, place[2], 0, 0))
    split = lambda x: x.reshape(2, -1, own, x.shape[1])
    shapes = [((rows, width), bf16), ((3, width), f32)]
    shapes = shapes + [((rows, cols), bf16)] * 4
    shapes = shapes + [((cols, width), t) for t in (f32, bf16, bf16, bf16)]
    return pl.pallas_call(
        turn_body,
        grid_spec=pltpu.PrefetchScalarGridSpec(
            num_scalar_prefetch=1,
            grid=(1,),
            in_specs=[spec(keep.shape)] * 3
            + [mine(width)]
            + [half(cols)] * 4
            + [spec(w.shape) for w in wos]
            + [spec(gain.shape)],
            out_specs=[spec(s) for s, _ in shapes],
        ),
        out_shape=[jax.ShapeDtypeStruct(s, t) for s, t in shapes],
        compiler_params=params(),
        cost_estimate=cost(60),
        name="turn",
    )(
        place, keep, got, residual, split(cot), split(own_att), *[split(x) for x in others],
        *wos, gain,
    )


def close_body(place, keep0, keep1, near0, near1, got, t0, t1, res, gain, out):
    own = t0.shape[0]
    for part, keep, near, tokens in ((0, keep0, near0, t0), (1, keep1, near1, t1)):
        rows = slice(part * own, (part + 1) * own)
        total = keep[...].astype(f32) + near[...].astype(f32) + got[rows].astype(f32)
        normed, scale = norm_parts(tokens[...].astype(f32))
        e = total * gain[...]
        inner = (
            e
            - jnp.mean(e, axis=-1, keepdims=True)
            - normed * jnp.mean(e * normed, axis=-1, keepdims=True)
        )
        out[rows] = (res[rows].astype(f32) + scale * inner).astype(bf16)


def close(place, keep, near, got, tokens, res, gain):
    rows, width = got.shape
    own = rows // 2
    spec = pl.BlockSpec((rows, width), lambda i, place: (0, 0))
    mine = lambda part: pl.BlockSpec((own, width), lambda i, place: (4 * part + place[0], 0))
    at = lambda part: pl.BlockSpec((own, width), lambda i, place: (2 * part + place[2], 0))
    return pl.pallas_call(
        close_body,
        grid_spec=pltpu.PrefetchScalarGridSpec(
            num_scalar_prefetch=1,
            grid=(1,),
            in_specs=[
                at(0), at(1), at(0), at(1), spec, mine(0), mine(1), spec,
                pl.BlockSpec((1, width), lambda i, place: (0, 0)),
            ],
            out_specs=spec,
        ),
        out_shape=jax.ShapeDtypeStruct((rows, width), bf16),
        compiler_params=params(),
        cost_estimate=cost(2),
        name="close",
    )(place, keep, keep, near, near, got, tokens, tokens, res, gain)


def collect_body(place, m0, m1, g0, g1, g2, g3, mixed, grad, sems):
    own = g0.shape[0] // 2
    core = place[1]
    copies = []
    for part in range(2):
        for flip, ref in ((0, m0), (1, m1)):
            for at_high in range(2):
                put = pl.multiple_of((4 * part + 2 * at_high + (core ^ flip)) * own, own)
                copies.append((ref.at[pl.ds((2 * part + at_high) * own, own)], mixed, put))
        for n, ref in enumerate((g0, g1, g2, g3)):
            put = pl.multiple_of((4 * part + (place[0] ^ n)) * own, own)
            copies.append((ref.at[pl.ds(part * own, own)], grad, put))
    copies = [
        pltpu.make_async_copy(source, target.at[pl.ds(put, own)], sems.at[at])
        for at, (source, target, put) in enumerate(copies)
    ]
    for copy in copies:
        copy.start()
    for copy in copies:
        copy.wait()


def collect(place, mixed, grads):
    rows, width = grads[0].shape
    hbm = pl.BlockSpec(memory_space=pl.ANY)
    shape = jax.ShapeDtypeStruct((4 * rows, width), bf16)
    return pl.pallas_call(
        collect_body,
        in_specs=[pl.BlockSpec(memory_space=pltpu.SMEM)]
        + [pl.BlockSpec(memory_space=pltpu.VMEM)] * 6,
        out_specs=[hbm] * 2,
        out_shape=[shape] * 2,
        scratch_shapes=[pltpu.SemaphoreType.DMA((16,))],
        compiler_params=pltpu.CompilerParams(vmem_limit_bytes=16 * 2**20),
        cost_estimate=cost(3),
        name="collect",
    )(place, *mixed, *grads)


def swap(value, axis, mask):
    size = lax.axis_size(axis)
    return lax.ppermute(value, axis, [(i, i ^ mask) for i in range(size)])


def block_of(value, index, count):
    return lax.dynamic_slice_in_dim(value, index * count, count, 0)


def levels(size):
    bits = size.bit_length() - 1
    out = []
    shift = 0
    while shift < bits:
        wide = min(3, bits - shift)
        out.append((shift, wide))
        shift += wide
    return out


def groups_of(shift, wide):
    size = lax.axis_size("dp")
    count = 1 << wide
    return [
        [base + (n << shift) for n in range(count)]
        for base in range(size)
        if not (base >> shift) & (count - 1)
    ]


def exchange(value, shift, wide):
    return lax.all_to_all(
        value, "dp", split_axis=0, concat_axis=0, tiled=True,
        axis_index_groups=None if 1 << wide == lax.axis_size("dp") else groups_of(shift, wide),
    )


def gather_dp(value):
    sizes = [1 << wide for _, wide in levels(lax.axis_size("dp"))]
    whole_value = lax.all_gather(value, "dp", axis=0)
    if len(sizes) > 1:
        whole_value = whole_value.reshape(*sizes[::-1], *value.shape)
        whole_value = whole_value.transpose(
            *reversed(range(len(sizes))), len(sizes), len(sizes) + 1
        )
    return whole_value.reshape(sizes[0], -1, value.shape[1])


def first_parts():
    return 1 << levels(lax.axis_size("dp"))[0][1]


def start_dp(parts):
    return exchange(parts, *levels(lax.axis_size("dp"))[0])


def fold_dp(got):
    total = jnp.sum(got.astype(f32), axis=0)
    for shift, wide in levels(lax.axis_size("dp"))[1:]:
        parts = total.astype(bf16).reshape(1 << wide, -1, total.shape[1])
        total = jnp.sum(exchange(parts, shift, wide).astype(f32), axis=0)
    return total.astype(bf16)


def masks():
    return [1 << bit for bit in range(lax.axis_size("dp").bit_length() - 1)]


def halves(value, mask):
    bit = (lax.axis_index("dp") & mask) != 0
    rows = value.shape[0] // 2
    low, high = value[:rows], value[rows:]
    return jnp.where(bit, low, high), jnp.where(bit, high, low)


def give(value, small, mask):
    return jnp.concatenate([halves(value, mask)[0], small], axis=0)


def halve_dp(value, small, mask, other=None):
    return take(give(value, small, mask), halves(value, mask)[1], small, mask, other)


def take(given, kept, small, mask, other=None):
    got, other = lax.optimization_barrier((swap(given, "dp", mask), other))
    got = got.astype(f32)
    rows = kept.shape[0]
    value = (kept.astype(f32) + got[:rows]).astype(bf16)
    return value, (small.astype(f32) + got[rows:]).astype(bf16), other


def after(value, *others):
    return lax.optimization_barrier((value, others))[0]


def double_dp(value, mask, other=None):
    bit = (lax.axis_index("dp") & mask) != 0
    got, other = lax.optimization_barrier((swap(value, "dp", mask), other))
    value = jnp.concatenate([jnp.where(bit, got, value), jnp.where(bit, value, got)], axis=0)
    return value, other


def by_index(value):
    bits = len(masks())
    width = value.shape[-1]
    value = value.reshape((2,) * bits + (-1, width)).transpose(*reversed(range(bits)), bits, bits + 1)
    wides = [wide for _, wide in levels(lax.axis_size("dp"))]
    value = value.reshape(*[1 << wide for wide in reversed(wides)], -1, width)
    count = len(wides)
    value = value.transpose(*reversed(range(count)), count, count + 1)
    return value.reshape(1 << wides[0], -1, width)


def shards(
    tokens, item_kind, first_gain, first_shift, query_weight, key_weight, value_weight,
    position_weight, content_bias, position_bias, output_weight, second_gain, second_shift,
    inner_weight, inner_bias, outer_weight, outer_bias, cotangent,
):
    length, width = tokens.shape
    cols = query_weight.shape[1]
    share = inner_weight.shape[1]
    mp = lax.axis_index("mp").astype(jnp.int32)
    core, high = mp & 1, mp >> 1
    low = lax.axis_index("dp").astype(jnp.int32) & 1
    place = jnp.stack([mp, core, high, low])
    half = length // 2
    block = min(512, half)
    per_half = half // block
    own = half // 4
    sin_table, cos_table = sinusoid(length, width)
    table = jnp.asarray(np.concatenate([sin_table, cos_table], axis=1), bf16)
    table_t = jnp.asarray(np.concatenate([sin_table, cos_table], axis=1).T, bf16)
    st = jnp.asarray(sin_table.T, f32)
    ct = jnp.asarray(cos_table.T, f32)
    gain1, shift1, gain2, shift2, bu = (
        v[None] for v in (first_gain, first_shift, second_gain, second_shift, outer_bias)
    )

    tie = lax.optimization_barrier
    wos = [output_weight] + [swap(output_weight, "mp", n) for n in (1, 2, 3)]
    bis = [inner_bias[None], swap(inner_bias[None], "mp", 1)]
    projections = (query_weight, key_weight, value_weight)
    normed, qc, qp, v, kt, p, ot, near, far, linv = attention_forward(
        item_kind, tokens, gain1, shift1, *projections, content_bias[None], position_bias[None],
        position_weight, st, ct, table, block,
    )
    near, far, wi, wu, wos, bis = tie((near, far, inner_weight, outer_weight, wos, bis))
    wis = [inner_weight, swap(wi, "mp", 1)]
    wus = [outer_weight, swap(wu, "mp", 1)]
    atts = [swap(near, "mp", 1), swap(far, "mp", 2), swap(near, "mp", 3)]
    attended = far
    back_keep, back_send, out, residual, bias, near, keep = feed(
        place, tokens, cotangent, far, atts, wos, wis, wus, bis, bu, gain2, shift2
    )
    back_got = swap(back_send, "mp", 2)
    near_got = swap(near, "mp", 1)
    feed_sum = (keep.astype(f32) + near_got.astype(f32)).astype(bf16)
    feed_got = start_dp(feed_sum)

    res, sums, *turned = turn(
        place, back_keep, back_got, residual, cotangent, attended, atts, wos, gain2
    )
    grads, weight_parts = turned[:4], turned[4:]
    grads = [grads[0]] + [swap(grads[n], "mp", n) for n in (1, 2, 3)]
    sums = jnp.concatenate([sums, bias[:1] + swap(bias[1:], "mp", 1)], axis=0)
    out_send = after(out, grads[1])
    weight_parts = after(weight_parts, grads[1])
    weight_parts = [weight_parts[0]] + [swap(weight_parts[n], "mp", n) for n in (1, 2, 3)]
    out_got = swap(out_send, "mp", 2)

    given, kept, small, near, keep = attention_backward(
        item_kind, place, p, grads, ot, linv, qc, qp, v, kt, table_t, position_weight,
        st, ct, *projections, normed, gain1, shift1, sums, block,
    )
    given, kept, small, near, keep, weight_parts, out_got, feed_got = tie(
        (given, kept, small, near, keep, weight_parts, out_got, feed_got)
    )
    near = swap(near, "mp", 1)
    out_sum = sum(x.astype(f32) for x in weight_parts)
    fill = lambda value, there: (
        value.astype(f32)
        + jnp.pad(out_sum * there.astype(f32), ((0, value.shape[0] - cols), (0, 0)))
    ).astype(bf16)
    given = fill(given, low)
    kept = fill(kept, 1 - low)
    pick = lambda x: lax.dynamic_index_in_dim(x.reshape(2, 2, own, width), 1 - high, 1, False)
    far = (pick(keep).astype(f32) + pick(near).astype(f32)).astype(bf16).reshape(2 * own, width)
    first, *middle = masks()
    feed_total = fold_dp(after(feed_got, given, far))
    far = swap(far, "mp", 2)

    last, small, far = take(given, kept, small, first, far)
    mixed = (out.astype(f32) + out_got.astype(f32)).astype(bf16)
    mixed = [mixed, swap(mixed, "mp", 1)]
    grad = close(place, keep, near, far, tokens, res, gain1)
    beyond = swap(grad, "mp", 2)
    for mask in reversed(masks()):
        feed_total, _ = double_dp(feed_total, mask)
    for mask in middle:
        last, small, _ = halve_dp(last, small, mask)
    for mask in reversed(middle):
        last, _ = double_dp(last, mask)
    tokens_grad = [grad, swap(grad, "mp", 1), beyond, swap(beyond, "mp", 1)]
    small = after(small, last)
    mixed, tokens_grad = collect(place, mixed, tokens_grad)
    last_total, (mixed, tokens_grad) = double_dp(last, first, (mixed, tokens_grad))
    last_total = last_total.astype(f32)
    last_small = small.astype(f32)
    feed_total = by_index(feed_total)

    summed = last_small[:5]
    summed = summed + swap(summed, "mp", 1)
    summed = summed + swap(summed, "mp", 2)
    feed_total = feed_total.astype(f32)
    split = width // first_parts()
    inner_grad = feed_total[:, :split].reshape(width, share)
    outer_grad = feed_total[:, split:].reshape(share, width)
    whole_grad = last_total[cols:]

    return (
        mixed,
        tokens_grad,
        summed[0],
        summed[1],
        whole_grad[:, :cols],
        whole_grad[:, cols : 2 * cols],
        whole_grad[:, 2 * cols : 3 * cols],
        whole_grad[:, 3 * cols :],
        last_small[6, :cols],
        last_small[6, cols : 2 * cols],
        last_total[:cols],
        summed[2],
        summed[3],
        inner_grad,
        last_small[5],
        outer_grad,
        summed[4],
    )


def solution(mesh):
    return jax.shard_map(
        shards,
        mesh=mesh,
        in_specs=(
            P("dp", None), P("dp"), P(), P(), P(None, "mp"), P(None, "mp"), P(None, "mp"),
            P(None, "mp"), P("mp"), P("mp"), P("mp", None), P(), P(), P(None, "mp"), P("mp"),
            P("mp", None), P(), P("dp", None),
        ),
        out_specs=(
            P("dp", None), P("dp", None), P(), P(), P(None, "mp"), P(None, "mp"), P(None, "mp"),
            P(None, "mp"), P("mp"), P("mp"), P("mp", None), P(), P(), P(None, "mp"), P("mp"),
            P("mp", None), P(),
        ),
        check_vma=False,
    )
```

```python
import functools
import math

import jax
import jax.numpy as jnp
import numpy as np
from jax import lax
from jax.experimental import pallas as pl
from jax.experimental.pallas import tpu as pltpu
from jax.sharding import PartitionSpec as P

DH = 64
EPS = 1e-05
NEG = -1e30
LOG2E = 1.4426950408889634
GELU_A = 0.7978845608028654
GELU_B = 0.044715

f32 = jnp.float32
bf16 = jnp.bfloat16


def sinusoid(count, model_width):
    freqs = np.exp(np.arange(model_width // 2) * (-2.0 * math.log(10000.0) / model_width))
    angles = np.arange(count)[:, None] * freqs[None, :]
    return np.sin(angles), np.cos(angles)


def dot(left, right):
    return jnp.dot(left, right, preferred_element_type=f32)


def dot_nt(left, right):
    return lax.dot_general(left, right, (((1,), (1,)), ((), ())), preferred_element_type=f32)


def whole(shape):
    return pl.BlockSpec(shape, lambda *ids: (0,) * len(shape))


def params(mib=57):
    return pltpu.CompilerParams(
        vmem_limit_bytes=mib * 2**20, dimension_semantics=("arbitrary",)
    )


def cost(microseconds):
    return pl.CostEstimate(
        flops=int(microseconds * 1.1e9), bytes_accessed=1 << 10, transcendentals=0
    )


def keep_rows(values, head):
    ids = lax.broadcasted_iota(jnp.int32, values.shape, 0)
    return jnp.where(ids // DH == head, values, jnp.zeros_like(values))


def keep_cols(values, head):
    ids = lax.broadcasted_iota(jnp.int32, values.shape, 1)
    return jnp.where(ids // DH == head, values, jnp.zeros_like(values))


def norm_parts(values):
    center = values - jnp.mean(values, axis=-1, keepdims=True)
    spread = jnp.mean(center * center, axis=-1, keepdims=True)
    scale = lax.rsqrt(spread + EPS)
    return center * scale, scale


def forward_body(
    block, half_rows,
    kind, tokens, gain, shift, wq, wk, wv, cbias, pbias, wp, st, ct, table,
    normed_out, qc_out, qp_out, v_out, kt_out, p_out, ot_out, near_out, far_out, linv_out,
    pbuf, puts, sems, wcat, kcat, vt, qa, s_scr, m_scr, l_scr, acc,
):
    ib = pl.program_id(0)
    here = pl.multiple_of(ib * block, block)
    width, cols = wp.shape
    half = width // 2
    mid = block // 2

    def put(of, c, slot):
        at = pl.multiple_of(c * block, block), pl.multiple_of(of * 2 * block, 2 * block)
        target = p_out.at[pl.ds(at[0], block), pl.ds(at[1], 2 * block)]
        return pltpu.make_async_copy(pbuf.at[slot], target, sems.at[slot])

    @pl.when(ib == 0)
    def start():
        puts[0] = 0
        for n, ref in enumerate((wq, wk, wv)):
            wcat[:, n * cols : (n + 1) * cols] = ref[...]

    normed, _ = norm_parts(tokens[...].astype(f32))
    normed_out[...] = normed.astype(bf16)
    hidden = (normed * gain[...] + shift[...]).astype(bf16)
    qkv = dot(hidden, wcat[...])
    queries, keys, values = (qkv[:, n * cols : (n + 1) * cols] for n in range(3))
    qc_out[...] = ((queries + cbias[...]) * 0.125).astype(bf16)
    qp_out[...] = ((queries + pbias[...]) * 0.125).astype(bf16)
    v_out[...] = values.astype(bf16)
    kcat[pl.ds(here, block), :width] = table[...]
    kcat[pl.ds(here, block), width:] = keys.astype(bf16)
    vt[:, pl.ds(here, block)] = values.T.astype(bf16)
    kt_out[...] = keys.T.astype(bf16)
    queries_t = queries.T
    column = lambda row: jnp.broadcast_to(row, (8, row.shape[1])).T[:, :1]
    content = ((queries_t + column(cbias[...])) * (0.125 * LOG2E)).astype(bf16)
    position = ((queries_t + column(pbias[...])) * (0.125 * LOG2E)).astype(bf16)
    for h in range(2):
        u = dot(wp[...], keep_rows(position, h))
        us, uc = u[:half], u[half:]
        to = slice(h * block, (h + 1) * block)
        qa[:half, to] = (uc * st[...] - us * ct[...]).astype(bf16)
        qa[half:width, to] = (us * st[...] + uc * ct[...]).astype(bf16)
        qa[width:, to] = keep_rows(content, h)
    lo = jnp.where((kind[0] == 1) & (ib * block >= half_rows), half_rows // block, 0)
    fold = lambda x, op: op(x.reshape(x.shape[0] // 8, 8, x.shape[1]), axis=0)
    rj = lax.broadcasted_iota(jnp.int32, (mid, block), 0)
    ri = lax.broadcasted_iota(jnp.int32, (mid, block), 1)
    first = pl.ds(here, mid)
    second = pl.ds(pl.multiple_of(here + mid, mid), mid)

    s = dot(kcat[first, :], qa[...])
    s = jnp.where(jnp.concatenate([rj <= ri] * 2, axis=1), s, NEG)
    s_scr[first, :] = s
    m_scr[...] = fold(s, jnp.max)
    for h in range(2):
        to = slice(h * block + mid, (h + 1) * block)
        s = dot(kcat[second, :], qa[:, to])
        s = jnp.where(rj[:, :mid] <= ri[:, :mid], s, NEG)
        s_scr[second, to] = s
        m_scr[:, to] = jnp.maximum(m_scr[:, to], fold(s, jnp.max))

    def score_loop(c, carry):
        rows = pl.ds(pl.multiple_of(c * block, block), block)
        s = dot(kcat[rows, :], qa[...])
        s_scr[rows, :] = s
        m_scr[...] = jnp.maximum(m_scr[...], fold(s, jnp.max))
        return carry

    lax.fori_loop(lo, ib, score_loop, 0)
    m_scr[...] = jnp.broadcast_to(jnp.max(m_scr[...], axis=0, keepdims=True), m_scr.shape)

    done = puts[0]
    slot = done & 3

    @pl.when(done >= 4)
    def free():
        put(ib, ib, slot).wait()

    p = jnp.exp2(s_scr[first, :] - m_scr[0:1])
    l_scr[...] = fold(p, jnp.sum)
    low = p.astype(bf16)
    pbuf[slot, :mid] = low
    for h in range(2):
        rows = slice(DH * h, DH * h + DH)
        to = slice(h * block + mid, (h + 1) * block)
        acc[rows] = dot(vt[rows, first], low[:, h * block : (h + 1) * block])
        p = jnp.exp2(s_scr[second, to] - m_scr[0:1, to])
        l_scr[:, to] += fold(p, jnp.sum)
        part = p.astype(bf16)
        pbuf[slot, mid:, to] = part
        acc[rows, mid:] += dot(vt[rows, second], part)

    put(ib, ib, slot).start()

    def prob_loop(c, done):
        slot = done & 3

        @pl.when(done >= 4)
        def free():
            put(ib, c, slot).wait()

        rows = pl.ds(pl.multiple_of(c * block, block), block)
        p = jnp.exp2(s_scr[rows, :] - m_scr[0:1])
        l_scr[...] += fold(p, jnp.sum)
        low = p.astype(bf16)
        pbuf[slot] = low
        put(ib, c, slot).start()
        for h in range(2):
            heads = slice(DH * h, DH * h + DH)
            acc[heads] += dot(vt[heads, rows], low[:, h * block : (h + 1) * block])
        return done + 1

    puts[0] = lax.fori_loop(lo, ib, prob_loop, done + 1)
    inverse = 1.0 / jnp.sum(l_scr[...], axis=0, keepdims=True)
    linv_out[...] = inverse
    attended = jnp.concatenate(
        [acc[DH * h : DH * h + DH] * inverse[:, h * block : (h + 1) * block] for h in range(2)],
        axis=0,
    )
    ot_out[...] = attended
    rows = attended.T.astype(bf16)
    even = (lax.axis_index("mp") & 1) == 0
    near_out[...] = jnp.where(even, rows[mid:], rows[:mid])
    far_out[...] = jnp.where(even, rows[:mid], rows[mid:])

    @pl.when(ib == pl.num_programs(0) - 1)
    def finish():
        for slot in range(4):
            put(ib, ib, slot).wait()


def attention_forward(
    kind, tokens, gain, shift, wq, wk, wv, cbias, pbias, wp, st, ct, table, block
):
    length, width = table.shape
    cols = wp.shape[1]
    count = length // block
    row = lambda n, w: pl.BlockSpec((n, w), lambda i: (i, 0))
    col = lambda n, w: pl.BlockSpec((n, w), lambda i: (0, i))
    shape = jax.ShapeDtypeStruct
    return pl.pallas_call(
        functools.partial(forward_body, block, length // 2),
        grid=(count,),
        in_specs=[
            pl.BlockSpec(memory_space=pltpu.SMEM), row(block, width),
            whole((1, width)), whole((1, width)), *[whole((width, cols))] * 3,
            whole((1, cols)), whole((1, cols)), whole((width, cols)),
            col(width // 2, block), col(width // 2, block), row(block, width),
        ],
        out_specs=[
            row(block, width), row(block, cols), row(block, cols), row(block, cols),
            col(cols, block), pl.BlockSpec(memory_space=pl.ANY), col(cols, block),
            row(block // 2, cols), row(block // 2, cols), col(1, 2 * block),
        ],
        out_shape=[
            shape((length, width), bf16),
            shape((length, cols), bf16), shape((length, cols), bf16), shape((length, cols), bf16),
            shape((cols, length), bf16),
            shape((length, 2 * length), bf16), shape((cols, length), f32),
            shape((length // 2, cols), bf16), shape((length // 2, cols), bf16),
            shape((1, 2 * length), f32),
        ],
        scratch_shapes=[
            pltpu.VMEM((4, block, 2 * block), bf16),
            pltpu.SMEM((1,), jnp.int32),
            pltpu.SemaphoreType.DMA((4,)),
            pltpu.VMEM((width, 3 * cols), bf16),
            pltpu.VMEM((length, width + cols), bf16),
            pltpu.VMEM((cols, length), bf16),
            pltpu.VMEM((width + cols, 2 * block), bf16),
            pltpu.VMEM((length, 2 * block), f32),
            pltpu.VMEM((8, 2 * block), f32),
            pltpu.VMEM((8, 2 * block), f32),
            pltpu.VMEM((cols, block), f32),
        ],
        compiler_params=params(),
        cost_estimate=cost(25),
        name="attention_forward",
    )(kind, tokens, gain, shift, wq, wk, wv, cbias, pbias, wp, st, ct, table)


def backward_body(
    count, block, half_rows,
    kind, place, p, d0, d1, d2, d3, ot, linv, qc, qp, v, kt, tt, wp, st, ct,
    wq, wk, wv, normed, gain, shift, sums,
    given, kept, small, near, mine,
    last, ktt, wcat, acc, dk, dv, low, low_t, d_scr, dcat, dstack, qstack, delta, mom, colsum, dwp, cb, pb,
):
    step = pl.program_id(0)
    ib = count - 1 - step
    width, cols = wp.shape
    half = width // 2
    mid = block // 2
    own = d0.shape[0] // 2

    @pl.when(step == 0)
    def start():
        for ref in (dk, dv, dwp, cb, pb, mom, colsum):
            ref[...] = jnp.zeros(ref.shape, f32)
        for n, ref in enumerate((wq, wk, wv)):
            wcat[:, n * cols : (n + 1) * cols] = ref[...]
        ktt[:DH] = kt[:DH]
        ktt[DH : DH + width] = tt[...]
        ktt[DH + width :] = kt[DH:]
        for n, ref in enumerate((d0, d1, d2, d3)):
            for part in range(2):
                at = pl.multiple_of((4 * part + (place[0] ^ n)) * own, own)
                d_scr[pl.ds(at, own), :] = ref[part * own : (part + 1) * own]

    lo = jnp.where((kind[0] == 1) & (ib * block >= half_rows), half_rows // block, 0)
    here = pl.multiple_of(ib * block, block)
    dt = d_scr[pl.ds(here, block), :].astype(f32).T
    scaled = jnp.concatenate(
        [
            dt[DH * h : DH * h + DH] * linv[:, h * block : (h + 1) * block]
            for h in range(2)
        ],
        axis=0,
    )
    scaled_rows = scaled.T.astype(bf16)
    scaled = scaled.astype(bf16)
    product = scaled.astype(f32) * ot[...]
    for h in range(2):
        to = slice(h * block, (h + 1) * block)
        dcat[:, to] = keep_rows(scaled, h)
        dstack[to] = keep_cols(scaled_rows, h)
        qstack[to] = keep_cols(qc[...], h)
        delta[:, to] = jnp.sum(product[DH * h : DH * h + DH], axis=0, keepdims=True)

    first = pl.ds(here, mid)
    second = pl.ds(pl.multiple_of(here + mid, mid), mid)
    pt = p[first, :]
    dp = dot(v[first, :], dcat[...])
    ds = (pt.astype(f32) * (dp - delta[...])).astype(bf16)
    dv[first, :] += dot(pt, dstack[...])
    dk[first, :] += dot(ds, qstack[...])
    for h in range(2):
        to = slice(h * block + mid, (h + 1) * block)
        rows = slice(DH * h, DH * h + DH + width)
        acc[h] = dot(ktt[rows, first], ds[:, h * block : (h + 1) * block])
        pt2 = p[second, to]
        dp2 = dot(v[second, :], dcat[:, to])
        ds2 = (pt2.astype(f32) * (dp2 - delta[:, to])).astype(bf16)
        dv[second, :] += dot(pt2, dstack[to])
        dk[second, :] += dot(ds2, qstack[to])
        acc[h, :, mid:] += dot(ktt[rows, second], ds2)

    def loop(c, carry):
        rows = pl.ds(pl.multiple_of(c * block, block), block)
        pt = p[rows, :]
        dp = dot(v[rows, :], dcat[...])
        ds = (pt.astype(f32) * (dp - delta[...])).astype(bf16)
        dv[rows, :] += dot(pt, dstack[...])
        dk[rows, :] += dot(ds, qstack[...])
        for h in range(2):
            acc[h] += dot(
                ktt[DH * h : DH * h + DH + width, rows], ds[:, h * block : (h + 1) * block]
            )
        return carry

    lax.fori_loop(lo, ib, loop, 0)
    wpt = wp[...].astype(f32).T.astype(bf16)
    dqs = []
    for h in range(2):
        base = DH * (1 - h)
        gs = acc[h, base : base + half]
        gc = acc[h, base + half : base + width]
        rs = (st[...] * gc - ct[...] * gs).astype(bf16)
        rc = (ct[...] * gc + st[...] * gs).astype(bf16)
        wh = wpt[DH * h : DH * h + DH]
        by_position = (dot(wh[:, :half], rs) + dot(wh[:, half:], rc)) * 0.125
        by_content = acc[h, width * h : width * h + DH] * 0.125
        qph = keep_cols(qp[...], h)
        dwp[:half] += dot(rs, qph)
        dwp[half:] += dot(rc, qph)
        cb[DH * h : DH * h + DH] += by_content
        pb[DH * h : DH * h + DH] += by_position
        dqs.append(by_content + by_position)
    dqt = jnp.concatenate(dqs, axis=0)
    rows = pl.ds(here, block)
    for n, (value, value_t) in enumerate(
        ((dqt.T, dqt), (dk[rows, :], dk[rows, :].T), (dv[rows, :], dv[rows, :].T))
    ):
        to = slice(n * cols, (n + 1) * cols)
        low[:, to] = value.astype(bf16)
        low_t[to] = value_t.astype(bf16)
    mom[...] += dot(low_t[...], normed[...])
    colsum[...] += jnp.sum(low[...].astype(f32), axis=0, keepdims=True)
    for ref, core in ((near, 1 - place[1]), (mine, place[1])):
        at = pl.multiple_of(core * own, own)
        ref[...] = dot_nt(low[pl.ds(at, own), :], wcat[...]).astype(ref.dtype)

    @pl.when(step == count - 1)
    def finish():
        as_row = lambda values: jnp.broadcast_to(
            jnp.sum(values, axis=1, keepdims=True), (values.shape[0], 128)
        ).T[:1]
        column = jnp.broadcast_to(colsum[...], (8, 3 * cols)).T[:, :1]
        weights = wcat[...].astype(f32).T
        by_gain = jnp.sum(mom[...] * weights, axis=0, keepdims=True)
        by_shift = jnp.sum(column * weights, axis=0, keepdims=True)
        full = (gain[...] * mom[...] + shift[...] * column).T.astype(bf16)
        biases = jnp.concatenate(
            [as_row(cb[...]), as_row(pb[...]), jnp.zeros((1, width - 2 * cols), f32)], axis=1
        )
        small[...] = jnp.concatenate(
            [by_gain, by_shift, sums[...], biases, jnp.zeros((9, width), f32)], axis=0
        ).astype(bf16)
        last[:cols] = jnp.zeros((cols, width), bf16)
        last[cols:, : 3 * cols] = full
        last[cols:, 3 * cols :] = dwp[...].astype(bf16)
        rows = kept.shape[0]
        given[:rows] = last[pl.ds(pl.multiple_of((1 - place[3]) * rows, rows), rows), :]
        given[rows:] = small[...]
        kept[...] = last[pl.ds(pl.multiple_of(place[3] * rows, rows), rows), :]


def attention_backward(
    kind, place, p, grads, ot, linv, qc, qp, v, kt, tt, wp, st, ct, wq, wk, wv, normed,
    gain, shift, sums, block,
):
    length, width = normed.shape
    cols = qc.shape[1]
    count = length // block
    quarter = length // 4
    col = lambda n, w: pl.BlockSpec((n, w), lambda i: (0, count - 1 - i))
    row = lambda n, w: pl.BlockSpec((n, w), lambda i: (count - 1 - i, 0))
    smem = pl.BlockSpec(memory_space=pltpu.SMEM)
    rows = (cols + width) // 2
    return pl.pallas_call(
        functools.partial(backward_body, count, block, length // 2),
        grid=(count,),
        in_specs=[
            smem, smem, col(length, 2 * block),
            *[whole((quarter, cols))] * 4,
            col(cols, block), col(1, 2 * block), row(block, cols), row(block, cols),
            whole(v.shape), whole(kt.shape), whole(tt.shape), whole(wp.shape),
            col(width // 2, block), col(width // 2, block),
            *[whole((width, cols))] * 3, row(block, width),
            whole(gain.shape), whole(shift.shape), whole(sums.shape),
        ],
        out_specs=[
            whole((rows + 16, width)), whole((rows, width)), whole((16, width)), row(block // 2, width), row(block // 2, width)
        ],
        out_shape=[
            jax.ShapeDtypeStruct((rows + 16, width), bf16),
            jax.ShapeDtypeStruct((rows, width), bf16),
            jax.ShapeDtypeStruct((16, width), bf16),
            jax.ShapeDtypeStruct((length // 2, width), bf16),
            jax.ShapeDtypeStruct((length // 2, width), bf16),
        ],
        scratch_shapes=[
            pltpu.VMEM((2 * rows, width), bf16),
            pltpu.VMEM((cols + width, length), bf16),
            pltpu.VMEM((width, 3 * cols), bf16),
            pltpu.VMEM((2, DH + width, block), f32),
            pltpu.VMEM((length, cols), f32),
            pltpu.VMEM((length, cols), f32),
            pltpu.VMEM((block, 3 * cols), bf16),
            pltpu.VMEM((3 * cols, block), bf16),
            pltpu.VMEM((length, cols), bf16),
            pltpu.VMEM((cols, 2 * block), bf16),
            pltpu.VMEM((2 * block, cols), bf16),
            pltpu.VMEM((2 * block, cols), bf16),
            pltpu.VMEM((1, 2 * block), f32),
            pltpu.VMEM((3 * cols, width), f32),
            pltpu.VMEM((1, 3 * cols), f32),
            pltpu.VMEM((width, cols), f32),
            pltpu.VMEM((cols, block), f32),
            pltpu.VMEM((cols, block), f32),
        ],
        compiler_params=params(),
        cost_estimate=cost(8),
        name="attention_backward",
    )(
        kind, place, p, *grads, ot, linv, qc, qp, v, kt, tt, wp, st, ct, wq, wk, wv, normed,
        gain, shift, sums,
    )


def feed_body(
    place, tokens, cot, own_att, a1, a2, a3, w0, w1, w2, w3, i0, i1, u0, u1, b0, b1,
    bu, gain, shift,
    back_keep, back_send, out, res_own, bias, near, keep,
    hidden_t, act_t, pres, cots,
):
    step = pl.program_id(0)
    own, width = res_own.shape
    steps = cots.shape[0] // (2 * own)

    @pl.when(step < steps)
    def rows():
        c = cot[...].reshape(2 * own, width)
        residual = tokens[...].reshape(2 * own, width).astype(f32)
        for att, wo in ((own_att, w0), (a1, w1), (a2, w2), (a3, w3)):
            residual = residual + dot(att[...], wo[...])
        normed, _ = norm_parts(residual)
        hidden = (normed * gain[...] + shift[...]).astype(bf16)
        here = pl.ds(pl.multiple_of(step * 2 * own, 2 * own), 2 * own)
        cots[here, :] = c
        hidden_t[:, here] = hidden.T
        mixed = 0.5 * (residual + bu[...])
        back = None
        sums = []
        for n, wi, wu, bi in ((0, i0, u0, b0), (1, i1, u1, b1)):
            x = dot(hidden, wi[...]) + bi[...]
            square = x * x
            t = jnp.tanh(GELU_A * x * (1.0 + GELU_B * square))
            act = (0.5 * x * (1.0 + t)).astype(bf16)
            slope = 0.5 * (1.0 + t) + (0.5 * GELU_A) * x * (1.0 - t * t) * (
                1.0 + (3.0 * GELU_B) * square
            )
            act_t[n, :, here] = act.T
            mixed = mixed + dot(act, wu[...])
            pre = (dot_nt(c, wu[...]) * slope).astype(bf16)
            pres[n, here, :] = pre
            sums.append(jnp.sum(pre.astype(f32), axis=0, keepdims=True))
            back_n = dot_nt(pre, wi[...])
            back = back_n if back is None else back + back_n
        out[...] = mixed.astype(bf16)
        sums = jnp.concatenate(sums, axis=0)
        low = place[2] == 0
        res_own[...] = jnp.where(low, residual[:own], residual[own:])
        back_keep[...] = jnp.where(low, back[:own], back[own:]).astype(bf16)
        back_send[...] = jnp.where(low, back[own:], back[:own]).astype(bf16)

        @pl.when(step == 0)
        def first():
            bias[...] = sums

        @pl.when(step > 0)
        def later():
            bias[...] += sums

    @pl.when(step == steps)
    def grads():
        for n, ref in ((1, near), (0, keep)):
            parts, length, _ = ref.shape
            share = length // 2
            inner = dot(hidden_t[...], pres[n]).astype(bf16)
            outer = dot(act_t[n], cots[...]).astype(bf16)
            for r in range(parts):
                ref[r, :share] = inner[r * share : (r + 1) * share]
                ref[r, share:] = outer[r * share : (r + 1) * share]


def feed(place, tokens, cot, own_att, atts, wos, wis, wus, bis, bu, gain, shift):
    length, width = tokens.shape
    cols = own_att.shape[1]
    share = wis[0].shape[1]
    rows = length // 2
    own = rows // 4
    spec = lambda s: pl.BlockSpec(s, lambda i, place: (0,) * len(s))
    at = lambda i: jnp.minimum(i, 1)
    step = lambda w: pl.BlockSpec((2 * own, w), lambda i, place: (at(i), 0))
    half = pl.BlockSpec((own, width), lambda i, place: (at(i), 0))
    parts = first_parts()
    grad_shape = (parts, (width + share) // parts, width)
    mine = lambda w: pl.BlockSpec((2, 1, own, w), lambda i, place: (at(i), place[1], 0, 0))
    split = lambda x: x.reshape(4, 2, own, x.shape[1])
    others = (*wos, *wis, *wus, *bis, bu, gain, shift)
    shape = jax.ShapeDtypeStruct
    return pl.pallas_call(
        feed_body,
        grid_spec=pltpu.PrefetchScalarGridSpec(
            num_scalar_prefetch=1,
            grid=(3,),
            in_specs=[mine(width), mine(width)]
            + [step(cols)] * 4
            + [spec(o.shape) for o in others],
            out_specs=[
                half, half, step(width), half, spec((2, share)), spec(grad_shape),
                spec(grad_shape),
            ],
            scratch_shapes=[
                pltpu.VMEM((width, rows), bf16),
                pltpu.VMEM((2, share, rows), bf16),
                pltpu.VMEM((2, rows, share), bf16),
                pltpu.VMEM((rows, width), bf16),
            ],
        ),
        out_shape=[
            shape((2 * own, width), bf16), shape((2 * own, width), bf16),
            shape((rows, width), bf16), shape((2 * own, width), f32), shape((2, share), f32),
            shape(grad_shape, bf16), shape(grad_shape, bf16),
        ],
        compiler_params=params(),
        cost_estimate=cost(13),
        name="feed",
    )(place, split(tokens), split(cot), own_att, *atts, *others)


def turn_body(
    place, keep, got, residual, cot, a0, a1, a2, a3, w0, w1, w2, w3, gain,
    res_out, sums_out, g0, g1, g2, g3, o0, o1, o2, o3,
):
    rows, width = keep.shape
    back = keep[...].astype(f32) + got[...].astype(f32)
    c = cot[...].reshape(rows, width).astype(f32)
    normed, scale = norm_parts(residual[...])
    fold = lambda values: jnp.sum(values, axis=0, keepdims=True)
    sums_out[...] = jnp.concatenate([fold(back * normed), fold(back), fold(c)], axis=0)
    e = back * gain[...]
    inner = (
        e
        - jnp.mean(e, axis=-1, keepdims=True)
        - normed * jnp.mean(e * normed, axis=-1, keepdims=True)
    )
    branch = (c + scale * inner).astype(bf16)
    res_out[...] = branch
    for wo, out in ((w0, g0), (w1, g1), (w2, g2), (w3, g3)):
        out[...] = dot_nt(branch, wo[...]).astype(bf16)
    for att, out in ((a0, o0), (a1, o1), (a2, o2), (a3, o3)):
        out[...] = dot(att[...].reshape(rows, out.shape[0]).T, branch).astype(out.dtype)


def turn(place, keep, got, residual, cot, own_att, others, wos, gain):
    rows, width = keep.shape
    own = rows // 2
    cols = wos[0].shape[0]
    spec = lambda s: pl.BlockSpec(s, lambda i, place: (0,) * len(s))
    mine = lambda w: pl.BlockSpec((2, 1, own, w), lambda i, place: (0, place[0], 0, 0))
    half = lambda w: pl.BlockSpec((2, 1, own, w), lambda i, place: (0, place[2], 0, 0))
    split = lambda x: x.reshape(2, -1, own, x.shape[1])
    shapes = [((rows, width), bf16), ((3, width), f32)]
    shapes = shapes + [((rows, cols), bf16)] * 4
    shapes = shapes + [((cols, width), t) for t in (f32, bf16, bf16, bf16)]
    return pl.pallas_call(
        turn_body,
        grid_spec=pltpu.PrefetchScalarGridSpec(
            num_scalar_prefetch=1,
            grid=(1,),
            in_specs=[spec(keep.shape)] * 3
            + [mine(width)]
            + [half(cols)] * 4
            + [spec(w.shape) for w in wos]
            + [spec(gain.shape)],
            out_specs=[spec(s) for s, _ in shapes],
        ),
        out_shape=[jax.ShapeDtypeStruct(s, t) for s, t in shapes],
        compiler_params=params(),
        cost_estimate=cost(60),
        name="turn",
    )(
        place, keep, got, residual, split(cot), split(own_att), *[split(x) for x in others],
        *wos, gain,
    )


def close_body(place, keep0, keep1, near0, near1, got, t0, t1, res, gain, out):
    own = t0.shape[0]
    for part, keep, near, tokens in ((0, keep0, near0, t0), (1, keep1, near1, t1)):
        rows = slice(part * own, (part + 1) * own)
        total = keep[...].astype(f32) + near[...].astype(f32) + got[rows].astype(f32)
        normed, scale = norm_parts(tokens[...].astype(f32))
        e = total * gain[...]
        inner = (
            e
            - jnp.mean(e, axis=-1, keepdims=True)
            - normed * jnp.mean(e * normed, axis=-1, keepdims=True)
        )
        out[rows] = (res[rows].astype(f32) + scale * inner).astype(bf16)


def close(place, keep, near, got, tokens, res, gain):
    rows, width = got.shape
    own = rows // 2
    spec = pl.BlockSpec((rows, width), lambda i, place: (0, 0))
    mine = lambda part: pl.BlockSpec((own, width), lambda i, place: (4 * part + place[0], 0))
    at = lambda part: pl.BlockSpec((own, width), lambda i, place: (2 * part + place[2], 0))
    return pl.pallas_call(
        close_body,
        grid_spec=pltpu.PrefetchScalarGridSpec(
            num_scalar_prefetch=1,
            grid=(1,),
            in_specs=[
                at(0), at(1), at(0), at(1), spec, mine(0), mine(1), spec,
                pl.BlockSpec((1, width), lambda i, place: (0, 0)),
            ],
            out_specs=spec,
        ),
        out_shape=jax.ShapeDtypeStruct((rows, width), bf16),
        compiler_params=params(),
        cost_estimate=cost(2),
        name="close",
    )(place, keep, keep, near, near, got, tokens, tokens, res, gain)


def collect_body(place, m0, m1, g0, g1, g2, g3, mixed, grad, sems):
    own = g0.shape[0] // 2
    core = place[1]
    copies = []
    for part in range(2):
        for flip, ref in ((0, m0), (1, m1)):
            for at_high in range(2):
                put = pl.multiple_of((4 * part + 2 * at_high + (core ^ flip)) * own, own)
                copies.append((ref.at[pl.ds((2 * part + at_high) * own, own)], mixed, put))
        for n, ref in enumerate((g0, g1, g2, g3)):
            put = pl.multiple_of((4 * part + (place[0] ^ n)) * own, own)
            copies.append((ref.at[pl.ds(part * own, own)], grad, put))
    copies = [
        pltpu.make_async_copy(source, target.at[pl.ds(put, own)], sems.at[at])
        for at, (source, target, put) in enumerate(copies)
    ]
    for copy in copies:
        copy.start()
    for copy in copies:
        copy.wait()


def collect(place, mixed, grads):
    rows, width = grads[0].shape
    hbm = pl.BlockSpec(memory_space=pl.ANY)
    shape = jax.ShapeDtypeStruct((4 * rows, width), bf16)
    return pl.pallas_call(
        collect_body,
        in_specs=[pl.BlockSpec(memory_space=pltpu.SMEM)]
        + [pl.BlockSpec(memory_space=pltpu.VMEM)] * 6,
        out_specs=[hbm] * 2,
        out_shape=[shape] * 2,
        scratch_shapes=[pltpu.SemaphoreType.DMA((16,))],
        compiler_params=pltpu.CompilerParams(vmem_limit_bytes=16 * 2**20),
        cost_estimate=cost(3),
        name="collect",
    )(place, *mixed, *grads)


def swap(value, axis, mask):
    size = lax.axis_size(axis)
    return lax.ppermute(value, axis, [(i, i ^ mask) for i in range(size)])


def block_of(value, index, count):
    return lax.dynamic_slice_in_dim(value, index * count, count, 0)


def levels(size):
    bits = size.bit_length() - 1
    out = []
    shift = 0
    while shift < bits:
        wide = min(3, bits - shift)
        out.append((shift, wide))
        shift += wide
    return out


def groups_of(shift, wide):
    size = lax.axis_size("dp")
    count = 1 << wide
    return [
        [base + (n << shift) for n in range(count)]
        for base in range(size)
        if not (base >> shift) & (count - 1)
    ]


def exchange(value, shift, wide):
    return lax.all_to_all(
        value, "dp", split_axis=0, concat_axis=0, tiled=True,
        axis_index_groups=None if 1 << wide == lax.axis_size("dp") else groups_of(shift, wide),
    )


def gather_dp(value):
    sizes = [1 << wide for _, wide in levels(lax.axis_size("dp"))]
    whole_value = lax.all_gather(value, "dp", axis=0)
    if len(sizes) > 1:
        whole_value = whole_value.reshape(*sizes[::-1], *value.shape)
        whole_value = whole_value.transpose(
            *reversed(range(len(sizes))), len(sizes), len(sizes) + 1
        )
    return whole_value.reshape(sizes[0], -1, value.shape[1])


def first_parts():
    return 1 << levels(lax.axis_size("dp"))[0][1]


def start_dp(parts):
    return exchange(parts, *levels(lax.axis_size("dp"))[0])


def fold_dp(got):
    total = jnp.sum(got.astype(f32), axis=0)
    for shift, wide in levels(lax.axis_size("dp"))[1:]:
        parts = total.astype(bf16).reshape(1 << wide, -1, total.shape[1])
        total = jnp.sum(exchange(parts, shift, wide).astype(f32), axis=0)
    return total.astype(bf16)


def masks():
    return [1 << bit for bit in range(lax.axis_size("dp").bit_length() - 1)]


def halves(value, mask):
    bit = (lax.axis_index("dp") & mask) != 0
    rows = value.shape[0] // 2
    low, high = value[:rows], value[rows:]
    return jnp.where(bit, low, high), jnp.where(bit, high, low)


def give(value, small, mask):
    return jnp.concatenate([halves(value, mask)[0], small], axis=0)


def halve_dp(value, small, mask, other=None):
    return take(give(value, small, mask), halves(value, mask)[1], small, mask, other)


def take(given, kept, small, mask, other=None):
    got, other = lax.optimization_barrier((swap(given, "dp", mask), other))
    got = got.astype(f32)
    rows = kept.shape[0]
    value = (kept.astype(f32) + got[:rows]).astype(bf16)
    return value, (small.astype(f32) + got[rows:]).astype(bf16), other


def add_dp(value, small, mask):
    got = swap(jnp.concatenate([value, small], axis=0), "dp", mask).astype(f32)
    rows = value.shape[0]
    value = (value.astype(f32) + got[:rows]).astype(bf16)
    return value, (small.astype(f32) + got[rows:]).astype(bf16)


def after(value, *others):
    return lax.optimization_barrier((value, others))[0]


def double_dp(value, mask, other=None):
    bit = (lax.axis_index("dp") & mask) != 0
    got, other = lax.optimization_barrier((swap(value, "dp", mask), other))
    value = jnp.concatenate([jnp.where(bit, got, value), jnp.where(bit, value, got)], axis=0)
    return value, other


def by_index(value):
    bits = len(masks())
    width = value.shape[-1]
    value = value.reshape((2,) * bits + (-1, width)).transpose(*reversed(range(bits)), bits, bits + 1)
    wides = [wide for _, wide in levels(lax.axis_size("dp"))]
    value = value.reshape(*[1 << wide for wide in reversed(wides)], -1, width)
    count = len(wides)
    value = value.transpose(*reversed(range(count)), count, count + 1)
    return value.reshape(1 << wides[0], -1, width)


def shards(
    tokens, item_kind, first_gain, first_shift, query_weight, key_weight, value_weight,
    position_weight, content_bias, position_bias, output_weight, second_gain, second_shift,
    inner_weight, inner_bias, outer_weight, outer_bias, cotangent,
):
    length, width = tokens.shape
    cols = query_weight.shape[1]
    share = inner_weight.shape[1]
    mp = lax.axis_index("mp").astype(jnp.int32)
    core, high = mp & 1, mp >> 1
    low = lax.axis_index("dp").astype(jnp.int32) & 1
    place = jnp.stack([mp, core, high, low])
    half = length // 2
    block = min(512, half)
    per_half = half // block
    own = half // 4
    sin_table, cos_table = sinusoid(length, width)
    table = jnp.asarray(np.concatenate([sin_table, cos_table], axis=1), bf16)
    table_t = jnp.asarray(np.concatenate([sin_table, cos_table], axis=1).T, bf16)
    st = jnp.asarray(sin_table.T, f32)
    ct = jnp.asarray(cos_table.T, f32)
    gain1, shift1, gain2, shift2, bu = (
        v[None] for v in (first_gain, first_shift, second_gain, second_shift, outer_bias)
    )

    tie = lax.optimization_barrier
    wos = [output_weight] + [swap(output_weight, "mp", n) for n in (1, 2, 3)]
    bis = [inner_bias[None], swap(inner_bias[None], "mp", 1)]
    projections = (query_weight, key_weight, value_weight)
    normed, qc, qp, v, kt, p, ot, near, far, linv = attention_forward(
        item_kind, tokens, gain1, shift1, *projections, content_bias[None], position_bias[None],
        position_weight, st, ct, table, block,
    )
    near, far, wi, wu, wos, bis = tie((near, far, inner_weight, outer_weight, wos, bis))
    wis = [inner_weight, swap(wi, "mp", 1)]
    wus = [outer_weight, swap(wu, "mp", 1)]
    atts = [swap(near, "mp", 1), swap(far, "mp", 2), swap(near, "mp", 3)]
    attended = far
    back_keep, back_send, out, residual, bias, near, keep = feed(
        place, tokens, cotangent, far, atts, wos, wis, wus, bis, bu, gain2, shift2
    )
    back_got = swap(back_send, "mp", 2)
    near_got = swap(near, "mp", 1)
    feed_sum = (keep.astype(f32) + near_got.astype(f32)).astype(bf16)
    feed_got = start_dp(feed_sum)

    res, sums, *turned = turn(
        place, back_keep, back_got, residual, cotangent, attended, atts, wos, gain2
    )
    grads, weight_parts = turned[:4], turned[4:]
    grads = [grads[0]] + [swap(grads[n], "mp", n) for n in (1, 2, 3)]
    sums = jnp.concatenate([sums, bias[:1] + swap(bias[1:], "mp", 1)], axis=0)
    out_send = after(out, grads[1])
    weight_parts = after(weight_parts, grads[1])
    weight_parts = [weight_parts[0]] + [swap(weight_parts[n], "mp", n) for n in (1, 2, 3)]
    out_got = swap(out_send, "mp", 2)

    given, kept, small, near, keep = attention_backward(
        item_kind, place, p, grads, ot, linv, qc, qp, v, kt, table_t, position_weight,
        st, ct, *projections, normed, gain1, shift1, sums, block,
    )
    given, kept, small, near, keep, weight_parts, out_got, feed_got = tie(
        (given, kept, small, near, keep, weight_parts, out_got, feed_got)
    )
    near = swap(near, "mp", 1)
    out_sum = sum(x.astype(f32) for x in weight_parts)
    fill = lambda value, there: (
        value.astype(f32)
        + jnp.pad(out_sum * there.astype(f32), ((0, value.shape[0] - cols), (0, 0)))
    ).astype(bf16)
    given = fill(given, low)
    kept = fill(kept, 1 - low)
    pick = lambda x: lax.dynamic_index_in_dim(x.reshape(2, 2, own, width), 1 - high, 1, False)
    far = (pick(keep).astype(f32) + pick(near).astype(f32)).astype(bf16).reshape(2 * own, width)
    first, *middle = masks()
    feed_total = fold_dp(after(feed_got, given, far))
    far = swap(far, "mp", 2)

    last, small, far = take(given, kept, small, first, far)
    mixed = (out.astype(f32) + out_got.astype(f32)).astype(bf16)
    mixed = [mixed, swap(mixed, "mp", 1)]
    grad = close(place, keep, near, far, tokens, res, gain1)
    beyond = swap(grad, "mp", 2)
    for mask in reversed(masks()):
        feed_total, _ = double_dp(feed_total, mask)
    for mask in middle[:-1]:
        last, small, _ = halve_dp(last, small, mask)
    last, small = add_dp(last, small, middle[-1])
    for mask in reversed(middle[:-1]):
        last, _ = double_dp(last, mask)
    tokens_grad = [grad, swap(grad, "mp", 1), beyond, swap(beyond, "mp", 1)]
    small = after(small, last)
    mixed, tokens_grad = collect(place, mixed, tokens_grad)
    last_total, (mixed, tokens_grad) = double_dp(last, first, (mixed, tokens_grad))
    last_total = last_total.astype(f32)
    last_small = small.astype(f32)
    feed_total = by_index(feed_total)

    summed = last_small[:5]
    summed = summed + swap(summed, "mp", 1)
    summed = summed + swap(summed, "mp", 2)
    feed_total = feed_total.astype(f32)
    split = width // first_parts()
    inner_grad = feed_total[:, :split].reshape(width, share)
    outer_grad = feed_total[:, split:].reshape(share, width)
    whole_grad = last_total[cols:]

    return (
        mixed,
        tokens_grad,
        summed[0],
        summed[1],
        whole_grad[:, :cols],
        whole_grad[:, cols : 2 * cols],
        whole_grad[:, 2 * cols : 3 * cols],
        whole_grad[:, 3 * cols :],
        last_small[6, :cols],
        last_small[6, cols : 2 * cols],
        last_total[:cols],
        summed[2],
        summed[3],
        inner_grad,
        last_small[5],
        outer_grad,
        summed[4],
    )


def solution(mesh):
    return jax.shard_map(
        shards,
        mesh=mesh,
        in_specs=(
            P("dp", None), P("dp"), P(), P(), P(None, "mp"), P(None, "mp"), P(None, "mp"),
            P(None, "mp"), P("mp"), P("mp"), P("mp", None), P(), P(), P(None, "mp"), P("mp"),
            P("mp", None), P(), P("dp", None),
        ),
        out_specs=(
            P("dp", None), P("dp", None), P(), P(), P(None, "mp"), P(None, "mp"), P(None, "mp"),
            P(None, "mp"), P("mp"), P("mp"), P("mp", None), P(), P(), P(None, "mp"), P("mp"),
            P("mp", None), P(),
        ),
        check_vma=False,
    )
```

```python
import functools
import math

import jax
import jax.numpy as jnp
import numpy as np
from jax import lax
from jax.experimental import pallas as pl
from jax.experimental.pallas import tpu as pltpu
from jax.sharding import PartitionSpec as P

DH = 64
EPS = 1e-05
NEG = -1e30
LOG2E = 1.4426950408889634
GELU_A = 0.7978845608028654
GELU_B = 0.044715

f32 = jnp.float32
bf16 = jnp.bfloat16


def sinusoid(count, model_width):
    freqs = np.exp(np.arange(model_width // 2) * (-2.0 * math.log(10000.0) / model_width))
    angles = np.arange(count)[:, None] * freqs[None, :]
    return np.sin(angles), np.cos(angles)


def dot(left, right):
    return jnp.dot(left, right, preferred_element_type=f32)


def dot_nt(left, right):
    return lax.dot_general(left, right, (((1,), (1,)), ((), ())), preferred_element_type=f32)


def whole(shape):
    return pl.BlockSpec(shape, lambda *ids: (0,) * len(shape))


def params(mib=57):
    return pltpu.CompilerParams(
        vmem_limit_bytes=mib * 2**20, dimension_semantics=("arbitrary",)
    )


def cost(microseconds):
    return pl.CostEstimate(
        flops=int(microseconds * 1.1e9), bytes_accessed=1 << 10, transcendentals=0
    )


def keep_rows(values, head):
    ids = lax.broadcasted_iota(jnp.int32, values.shape, 0)
    return jnp.where(ids // DH == head, values, jnp.zeros_like(values))


def keep_cols(values, head):
    ids = lax.broadcasted_iota(jnp.int32, values.shape, 1)
    return jnp.where(ids // DH == head, values, jnp.zeros_like(values))


def norm_parts(values):
    center = values - jnp.mean(values, axis=-1, keepdims=True)
    spread = jnp.mean(center * center, axis=-1, keepdims=True)
    scale = lax.rsqrt(spread + EPS)
    return center * scale, scale


def forward_body(
    block, half_rows,
    kind, tokens, gain, shift, wq, wk, wv, cbias, pbias, wp, st, ct, table,
    normed_out, qc_out, qp_out, v_out, kt_out, p_out, ot_out, near_out, far_out, linv_out,
    pbuf, puts, sems, wcat, kcat, vt, qa, s_scr, m_scr, l_scr, acc,
):
    ib = pl.program_id(0)
    here = pl.multiple_of(ib * block, block)
    width, cols = wp.shape
    half = width // 2
    mid = block // 2

    def put(of, c, slot):
        at = pl.multiple_of(c * block, block), pl.multiple_of(of * 2 * block, 2 * block)
        target = p_out.at[pl.ds(at[0], block), pl.ds(at[1], 2 * block)]
        return pltpu.make_async_copy(pbuf.at[slot], target, sems.at[slot])

    @pl.when(ib == 0)
    def start():
        puts[0] = 0
        for n, ref in enumerate((wq, wk, wv)):
            wcat[:, n * cols : (n + 1) * cols] = ref[...]

    normed, _ = norm_parts(tokens[...].astype(f32))
    normed_out[...] = normed.astype(bf16)
    hidden = (normed * gain[...] + shift[...]).astype(bf16)
    qkv = dot(hidden, wcat[...])
    queries, keys, values = (qkv[:, n * cols : (n + 1) * cols] for n in range(3))
    qc_out[...] = ((queries + cbias[...]) * 0.125).astype(bf16)
    qp_out[...] = ((queries + pbias[...]) * 0.125).astype(bf16)
    v_out[...] = values.astype(bf16)
    kcat[pl.ds(here, block), :width] = table[...]
    kcat[pl.ds(here, block), width:] = keys.astype(bf16)
    vt[:, pl.ds(here, block)] = values.T.astype(bf16)
    kt_out[...] = keys.T.astype(bf16)
    queries_t = queries.T
    column = lambda row: jnp.broadcast_to(row, (8, row.shape[1])).T[:, :1]
    content = ((queries_t + column(cbias[...])) * (0.125 * LOG2E)).astype(bf16)
    position = ((queries_t + column(pbias[...])) * (0.125 * LOG2E)).astype(bf16)
    for h in range(2):
        u = dot(wp[...], keep_rows(position, h))
        us, uc = u[:half], u[half:]
        to = slice(h * block, (h + 1) * block)
        qa[:half, to] = (uc * st[...] - us * ct[...]).astype(bf16)
        qa[half:width, to] = (us * st[...] + uc * ct[...]).astype(bf16)
        qa[width:, to] = keep_rows(content, h)
    lo = jnp.where((kind[0] == 1) & (ib * block >= half_rows), half_rows // block, 0)
    fold = lambda x, op: op(x.reshape(x.shape[0] // 8, 8, x.shape[1]), axis=0)
    rj = lax.broadcasted_iota(jnp.int32, (mid, block), 0)
    ri = lax.broadcasted_iota(jnp.int32, (mid, block), 1)
    first = pl.ds(here, mid)
    second = pl.ds(pl.multiple_of(here + mid, mid), mid)

    s = dot(kcat[first, :], qa[...])
    s = jnp.where(jnp.concatenate([rj <= ri] * 2, axis=1), s, NEG)
    s_scr[first, :] = s
    m_scr[...] = fold(s, jnp.max)
    for h in range(2):
        to = slice(h * block + mid, (h + 1) * block)
        s = dot(kcat[second, :], qa[:, to])
        s = jnp.where(rj[:, :mid] <= ri[:, :mid], s, NEG)
        s_scr[second, to] = s
        m_scr[:, to] = jnp.maximum(m_scr[:, to], fold(s, jnp.max))

    def score_loop(c, carry):
        rows = pl.ds(pl.multiple_of(c * block, block), block)
        s = dot(kcat[rows, :], qa[...])
        s_scr[rows, :] = s
        m_scr[...] = jnp.maximum(m_scr[...], fold(s, jnp.max))
        return carry

    lax.fori_loop(lo, ib, score_loop, 0)
    m_scr[...] = jnp.broadcast_to(jnp.max(m_scr[...], axis=0, keepdims=True), m_scr.shape)

    done = puts[0]
    slot = done & 3

    @pl.when(done >= 4)
    def free():
        put(ib, ib, slot).wait()

    p = jnp.exp2(s_scr[first, :] - m_scr[0:1])
    l_scr[...] = fold(p, jnp.sum)
    low = p.astype(bf16)
    pbuf[slot, :mid] = low
    for h in range(2):
        rows = slice(DH * h, DH * h + DH)
        to = slice(h * block + mid, (h + 1) * block)
        acc[rows] = dot(vt[rows, first], low[:, h * block : (h + 1) * block])
        p = jnp.exp2(s_scr[second, to] - m_scr[0:1, to])
        l_scr[:, to] += fold(p, jnp.sum)
        part = p.astype(bf16)
        pbuf[slot, mid:, to] = part
        acc[rows, mid:] += dot(vt[rows, second], part)

    put(ib, ib, slot).start()

    def prob_loop(c, done):
        slot = done & 3

        @pl.when(done >= 4)
        def free():
            put(ib, c, slot).wait()

        rows = pl.ds(pl.multiple_of(c * block, block), block)
        p = jnp.exp2(s_scr[rows, :] - m_scr[0:1])
        l_scr[...] += fold(p, jnp.sum)
        low = p.astype(bf16)
        pbuf[slot] = low
        put(ib, c, slot).start()
        for h in range(2):
            heads = slice(DH * h, DH * h + DH)
            acc[heads] += dot(vt[heads, rows], low[:, h * block : (h + 1) * block])
        return done + 1

    puts[0] = lax.fori_loop(lo, ib, prob_loop, done + 1)
    inverse = 1.0 / jnp.sum(l_scr[...], axis=0, keepdims=True)
    linv_out[...] = inverse
    attended = jnp.concatenate(
        [acc[DH * h : DH * h + DH] * inverse[:, h * block : (h + 1) * block] for h in range(2)],
        axis=0,
    )
    ot_out[...] = attended
    rows = attended.T.astype(bf16)
    even = (lax.axis_index("mp") & 1) == 0
    near_out[...] = jnp.where(even, rows[mid:], rows[:mid])
    far_out[...] = jnp.where(even, rows[:mid], rows[mid:])

    @pl.when(ib == pl.num_programs(0) - 1)
    def finish():
        for slot in range(4):
            put(ib, ib, slot).wait()


def attention_forward(
    kind, tokens, gain, shift, wq, wk, wv, cbias, pbias, wp, st, ct, table, block
):
    length, width = table.shape
    cols = wp.shape[1]
    count = length // block
    row = lambda n, w: pl.BlockSpec((n, w), lambda i: (i, 0))
    col = lambda n, w: pl.BlockSpec((n, w), lambda i: (0, i))
    shape = jax.ShapeDtypeStruct
    return pl.pallas_call(
        functools.partial(forward_body, block, length // 2),
        grid=(count,),
        in_specs=[
            pl.BlockSpec(memory_space=pltpu.SMEM), row(block, width),
            whole((1, width)), whole((1, width)), *[whole((width, cols))] * 3,
            whole((1, cols)), whole((1, cols)), whole((width, cols)),
            col(width // 2, block), col(width // 2, block), row(block, width),
        ],
        out_specs=[
            row(block, width), row(block, cols), row(block, cols), row(block, cols),
            col(cols, block), pl.BlockSpec(memory_space=pl.ANY), col(cols, block),
            row(block // 2, cols), row(block // 2, cols), col(1, 2 * block),
        ],
        out_shape=[
            shape((length, width), bf16),
            shape((length, cols), bf16), shape((length, cols), bf16), shape((length, cols), bf16),
            shape((cols, length), bf16),
            shape((length, 2 * length), bf16), shape((cols, length), f32),
            shape((length // 2, cols), bf16), shape((length // 2, cols), bf16),
            shape((1, 2 * length), f32),
        ],
        scratch_shapes=[
            pltpu.VMEM((4, block, 2 * block), bf16),
            pltpu.SMEM((1,), jnp.int32),
            pltpu.SemaphoreType.DMA((4,)),
            pltpu.VMEM((width, 3 * cols), bf16),
            pltpu.VMEM((length, width + cols), bf16),
            pltpu.VMEM((cols, length), bf16),
            pltpu.VMEM((width + cols, 2 * block), bf16),
            pltpu.VMEM((length, 2 * block), f32),
            pltpu.VMEM((8, 2 * block), f32),
            pltpu.VMEM((8, 2 * block), f32),
            pltpu.VMEM((cols, block), f32),
        ],
        compiler_params=params(),
        cost_estimate=cost(25),
        name="attention_forward",
    )(kind, tokens, gain, shift, wq, wk, wv, cbias, pbias, wp, st, ct, table)


def backward_body(
    count, block, half_rows,
    kind, place, p, d0, d1, d2, d3, ot, linv, qc, qp, v, kt, tt, wp, st, ct,
    wq, wk, wv, normed, gain, shift, sums,
    given, kept, small, near, mine,
    last, ktt, wcat, acc, dk, dv, low, low_t, d_scr, dcat, dstack, qstack, delta, mom, colsum, dwp, cb, pb,
):
    step = pl.program_id(0)
    ib = count - 1 - step
    width, cols = wp.shape
    half = width // 2
    mid = block // 2
    own = d0.shape[0] // 2

    @pl.when(step == 0)
    def start():
        for ref in (dk, dv, dwp, cb, pb, mom, colsum):
            ref[...] = jnp.zeros(ref.shape, f32)
        for n, ref in enumerate((wq, wk, wv)):
            wcat[:, n * cols : (n + 1) * cols] = ref[...]
        ktt[:DH] = kt[:DH]
        ktt[DH : DH + width] = tt[...]
        ktt[DH + width :] = kt[DH:]
        for n, ref in enumerate((d0, d1, d2, d3)):
            for part in range(2):
                at = pl.multiple_of((4 * part + (place[0] ^ n)) * own, own)
                d_scr[pl.ds(at, own), :] = ref[part * own : (part + 1) * own]

    lo = jnp.where((kind[0] == 1) & (ib * block >= half_rows), half_rows // block, 0)
    here = pl.multiple_of(ib * block, block)
    dt = d_scr[pl.ds(here, block), :].astype(f32).T
    scaled = jnp.concatenate(
        [
            dt[DH * h : DH * h + DH] * linv[:, h * block : (h + 1) * block]
            for h in range(2)
        ],
        axis=0,
    )
    scaled_rows = scaled.T.astype(bf16)
    scaled = scaled.astype(bf16)
    product = scaled.astype(f32) * ot[...]
    for h in range(2):
        to = slice(h * block, (h + 1) * block)
        dcat[:, to] = keep_rows(scaled, h)
        dstack[to] = keep_cols(scaled_rows, h)
        qstack[to] = keep_cols(qc[...], h)
        delta[:, to] = jnp.sum(product[DH * h : DH * h + DH], axis=0, keepdims=True)

    first = pl.ds(here, mid)
    second = pl.ds(pl.multiple_of(here + mid, mid), mid)
    pt = p[first, :]
    dp = dot(v[first, :], dcat[...])
    ds = (pt.astype(f32) * (dp - delta[...])).astype(bf16)
    dv[first, :] += dot(pt, dstack[...])
    dk[first, :] += dot(ds, qstack[...])
    for h in range(2):
        to = slice(h * block + mid, (h + 1) * block)
        rows = slice(DH * h, DH * h + DH + width)
        acc[h] = dot(ktt[rows, first], ds[:, h * block : (h + 1) * block])
        pt2 = p[second, to]
        dp2 = dot(v[second, :], dcat[:, to])
        ds2 = (pt2.astype(f32) * (dp2 - delta[:, to])).astype(bf16)
        dv[second, :] += dot(pt2, dstack[to])
        dk[second, :] += dot(ds2, qstack[to])
        acc[h, :, mid:] += dot(ktt[rows, second], ds2)

    def loop(c, carry):
        rows = pl.ds(pl.multiple_of(c * block, block), block)
        pt = p[rows, :]
        dp = dot(v[rows, :], dcat[...])
        ds = (pt.astype(f32) * (dp - delta[...])).astype(bf16)
        dv[rows, :] += dot(pt, dstack[...])
        dk[rows, :] += dot(ds, qstack[...])
        for h in range(2):
            acc[h] += dot(
                ktt[DH * h : DH * h + DH + width, rows], ds[:, h * block : (h + 1) * block]
            )
        return carry

    lax.fori_loop(lo, ib, loop, 0)
    wpt = wp[...].astype(f32).T.astype(bf16)
    dqs = []
    for h in range(2):
        base = DH * (1 - h)
        gs = acc[h, base : base + half]
        gc = acc[h, base + half : base + width]
        rs = (st[...] * gc - ct[...] * gs).astype(bf16)
        rc = (ct[...] * gc + st[...] * gs).astype(bf16)
        wh = wpt[DH * h : DH * h + DH]
        by_position = (dot(wh[:, :half], rs) + dot(wh[:, half:], rc)) * 0.125
        by_content = acc[h, width * h : width * h + DH] * 0.125
        qph = keep_cols(qp[...], h)
        dwp[:half] += dot(rs, qph)
        dwp[half:] += dot(rc, qph)
        cb[DH * h : DH * h + DH] += by_content
        pb[DH * h : DH * h + DH] += by_position
        dqs.append(by_content + by_position)
    dqt = jnp.concatenate(dqs, axis=0)
    rows = pl.ds(here, block)
    for n, (value, value_t) in enumerate(
        ((dqt.T, dqt), (dk[rows, :], dk[rows, :].T), (dv[rows, :], dv[rows, :].T))
    ):
        to = slice(n * cols, (n + 1) * cols)
        low[:, to] = value.astype(bf16)
        low_t[to] = value_t.astype(bf16)
    mom[...] += dot(low_t[...], normed[...])
    colsum[...] += jnp.sum(low[...].astype(f32), axis=0, keepdims=True)
    for ref, core in ((near, 1 - place[1]), (mine, place[1])):
        at = pl.multiple_of(core * own, own)
        ref[...] = dot_nt(low[pl.ds(at, own), :], wcat[...]).astype(ref.dtype)

    @pl.when(step == count - 1)
    def finish():
        as_row = lambda values: jnp.broadcast_to(
            jnp.sum(values, axis=1, keepdims=True), (values.shape[0], 128)
        ).T[:1]
        column = jnp.broadcast_to(colsum[...], (8, 3 * cols)).T[:, :1]
        weights = wcat[...].astype(f32).T
        by_gain = jnp.sum(mom[...] * weights, axis=0, keepdims=True)
        by_shift = jnp.sum(column * weights, axis=0, keepdims=True)
        full = (gain[...] * mom[...] + shift[...] * column).T.astype(bf16)
        biases = jnp.concatenate(
            [as_row(cb[...]), as_row(pb[...]), jnp.zeros((1, width - 2 * cols), f32)], axis=1
        )
        small[...] = jnp.concatenate(
            [by_gain, by_shift, sums[...], biases, jnp.zeros((9, width), f32)], axis=0
        ).astype(bf16)
        last[:cols] = jnp.zeros((cols, width), bf16)
        last[cols:, : 3 * cols] = full
        last[cols:, 3 * cols :] = dwp[...].astype(bf16)
        rows = kept.shape[0]
        given[:rows] = last[pl.ds(pl.multiple_of((1 - place[3]) * rows, rows), rows), :]
        given[rows:] = small[...]
        kept[...] = last[pl.ds(pl.multiple_of(place[3] * rows, rows), rows), :]


def attention_backward(
    kind, place, p, grads, ot, linv, qc, qp, v, kt, tt, wp, st, ct, wq, wk, wv, normed,
    gain, shift, sums, block,
):
    length, width = normed.shape
    cols = qc.shape[1]
    count = length // block
    quarter = length // 4
    col = lambda n, w: pl.BlockSpec((n, w), lambda i: (0, count - 1 - i))
    row = lambda n, w: pl.BlockSpec((n, w), lambda i: (count - 1 - i, 0))
    smem = pl.BlockSpec(memory_space=pltpu.SMEM)
    rows = (cols + width) // 2
    return pl.pallas_call(
        functools.partial(backward_body, count, block, length // 2),
        grid=(count,),
        in_specs=[
            smem, smem, col(length, 2 * block),
            *[whole((quarter, cols))] * 4,
            col(cols, block), col(1, 2 * block), row(block, cols), row(block, cols),
            whole(v.shape), whole(kt.shape), whole(tt.shape), whole(wp.shape),
            col(width // 2, block), col(width // 2, block),
            *[whole((width, cols))] * 3, row(block, width),
            whole(gain.shape), whole(shift.shape), whole(sums.shape),
        ],
        out_specs=[
            whole((rows + 16, width)), whole((rows, width)), whole((16, width)), row(block // 2, width), row(block // 2, width)
        ],
        out_shape=[
            jax.ShapeDtypeStruct((rows + 16, width), bf16),
            jax.ShapeDtypeStruct((rows, width), bf16),
            jax.ShapeDtypeStruct((16, width), bf16),
            jax.ShapeDtypeStruct((length // 2, width), bf16),
            jax.ShapeDtypeStruct((length // 2, width), bf16),
        ],
        scratch_shapes=[
            pltpu.VMEM((2 * rows, width), bf16),
            pltpu.VMEM((cols + width, length), bf16),
            pltpu.VMEM((width, 3 * cols), bf16),
            pltpu.VMEM((2, DH + width, block), f32),
            pltpu.VMEM((length, cols), f32),
            pltpu.VMEM((length, cols), f32),
            pltpu.VMEM((block, 3 * cols), bf16),
            pltpu.VMEM((3 * cols, block), bf16),
            pltpu.VMEM((length, cols), bf16),
            pltpu.VMEM((cols, 2 * block), bf16),
            pltpu.VMEM((2 * block, cols), bf16),
            pltpu.VMEM((2 * block, cols), bf16),
            pltpu.VMEM((1, 2 * block), f32),
            pltpu.VMEM((3 * cols, width), f32),
            pltpu.VMEM((1, 3 * cols), f32),
            pltpu.VMEM((width, cols), f32),
            pltpu.VMEM((cols, block), f32),
            pltpu.VMEM((cols, block), f32),
        ],
        compiler_params=params(),
        cost_estimate=cost(8),
        name="attention_backward",
    )(
        kind, place, p, *grads, ot, linv, qc, qp, v, kt, tt, wp, st, ct, wq, wk, wv, normed,
        gain, shift, sums,
    )


def feed_body(
    place, tokens, cot, own_att, a1, a2, a3, w0, w1, w2, w3, i0, i1, u0, u1, b0, b1,
    bu, gain, shift,
    back_keep, back_send, out, res_own, bias, near, keep,
    hidden_t, act_t, pres, cots,
):
    step = pl.program_id(0)
    own, width = res_own.shape
    steps = cots.shape[0] // (2 * own)

    @pl.when(step < steps)
    def rows():
        c = cot[...].reshape(2 * own, width)
        residual = tokens[...].reshape(2 * own, width).astype(f32)
        for att, wo in ((own_att, w0), (a1, w1), (a2, w2), (a3, w3)):
            residual = residual + dot(att[...], wo[...])
        normed, _ = norm_parts(residual)
        hidden = (normed * gain[...] + shift[...]).astype(bf16)
        here = pl.ds(pl.multiple_of(step * 2 * own, 2 * own), 2 * own)
        cots[here, :] = c
        hidden_t[:, here] = hidden.T
        mixed = 0.5 * (residual + bu[...])
        back = None
        sums = []
        for n, wi, wu, bi in ((0, i0, u0, b0), (1, i1, u1, b1)):
            x = dot(hidden, wi[...]) + bi[...]
            square = x * x
            t = jnp.tanh(GELU_A * x * (1.0 + GELU_B * square))
            act = (0.5 * x * (1.0 + t)).astype(bf16)
            slope = 0.5 * (1.0 + t) + (0.5 * GELU_A) * x * (1.0 - t * t) * (
                1.0 + (3.0 * GELU_B) * square
            )
            act_t[n, :, here] = act.T
            mixed = mixed + dot(act, wu[...])
            pre = (dot_nt(c, wu[...]) * slope).astype(bf16)
            pres[n, here, :] = pre
            sums.append(jnp.sum(pre.astype(f32), axis=0, keepdims=True))
            back_n = dot_nt(pre, wi[...])
            back = back_n if back is None else back + back_n
        out[...] = mixed.astype(bf16)
        sums = jnp.concatenate(sums, axis=0)
        low = place[2] == 0
        res_own[...] = jnp.where(low, residual[:own], residual[own:]).astype(bf16)
        back_keep[...] = jnp.where(low, back[:own], back[own:]).astype(bf16)
        back_send[...] = jnp.where(low, back[own:], back[:own]).astype(bf16)

        @pl.when(step == 0)
        def first():
            bias[...] = sums

        @pl.when(step > 0)
        def later():
            bias[...] += sums

    @pl.when(step == steps)
    def grads():
        for n, ref in ((1, near), (0, keep)):
            parts, length, _ = ref.shape
            share = length // 2
            inner = dot(hidden_t[...], pres[n]).astype(bf16)
            outer = dot(act_t[n], cots[...]).astype(bf16)
            for r in range(parts):
                ref[r, :share] = inner[r * share : (r + 1) * share]
                ref[r, share:] = outer[r * share : (r + 1) * share]


def feed(place, tokens, cot, own_att, atts, wos, wis, wus, bis, bu, gain, shift):
    length, width = tokens.shape
    cols = own_att.shape[1]
    share = wis[0].shape[1]
    rows = length // 2
    own = rows // 4
    spec = lambda s: pl.BlockSpec(s, lambda i, place: (0,) * len(s))
    at = lambda i: jnp.minimum(i, 1)
    step = lambda w: pl.BlockSpec((2 * own, w), lambda i, place: (at(i), 0))
    half = pl.BlockSpec((own, width), lambda i, place: (at(i), 0))
    parts = first_parts()
    grad_shape = (parts, (width + share) // parts, width)
    mine = lambda w: pl.BlockSpec((2, 1, own, w), lambda i, place: (at(i), place[1], 0, 0))
    split = lambda x: x.reshape(4, 2, own, x.shape[1])
    others = (*wos, *wis, *wus, *bis, bu, gain, shift)
    shape = jax.ShapeDtypeStruct
    return pl.pallas_call(
        feed_body,
        grid_spec=pltpu.PrefetchScalarGridSpec(
            num_scalar_prefetch=1,
            grid=(3,),
            in_specs=[mine(width), mine(width)]
            + [step(cols)] * 4
            + [spec(o.shape) for o in others],
            out_specs=[
                half, half, step(width), half, spec((2, share)), spec(grad_shape),
                spec(grad_shape),
            ],
            scratch_shapes=[
                pltpu.VMEM((width, rows), bf16),
                pltpu.VMEM((2, share, rows), bf16),
                pltpu.VMEM((2, rows, share), bf16),
                pltpu.VMEM((rows, width), bf16),
            ],
        ),
        out_shape=[
            shape((2 * own, width), bf16), shape((2 * own, width), bf16),
            shape((rows, width), bf16), shape((2 * own, width), bf16), shape((2, share), f32),
            shape(grad_shape, bf16), shape(grad_shape, bf16),
        ],
        compiler_params=params(),
        cost_estimate=cost(13),
        name="feed",
    )(place, split(tokens), split(cot), own_att, *atts, *others)


def turn_body(
    place, keep, got, residual, cot, a0, a1, a2, a3, w0, w1, w2, w3, gain,
    res_out, sums_out, g0, g1, g2, g3, o0, o1, o2, o3,
):
    rows, width = keep.shape
    back = keep[...].astype(f32) + got[...].astype(f32)
    c = cot[...].reshape(rows, width).astype(f32)
    normed, scale = norm_parts(residual[...].astype(f32))
    fold = lambda values: jnp.sum(values, axis=0, keepdims=True)
    sums_out[...] = jnp.concatenate([fold(back * normed), fold(back), fold(c)], axis=0)
    e = back * gain[...]
    inner = (
        e
        - jnp.mean(e, axis=-1, keepdims=True)
        - normed * jnp.mean(e * normed, axis=-1, keepdims=True)
    )
    branch = (c + scale * inner).astype(bf16)
    res_out[...] = branch
    for wo, out in ((w0, g0), (w1, g1), (w2, g2), (w3, g3)):
        out[...] = dot_nt(branch, wo[...]).astype(bf16)
    for att, out in ((a0, o0), (a1, o1), (a2, o2), (a3, o3)):
        out[...] = dot(att[...].reshape(rows, out.shape[0]).T, branch).astype(out.dtype)


def turn(place, keep, got, residual, cot, own_att, others, wos, gain):
    rows, width = keep.shape
    own = rows // 2
    cols = wos[0].shape[0]
    spec = lambda s: pl.BlockSpec(s, lambda i, place: (0,) * len(s))
    mine = lambda w: pl.BlockSpec((2, 1, own, w), lambda i, place: (0, place[0], 0, 0))
    half = lambda w: pl.BlockSpec((2, 1, own, w), lambda i, place: (0, place[2], 0, 0))
    split = lambda x: x.reshape(2, -1, own, x.shape[1])
    shapes = [((rows, width), bf16), ((3, width), f32)]
    shapes = shapes + [((rows, cols), bf16)] * 4
    shapes = shapes + [((cols, width), t) for t in (f32, bf16, bf16, bf16)]
    return pl.pallas_call(
        turn_body,
        grid_spec=pltpu.PrefetchScalarGridSpec(
            num_scalar_prefetch=1,
            grid=(1,),
            in_specs=[spec(keep.shape)] * 3
            + [mine(width)]
            + [half(cols)] * 4
            + [spec(w.shape) for w in wos]
            + [spec(gain.shape)],
            out_specs=[spec(s) for s, _ in shapes],
        ),
        out_shape=[jax.ShapeDtypeStruct(s, t) for s, t in shapes],
        compiler_params=params(),
        cost_estimate=cost(60),
        name="turn",
    )(
        place, keep, got, residual, split(cot), split(own_att), *[split(x) for x in others],
        *wos, gain,
    )


def close_body(place, keep0, keep1, near0, near1, got, t0, t1, res, gain, out):
    own = t0.shape[0]
    for part, keep, near, tokens in ((0, keep0, near0, t0), (1, keep1, near1, t1)):
        rows = slice(part * own, (part + 1) * own)
        total = keep[...].astype(f32) + near[...].astype(f32) + got[rows].astype(f32)
        normed, scale = norm_parts(tokens[...].astype(f32))
        e = total * gain[...]
        inner = (
            e
            - jnp.mean(e, axis=-1, keepdims=True)
            - normed * jnp.mean(e * normed, axis=-1, keepdims=True)
        )
        out[rows] = (res[rows].astype(f32) + scale * inner).astype(bf16)


def close(place, keep, near, got, tokens, res, gain):
    rows, width = got.shape
    own = rows // 2
    spec = pl.BlockSpec((rows, width), lambda i, place: (0, 0))
    mine = lambda part: pl.BlockSpec((own, width), lambda i, place: (4 * part + place[0], 0))
    at = lambda part: pl.BlockSpec((own, width), lambda i, place: (2 * part + place[2], 0))
    return pl.pallas_call(
        close_body,
        grid_spec=pltpu.PrefetchScalarGridSpec(
            num_scalar_prefetch=1,
            grid=(1,),
            in_specs=[
                at(0), at(1), at(0), at(1), spec, mine(0), mine(1), spec,
                pl.BlockSpec((1, width), lambda i, place: (0, 0)),
            ],
            out_specs=spec,
        ),
        out_shape=jax.ShapeDtypeStruct((rows, width), bf16),
        compiler_params=params(),
        cost_estimate=cost(2),
        name="close",
    )(place, keep, keep, near, near, got, tokens, tokens, res, gain)


def collect_body(place, m0, m1, g0, g1, g2, g3, mixed, grad, sems):
    own = g0.shape[0] // 2
    core = place[1]
    copies = []
    for part in range(2):
        for flip, ref in ((0, m0), (1, m1)):
            for at_high in range(2):
                put = pl.multiple_of((4 * part + 2 * at_high + (core ^ flip)) * own, own)
                copies.append((ref.at[pl.ds((2 * part + at_high) * own, own)], mixed, put))
        for n, ref in enumerate((g0, g1, g2, g3)):
            put = pl.multiple_of((4 * part + (place[0] ^ n)) * own, own)
            copies.append((ref.at[pl.ds(part * own, own)], grad, put))
    copies = [
        pltpu.make_async_copy(source, target.at[pl.ds(put, own)], sems.at[at])
        for at, (source, target, put) in enumerate(copies)
    ]
    for copy in copies:
        copy.start()
    for copy in copies:
        copy.wait()


def collect(place, mixed, grads):
    rows, width = grads[0].shape
    hbm = pl.BlockSpec(memory_space=pl.ANY)
    shape = jax.ShapeDtypeStruct((4 * rows, width), bf16)
    return pl.pallas_call(
        collect_body,
        in_specs=[pl.BlockSpec(memory_space=pltpu.SMEM)]
        + [pl.BlockSpec(memory_space=pltpu.VMEM)] * 6,
        out_specs=[hbm] * 2,
        out_shape=[shape] * 2,
        scratch_shapes=[pltpu.SemaphoreType.DMA((16,))],
        compiler_params=pltpu.CompilerParams(vmem_limit_bytes=16 * 2**20),
        cost_estimate=cost(3),
        name="collect",
    )(place, *mixed, *grads)


def swap(value, axis, mask):
    size = lax.axis_size(axis)
    return lax.ppermute(value, axis, [(i, i ^ mask) for i in range(size)])


def block_of(value, index, count):
    return lax.dynamic_slice_in_dim(value, index * count, count, 0)


def levels(size):
    bits = size.bit_length() - 1
    out = []
    shift = 0
    while shift < bits:
        wide = min(3, bits - shift)
        out.append((shift, wide))
        shift += wide
    return out


def groups_of(shift, wide):
    size = lax.axis_size("dp")
    count = 1 << wide
    return [
        [base + (n << shift) for n in range(count)]
        for base in range(size)
        if not (base >> shift) & (count - 1)
    ]


def exchange(value, shift, wide):
    return lax.all_to_all(
        value, "dp", split_axis=0, concat_axis=0, tiled=True,
        axis_index_groups=None if 1 << wide == lax.axis_size("dp") else groups_of(shift, wide),
    )


def gather_dp(value):
    sizes = [1 << wide for _, wide in levels(lax.axis_size("dp"))]
    whole_value = lax.all_gather(value, "dp", axis=0)
    if len(sizes) > 1:
        whole_value = whole_value.reshape(*sizes[::-1], *value.shape)
        whole_value = whole_value.transpose(
            *reversed(range(len(sizes))), len(sizes), len(sizes) + 1
        )
    return whole_value.reshape(sizes[0], -1, value.shape[1])


def first_parts():
    return 1 << levels(lax.axis_size("dp"))[0][1]


def start_dp(parts):
    return exchange(parts, *levels(lax.axis_size("dp"))[0])


def fold_dp(got):
    total = jnp.sum(got.astype(f32), axis=0)
    for shift, wide in levels(lax.axis_size("dp"))[1:]:
        parts = total.astype(bf16).reshape(1 << wide, -1, total.shape[1])
        total = jnp.sum(exchange(parts, shift, wide).astype(f32), axis=0)
    return total.astype(bf16)


def masks():
    return [1 << bit for bit in range(lax.axis_size("dp").bit_length() - 1)]


def halves(value, mask):
    bit = (lax.axis_index("dp") & mask) != 0
    rows = value.shape[0] // 2
    low, high = value[:rows], value[rows:]
    return jnp.where(bit, low, high), jnp.where(bit, high, low)


def give(value, small, mask):
    return jnp.concatenate([halves(value, mask)[0], small], axis=0)


def halve_dp(value, small, mask, other=None):
    return take(give(value, small, mask), halves(value, mask)[1], small, mask, other)


def take(given, kept, small, mask, other=None):
    got, other = lax.optimization_barrier((swap(given, "dp", mask), other))
    got = got.astype(f32)
    rows = kept.shape[0]
    value = (kept.astype(f32) + got[:rows]).astype(bf16)
    return value, (small.astype(f32) + got[rows:]).astype(bf16), other


def add_dp(value, small, mask):
    got = swap(jnp.concatenate([value, small], axis=0), "dp", mask).astype(f32)
    rows = value.shape[0]
    value = (value.astype(f32) + got[:rows]).astype(bf16)
    return value, (small.astype(f32) + got[rows:]).astype(bf16)


def after(value, *others):
    return lax.optimization_barrier((value, others))[0]


def double_dp(value, mask, other=None):
    bit = (lax.axis_index("dp") & mask) != 0
    got, other = lax.optimization_barrier((swap(value, "dp", mask), other))
    value = jnp.concatenate([jnp.where(bit, got, value), jnp.where(bit, value, got)], axis=0)
    return value, other


def by_index(value):
    bits = len(masks())
    width = value.shape[-1]
    value = value.reshape((2,) * bits + (-1, width)).transpose(*reversed(range(bits)), bits, bits + 1)
    wides = [wide for _, wide in levels(lax.axis_size("dp"))]
    value = value.reshape(*[1 << wide for wide in reversed(wides)], -1, width)
    count = len(wides)
    value = value.transpose(*reversed(range(count)), count, count + 1)
    return value.reshape(1 << wides[0], -1, width)


def shards(
    tokens, item_kind, first_gain, first_shift, query_weight, key_weight, value_weight,
    position_weight, content_bias, position_bias, output_weight, second_gain, second_shift,
    inner_weight, inner_bias, outer_weight, outer_bias, cotangent,
):
    length, width = tokens.shape
    cols = query_weight.shape[1]
    share = inner_weight.shape[1]
    mp = lax.axis_index("mp").astype(jnp.int32)
    core, high = mp & 1, mp >> 1
    low = lax.axis_index("dp").astype(jnp.int32) & 1
    place = jnp.stack([mp, core, high, low])
    half = length // 2
    block = min(512, half)
    per_half = half // block
    own = half // 4
    sin_table, cos_table = sinusoid(length, width)
    table = jnp.asarray(np.concatenate([sin_table, cos_table], axis=1), bf16)
    table_t = jnp.asarray(np.concatenate([sin_table, cos_table], axis=1).T, bf16)
    st = jnp.asarray(sin_table.T, f32)
    ct = jnp.asarray(cos_table.T, f32)
    gain1, shift1, gain2, shift2, bu = (
        v[None] for v in (first_gain, first_shift, second_gain, second_shift, outer_bias)
    )

    tie = lax.optimization_barrier
    wos = [output_weight] + [swap(output_weight, "mp", n) for n in (1, 2, 3)]
    bis = [inner_bias[None], swap(inner_bias[None], "mp", 1)]
    projections = (query_weight, key_weight, value_weight)
    normed, qc, qp, v, kt, p, ot, near, far, linv = attention_forward(
        item_kind, tokens, gain1, shift1, *projections, content_bias[None], position_bias[None],
        position_weight, st, ct, table, block,
    )
    near, far, wi, wu, wos, bis = tie((near, far, inner_weight, outer_weight, wos, bis))
    wis = [inner_weight, swap(wi, "mp", 1)]
    wus = [outer_weight, swap(wu, "mp", 1)]
    atts = [swap(near, "mp", 1), swap(far, "mp", 2), swap(near, "mp", 3)]
    attended = far
    back_keep, back_send, out, residual, bias, near, keep = feed(
        place, tokens, cotangent, far, atts, wos, wis, wus, bis, bu, gain2, shift2
    )
    back_got = swap(back_send, "mp", 2)
    near_got = swap(near, "mp", 1)
    feed_sum = (keep.astype(f32) + near_got.astype(f32)).astype(bf16)
    feed_got = start_dp(feed_sum)

    res, sums, *turned = turn(
        place, back_keep, back_got, residual, cotangent, attended, atts, wos, gain2
    )
    grads, weight_parts = turned[:4], turned[4:]
    grads = [grads[0]] + [swap(grads[n], "mp", n) for n in (1, 2, 3)]
    sums = jnp.concatenate([sums, bias[:1] + swap(bias[1:], "mp", 1)], axis=0)
    out_send = after(out, grads[1])
    weight_parts = after(weight_parts, grads[1])
    weight_parts = [weight_parts[0]] + [swap(weight_parts[n], "mp", n) for n in (1, 2, 3)]
    out_got = swap(out_send, "mp", 2)

    given, kept, small, near, keep = attention_backward(
        item_kind, place, p, grads, ot, linv, qc, qp, v, kt, table_t, position_weight,
        st, ct, *projections, normed, gain1, shift1, sums, block,
    )
    given, kept, small, near, keep, weight_parts, out_got, feed_got = tie(
        (given, kept, small, near, keep, weight_parts, out_got, feed_got)
    )
    near = swap(near, "mp", 1)
    out_sum = sum(x.astype(f32) for x in weight_parts)
    fill = lambda value, there: (
        value.astype(f32)
        + jnp.pad(out_sum * there.astype(f32), ((0, value.shape[0] - cols), (0, 0)))
    ).astype(bf16)
    given = fill(given, low)
    kept = fill(kept, 1 - low)
    pick = lambda x: lax.dynamic_index_in_dim(x.reshape(2, 2, own, width), 1 - high, 1, False)
    far = (pick(keep).astype(f32) + pick(near).astype(f32)).astype(bf16).reshape(2 * own, width)
    first, *middle = masks()
    feed_total = fold_dp(after(feed_got, given, far))
    far = swap(far, "mp", 2)

    last, small, far = take(given, kept, small, first, far)
    mixed = (out.astype(f32) + out_got.astype(f32)).astype(bf16)
    mixed = [mixed, swap(mixed, "mp", 1)]
    grad = close(place, keep, near, far, tokens, res, gain1)
    beyond = swap(grad, "mp", 2)
    for mask in reversed(masks()):
        feed_total, _ = double_dp(feed_total, mask)
    for mask in middle[:-1]:
        last, small, _ = halve_dp(last, small, mask)
    last, small = add_dp(last, small, middle[-1])
    for mask in reversed(middle[:-1]):
        last, _ = double_dp(last, mask)
    tokens_grad = [grad, swap(grad, "mp", 1), beyond, swap(beyond, "mp", 1)]
    small = after(small, last)
    mixed, tokens_grad = collect(place, mixed, tokens_grad)
    last_total, (mixed, tokens_grad) = double_dp(last, first, (mixed, tokens_grad))
    last_total = last_total.astype(f32)
    last_small = small.astype(f32)
    feed_total = by_index(feed_total)

    summed = last_small[:5]
    summed = summed + swap(summed, "mp", 1)
    summed = summed + swap(summed, "mp", 2)
    feed_total = feed_total.astype(f32)
    split = width // first_parts()
    inner_grad = feed_total[:, :split].reshape(width, share)
    outer_grad = feed_total[:, split:].reshape(share, width)
    whole_grad = last_total[cols:]

    return (
        mixed,
        tokens_grad,
        summed[0],
        summed[1],
        whole_grad[:, :cols],
        whole_grad[:, cols : 2 * cols],
        whole_grad[:, 2 * cols : 3 * cols],
        whole_grad[:, 3 * cols :],
        last_small[6, :cols],
        last_small[6, cols : 2 * cols],
        last_total[:cols],
        summed[2],
        summed[3],
        inner_grad,
        last_small[5],
        outer_grad,
        summed[4],
    )


def solution(mesh):
    return jax.shard_map(
        shards,
        mesh=mesh,
        in_specs=(
            P("dp", None), P("dp"), P(), P(), P(None, "mp"), P(None, "mp"), P(None, "mp"),
            P(None, "mp"), P("mp"), P("mp"), P("mp", None), P(), P(), P(None, "mp"), P("mp"),
            P("mp", None), P(), P("dp", None),
        ),
        out_specs=(
            P("dp", None), P("dp", None), P(), P(), P(None, "mp"), P(None, "mp"), P(None, "mp"),
            P(None, "mp"), P("mp"), P("mp"), P("mp", None), P(), P(), P(None, "mp"), P("mp"),
            P("mp", None), P(),
        ),
        check_vma=False,
    )
```
